32 devices in a mesh: batch: 8 (over z, y), tensor: 4 (over x, core).
Axes of the slice: x: 2, y: 2, z: 4, core: 2. Of those that a mesh axis runs over, the one named last changes fastest.
Arguments:
- hidden_rows: bfloat16 [16384, 768], P(('batch', 'tensor')), may hold values from -6 to 6
- side_input: bfloat16 [16384, 96], P(('batch', 'tensor')), may hold values from -6 to 6
- segment_ids: int32 [16384], P(('batch', 'tensor')), may hold values from 0 to 2047, as said below
- side_cotangent: bfloat16 [16384, 96], P(('batch', 'tensor')), may hold values from -6 to 6
- backbone_gains: bfloat16 [2, 2, 768], replicated, may hold values from 0.5 to 1.5
- backbone_project: bfloat16 [2, 768, 3, 768], P(None, None, None, 'tensor'), may hold values from -0.21875 to 0.21875
- backbone_mixing: bfloat16 [2, 768, 768], P(None, 'tensor'), may hold values from -0.875 to 0.875
- backbone_expand: bfloat16 [2, 768, 3072], P(None, None, 'tensor'), may hold values from -0.21875 to 0.21875
- backbone_reduce: bfloat16 [2, 3072, 768], P(None, 'tensor'), may hold values from -0.109375 to 0.109375
- side_down: bfloat16 [2, 768, 96], replicated, may hold values from -0.21875 to 0.21875
- side_gate: float32 [2, 96], replicated, may hold values from -2 to 2
- side_gains: bfloat16 [2, 2, 96], replicated, may hold values from 0.25 to 1.75
- side_project: bfloat16 [2, 96, 288], replicated, may hold values from -0.625 to 0.625
- side_mixing: bfloat16 [2, 96, 96], replicated, may hold values from -2.5 to 2.5
- side_expand: bfloat16 [2, 96, 384], replicated, may hold values from -0.625 to 0.625
- side_reduce: bfloat16 [2, 384, 96], replicated, may hold values from -0.3125 to 0.3125
Outputs:
- backbone_out: bfloat16 [16384, 768], P(('batch', 'tensor'))
- side_out: float32 [16384, 96], P(('batch', 'tensor'))
- side_input_grad: float32 [16384, 96], P(('batch', 'tensor'))
- down_grad: float32 [2, 768, 96], replicated
- gate_grad: float32 [2, 96], replicated
- gains_grad: float32 [2, 2, 96], replicated
- project_grad: float32 [2, 96, 288], replicated
- mixing_grad: float32 [2, 96, 96], replicated
- expand_grad: float32 [2, 96, 384], replicated
- reduce_grad: float32 [2, 384, 96], replicated
The draws below stay inside these ranges and needn't reach their ends.
Inputs may be any that keep to these rules, and one draw needn't show every extreme that they name: `segment_ids`: within each packed sequence of 2048 consecutive rows the ids start at 0, never fall and may skip values; the last row of every sequence has id 2048 - 1; in every sequence one example starts within the first 512 rows and ends within the last 512 rows.
All inputs are finite; a program needn't handle non-finite values.
Results may differ from the reference program's by a relative error of at most 0.033.
Values may be sent and summed in bfloat16 or wider, within the bound.
A program may use at most 128 MiB of HBM per device.

```python
import jax
import jax.numpy as jnp
from jax import lax

D = 768
HEADS = 12
HEAD_DIM = 64
FF = 3072
SIDE = 96
SIDE_HEADS = 12
SIDE_HEAD_DIM = 8
SIDE_FF = 384
LAYERS = 2
TOK_DEV = 512
LENGTH = 2048
TOKENS = 16384
N_TENSOR = 4


def draw_segment_ids(key, part):
    key = jax.random.fold_in(key, 7)
    groups = TOKENS // LENGTH
    key_first, key_last, key_coins = jax.random.split(key, 3)
    first = jax.random.randint(key_first, (groups, 1), 1, TOK_DEV)
    last = jax.random.randint(key_last, (groups, 1), 3 * TOK_DEV + 1, LENGTH)
    place = jnp.arange(LENGTH, dtype=jnp.int32)[None, :]
    coins = jax.random.randint(key_coins, (groups, LENGTH), 0, max(2, TOK_DEV // 8))
    outside = (place < first) | (place > last)
    flags = (coins == 0) & outside & (place > 0)
    flags = flags | (place == first) | (place == last)
    ids = jnp.cumsum(flags.astype(jnp.int32), axis=1).astype(jnp.int32)
    final_id = ids[:, -1:]
    ids = jnp.where(ids == final_id, jnp.int32(LENGTH - 1), ids)
    return ids.reshape(TOKENS).astype(jnp.int32)


def block_levels(key, dims, cuts, least, largest):
    def one(dim, shards_of):
        heights = jax.random.uniform(jax.random.fold_in(jax.random.fold_in(key, 6), dim), (shards_of,), jnp.float32, least / len(cuts), largest / len(cuts))
        return jnp.repeat(jnp.exp(heights), dims[dim] // shards_of).reshape((-1,) + (1,) * (len(dims) - dim - 1))

    level = one(*cuts[0])
    for cut in cuts[1:]:
        level = level * one(*cut)
    return level


def centred(key, extent, deviation, most, cuts=(), kind=jnp.bfloat16):
    result = jax.random.normal(key, extent, jnp.float32) * deviation
    if len(cuts) > 0:
        result = block_levels(key, extent, cuts, -0.22, 0.18) * result
    return jnp.clip(result, min=-most, max=most).astype(kind)


def setup_inputs(seed: int = 0) -> dict:
    streams_of = jax.random.split(jax.random.key(seed), 17)
    return {
        "hidden_rows": centred(streams_of[0], (TOKENS, D), 1.0, 6.0, ((0, 32),)),
        "side_input": centred(streams_of[1], (TOKENS, SIDE), 1.0, 6.0, ((0, 32),)),
        "segment_ids": draw_segment_ids(jax.random.fold_in(streams_of[16], 71), 0),
        "side_cotangent": centred(streams_of[3], (TOKENS, SIDE), 1.0, 6.0, ((0, 32),)),
        "backbone_gains": jnp.clip(1.0 + 0.1 * jax.random.normal(streams_of[4], (LAYERS, 2, D), jnp.float32), 0.5, 1.5).astype(jnp.bfloat16),
        "backbone_project": centred(streams_of[5], (LAYERS, D, 3, D), D ** -0.5, 0.21875, ((3, 4),)),
        "backbone_mixing": centred(streams_of[6], (LAYERS, D, D), (max(1, D // 16)) ** -0.5, 0.875, ((1, 4),)),
        "backbone_expand": centred(streams_of[7], (LAYERS, D, FF), D ** -0.5, 0.21875, ((2, 4),)),
        "backbone_reduce": centred(streams_of[8], (LAYERS, FF, D), FF ** -0.5, 0.109375, ((1, 4),)),
        "side_down": centred(streams_of[9], (LAYERS, D, SIDE), D ** -0.5, 0.21875),
        "side_gate": jnp.clip(jax.random.uniform(streams_of[10], (LAYERS, SIDE), jnp.float32, -2.0, 2.0), -2.0, 2.0),
        "side_gains": jnp.clip(1.0 + 0.15 * jax.random.normal(streams_of[11], (LAYERS, 2, SIDE), jnp.float32), 0.25, 1.75).astype(jnp.bfloat16),
        "side_project": centred(streams_of[12], (LAYERS, SIDE, 3 * SIDE), SIDE ** -0.5, 0.625),
        "side_mixing": centred(streams_of[13], (LAYERS, SIDE, SIDE), (max(1, SIDE // 16)) ** -0.5, 2.5),
        "side_expand": centred(streams_of[14], (LAYERS, SIDE, SIDE_FF), SIDE ** -0.5, 0.625),
        "side_reduce": centred(streams_of[15], (LAYERS, SIDE_FF, SIDE), SIDE_FF ** -0.5, 0.3125),
    }


EPS = 1e-06
masked_out = -1e+30
HIGH = lax.Precision.HIGHEST

@jax.custom_vjp
def low(v):
    return lax.optimization_barrier(v.astype(jnp.bfloat16)).astype(jnp.float32)

@jax.custom_vjp
def low_back(v):
    return v

def low_keep(v):
    return (low(v), None)

def low_pass(kept, grad):
    return (grad,)

def back_keep(v):
    return (v, None)

def back_low(kept, grad):
    return (low(grad),)
low.defvjp(low_keep, low_pass)
low_back.defvjp(back_keep, back_low)

def product(left, right):
    return jnp.dot(left, right, precision=HIGH, preferred_element_type=jnp.float32)

def root_norm(values, gain):
    return values * lax.rsqrt(lax.optimization_barrier(jnp.mean(values * values, axis=-1, keepdims=True)) + EPS) * gain

def masked_softmax(scores, visible):
    scores = jnp.where(visible, scores, masked_out)
    top = lax.optimization_barrier(jnp.max(scores, axis=-1, keepdims=True))
    expo = jnp.exp(scores - top)
    return expo / lax.optimization_barrier(jnp.sum(expo, axis=-1, keepdims=True))

def shard_sum(values, weight):
    width = values.shape[1] // N_TENSOR
    parts = jnp.einsum('lnc,ncd->nld', values.reshape(values.shape[0], N_TENSOR, width), weight.reshape(N_TENSOR, width, weight.shape[1]), precision=HIGH)
    return lax.optimization_barrier(jnp.sum(low(parts), axis=0))

def backbone_layer(stream, visible, gains, project, mixing, expand, reduce_w):
    normed = low(root_norm(stream, gains[0]))
    query = low(product(normed, project[:, 0]))
    keys = low(product(normed, project[:, 1]))
    values = low(product(normed, project[:, 2]))

    def one_head(head):
        start = head * HEAD_DIM
        q_part = lax.dynamic_slice_in_dim(query, start, HEAD_DIM, 1)
        k_part = lax.dynamic_slice_in_dim(keys, start, HEAD_DIM, 1)
        v_part = lax.dynamic_slice_in_dim(values, start, HEAD_DIM, 1)
        probs = masked_softmax(product(q_part, k_part.T) * HEAD_DIM ** (-0.5), visible)
        return product(low(probs), v_part)
    heads = lax.map(one_head, jnp.arange(HEADS, dtype=jnp.int32))
    attended = low(heads.transpose(1, 0, 2).reshape(stream.shape[0], D))
    stream = stream + shard_sum(attended, mixing)
    normed = low(root_norm(stream, gains[1]))
    hidden = low(jax.nn.gelu(product(normed, expand)))
    return stream + shard_sum(hidden, reduce_w)

def side_attention(query, keys, values, visible):

    def one_head(head):
        start = head * SIDE_HEAD_DIM
        q_part = lax.dynamic_slice_in_dim(query, start, SIDE_HEAD_DIM, 1)
        k_part = lax.dynamic_slice_in_dim(keys, start, SIDE_HEAD_DIM, 1)
        v_part = lax.dynamic_slice_in_dim(values, start, SIDE_HEAD_DIM, 1)
        scores = low_back(product(q_part, k_part.T) * SIDE_HEAD_DIM ** (-0.5))
        probs = masked_softmax(scores, visible)
        return product(low(probs), v_part)
    heads = lax.map(jax.checkpoint(one_head), jnp.arange(SIDE_HEADS, dtype=jnp.int32))
    return heads.transpose(1, 0, 2).reshape(query.shape[0], SIDE)

def side_forward(params, frozen, state, visible):
    down, gate, gains, project, mixing, expand, reduce_w = params
    for layer in range(LAYERS):
        lifted = low_back(product(frozen[layer], down[layer]))
        weight = jax.nn.sigmoid(gate[layer])
        mixed = weight * lifted + (1.0 - weight) * state
        normed = low(root_norm(mixed, gains[layer, 0]))
        projected = product(normed, project[layer])
        query = low(low_back(projected[:, :SIDE]))
        keys = low(low_back(projected[:, SIDE:2 * SIDE]))
        values = low(low_back(projected[:, 2 * SIDE:]))
        attended = low(low_back(side_attention(query, keys, values, visible)))
        middle = mixed + low_back(product(attended, mixing[layer]))
        normed_two = low(root_norm(middle, gains[layer, 1]))
        inner = low_back(product(normed_two, expand[layer]))
        activated = low(jax.nn.gelu(inner))
        state = middle + low_back(product(activated, reduce_w[layer]))
    return state

def to_float(array):
    return array.astype(jnp.float32)

def reference(hidden_rows, side_input, segment_ids, side_cotangent, backbone_gains, backbone_project, backbone_mixing, backbone_expand, backbone_reduce, side_down, side_gate, side_gains, side_project, side_mixing, side_expand, side_reduce):
    params = (to_float(side_down), to_float(side_gate), to_float(side_gains), to_float(side_project), to_float(side_mixing), to_float(side_expand), to_float(side_reduce))
    groups = TOKENS // LENGTH

    def per_group(totals, inputs):
        stream, start_state, cotangent, ids = inputs
        visible = ids[:, None] == ids[None, :]
        frozen = []
        for layer in range(LAYERS):
            stream = backbone_layer(stream, visible, to_float(backbone_gains[layer]), to_float(backbone_project[layer]), to_float(backbone_mixing[layer]), to_float(backbone_expand[layer]), to_float(backbone_reduce[layer]))
            frozen.append(low(stream))
        frozen = jnp.stack(frozen)
        final, pull = jax.vjp(lambda prm, first: side_forward(prm, frozen, first, visible), params, start_state)
        grads, grad_start = pull(cotangent)
        totals = jax.tree.map(lambda left, right: left + right, totals, grads)
        return (totals, (stream.astype(jnp.bfloat16), final, grad_start))
    zeros = jax.tree.map(jnp.zeros_like, params)
    inputs = (to_float(hidden_rows).reshape(groups, LENGTH, D), to_float(side_input).reshape(groups, LENGTH, SIDE), to_float(side_cotangent).reshape(groups, LENGTH, SIDE), segment_ids.reshape(groups, LENGTH))
    totals, (outputs, finals, grad_starts) = lax.scan(per_group, zeros, inputs)
    return (outputs.reshape(TOKENS, D), finals.reshape(TOKENS, SIDE), grad_starts.reshape(TOKENS, SIDE), totals[0], totals[1], totals[2], totals[3], totals[4], totals[5], totals[6])
```

```python
import functools
import jax
import jax.numpy as jnp
from jax import lax
from jax.experimental import pallas as pl
from jax.experimental.pallas import tpu as pltpu
from jax.sharding import PartitionSpec as P

HEAD_DIM = 64
SIDE_HEADS = 12
SIDE_HEAD_DIM = 8
LAYERS = 2
EPS = 1e-06
BIG = 2.0**100
LOG2E = 1.4426950408889634
ID_BITS = 11
QUAD = 4
MESH = pl.DeviceIdType.MESH
F32 = jnp.float32
BF16 = jnp.bfloat16


def contract(left, right, dims):
    return lax.dot_general(left, right, ((dims[:1], dims[1:]), ((), ())), preferred_element_type=F32)


def nn(left, right):
    return contract(left, right, (1, 0))


def nt(left, right):
    return contract(left, right, (1, 1))


def tn(left, right):
    return contract(left, right, (0, 0))


def lanes_of(rows, lanes):
    return lax.broadcasted_iota(jnp.int32, (rows, lanes), 1)


def segment_lanes(id_row, offset):
    width = id_row.shape[1]
    place = lax.broadcasted_iota(jnp.int32, (128, width), 0) - offset
    flipped = place >= ID_BITS
    shift = jnp.clip(jnp.where(flipped, place - ID_BITS, place), 0, ID_BITS)
    bit = lax.shift_right_logical(jnp.broadcast_to(id_row, (128, width)), shift) & 1
    bit = jnp.where(flipped, 1 - bit, bit)
    used = (place >= 0) & (place < 2 * ID_BITS)
    keys = jnp.where(used, bit, 0).astype(F32)
    queries = jnp.where(used, (bit - 1).astype(F32) * BIG, 0.0)
    return keys.T, queries.T


def root_norm(values, gain):
    return values * lax.rsqrt(jnp.mean(values * values, axis=-1, keepdims=True) + EPS) * gain


def backbone_kernel(
    layer,
    x_ref,
    ids_ref,
    gains_ref,
    qkv_hbm,
    mix_hbm,
    exp_hbm,
    red_hbm,
    h_ref,
    f_ref,
    idall_ref,
    rows_all,
    ids_buf,
    qkv_w,
    mix_w,
    exp_w,
    red_w,
    q_s,
    k_s,
    vt_s,
    scores,
    heads_buf,
    acc,
    local_sem,
    row_send,
    row_recv,
    id_send,
    id_recv,
    head_send,
    head_recv,
    cross_send,
    spread_send,
    sib_send,
    far_send,
    w_recv,
):
    b = lax.axis_index("batch")
    t = lax.axis_index("tensor")
    part = lax.rem(b, QUAD)
    tokens = x_ref.shape[0]
    width = mix_w.shape[1]
    parts = rows_all.shape[0]
    half = tokens // 2
    sources = (mix_hbm, exp_hbm, red_hbm)
    fulls = (mix_w, exp_w, red_w)
    slices = tuple(w.shape[1] // QUAD for w in fulls)

    load_qkv = pltpu.make_async_copy(qkv_hbm.at[layer], qkv_w, local_sem.at[0])
    load_qkv.start()
    load_own = []
    for w in range(3):
        load_own.append(
            pltpu.make_async_copy(sources[w].at[layer], fulls[w].at[t], local_sem.at[1 + w])
        )
        load_own[w].start()

    barrier = pltpu.get_barrier_semaphore()
    for k in range(1, parts):
        pl.semaphore_signal(barrier, inc=1, device_id=(b, t ^ k), device_id_type=MESH)
    for k in range(1, QUAD):
        pl.semaphore_signal(barrier, inc=1, device_id=(b ^ k, t), device_id_type=MESH)
    pl.semaphore_wait(barrier, parts - 1 + QUAD - 1)

    def remote(src, dst, send, recv, target):
        return pltpu.make_async_remote_copy(
            src_ref=src, dst_ref=dst, send_sem=send, recv_sem=recv, device_id=target, device_id_type=MESH
        )

    ids_buf[t] = jnp.broadcast_to(ids_ref[...], (8, tokens))
    id_copies = [
        remote(ids_buf.at[t], ids_buf.at[t], id_send.at[k - 1], id_recv.at[t], (b, t ^ k))
        for k in range(1, parts)
    ]
    for copy in id_copies:
        copy.start()

    stream = x_ref[...].astype(F32)
    rows_all[t] = root_norm(stream, gains_ref[0:1, :].astype(F32)).astype(BF16)

    def row_copy(slot, chunk, send, target):
        view = rows_all.at[slot, pl.ds(chunk * half, half)]
        return remote(view, view, row_send.at[send, chunk], row_recv.at[slot, chunk], target)

    sib, across, far = t ^ 1, t ^ 2, t ^ 3
    for chunk in range(2):
        row_copy(t, chunk, 1, (b, across)).start()
    for chunk in range(2):
        row_copy(t, chunk, 0, (b, sib)).start()

    def cross(w):
        view = pl.ds(pl.multiple_of(part * slices[w], 16), slices[w])
        return remote(
            sources[w].at[layer, view],
            fulls[w].at[t, view],
            cross_send.at[w],
            w_recv.at[w, t, part],
            (b, across),
        )

    def spread(w, k):
        view = fulls[w].at[across, pl.ds(pl.multiple_of(part * slices[w], 16), slices[w])]
        return remote(view, view, spread_send.at[w, k], w_recv.at[w, across, part], (b ^ k, t))

    def whole(w, slot, send):
        return remote(
            fulls[w].at[slot], fulls[w].at[slot], send.at[w], w_recv.at[w, slot, 0], (b, sib)
        )

    def own_to_sib(w):
        return remote(
            sources[w].at[layer], fulls[w].at[t], sib_send.at[w], w_recv.at[w, t, 0], (b, sib)
        )

    def arrived_slice(w, k):
        source = part ^ k
        view = fulls[w].at[across, pl.ds(pl.multiple_of(source * slices[w], 16), slices[w])]
        return remote(view, view, cross_send.at[w], w_recv.at[w, across, source], (b, sib))

    lane = lanes_of(tokens, 256)

    def project(slot):
        rows = rows_all[slot]
        at = pl.ds(pl.multiple_of(slot * tokens, tokens), tokens)
        key_bits, query_bits = segment_lanes(ids_buf[slot][0:1, :], width - 128)
        query = nn(rows, qkv_w[0]) * (HEAD_DIM**-0.5 * LOG2E)
        keys = nn(rows, qkv_w[1])
        q_s[at, 0:128] = query[:, 0:128].astype(BF16)
        q_s[at, 128:256] = (query[:, 128:256] + query_bits).astype(BF16)
        k_s[at, 0:128] = keys[:, 0:128].astype(BF16)
        k_s[at, 128:256] = (keys[:, 128:256] + key_bits).astype(BF16)
        values = nn(rows, qkv_w[2]).T
        for h in range(width // HEAD_DIM):
            vt_s[h, 0:HEAD_DIM, at] = values[h * HEAD_DIM : (h + 1) * HEAD_DIM].astype(BF16)
            vt_s[h, HEAD_DIM:, at] = jnp.ones((16, tokens), BF16)

    load_qkv.wait()
    for copy in id_copies:
        copy.wait_send()
    for k in range(1, parts):
        remote(
            ids_buf.at[t ^ k], ids_buf.at[t ^ k], id_send.at[0], id_recv.at[t ^ k], (b, sib)
        ).wait_recv()

    def step(index, carry):
        @pl.when(index == 1)
        def _():
            for chunk in range(2):
                row_copy(sib, chunk, 0, (b, sib)).wait_recv()

        @pl.when(index == 2)
        def _():
            for chunk in range(2):
                row_copy(across, chunk, 0, (b, sib)).wait_recv()
                row_copy(across, chunk, 2, (b, sib)).start()
            for w in range(3):
                cross(w).start()

        @pl.when(index == 3)
        def _():
            for chunk in range(2):
                row_copy(far, chunk, 0, (b, sib)).wait_recv()
            for w in range(3):
                own_to_sib(w).start()

        project(t ^ index)
        return carry

    lax.fori_loop(0, parts, step, 0)
    for send, slot in ((0, sib), (1, across), (2, sib)):
        for chunk in range(2):
            row_copy(t if send < 2 else across, chunk, send, (b, slot)).wait_send()
    for slot in range(parts):
        idall_ref[slot] = ids_buf[slot]

    heads = width // HEAD_DIM
    count = parts * heads

    def make_scores(item, place):
        block = t ^ (parts - 1 - item // heads)
        h = lax.rem(item, heads)
        rows = q_s[pl.ds(pl.multiple_of(block * tokens, tokens), tokens), :]
        chosen = (lane // HEAD_DIM == h) | (lane >= width)
        scores[place] = nt(k_s[...], jnp.where(chosen, rows, jnp.zeros_like(rows)))

    def send_heads(block):
        return remote(
            heads_buf.at[block],
            heads_buf.at[parts + t],
            head_send.at[block],
            head_recv.at[t],
            (b, block),
        )

    def attend(item, place):
        block = t ^ (parts - 1 - item // heads)
        h = lax.rem(item, heads)
        values = scores[place]
        weights = jnp.exp2(values - jnp.max(values, axis=0, keepdims=True)).astype(BF16)
        out = nn(vt_s[h], weights)
        slot = jnp.where(block == t, parts + t, block)
        heads_buf[slot, pl.ds(pl.multiple_of(h * HEAD_DIM, HEAD_DIM), HEAD_DIM), :] = (
            out[0:HEAD_DIM] * (1.0 / out[HEAD_DIM : HEAD_DIM + 1])
        ).astype(BF16)

        @pl.when((h == heads - 1) & (item < count - heads))
        def _():
            send_heads(block).start()

    make_scores(0, 0)

    def pair(index, carry):
        item = 2 * index
        make_scores(item + 1, 1)
        attend(item, 0)

        @pl.when(index == 2)
        def _():
            for w in range(2):
                remote(
                    fulls[w].at[across, pl.ds(pl.multiple_of(part * slices[w], 16), slices[w])],
                    fulls[w].at[across, pl.ds(pl.multiple_of(part * slices[w], 16), slices[w])],
                    cross_send.at[w],
                    w_recv.at[w, across, part],
                    (b, across),
                ).wait_recv()
                for k in range(1, QUAD):
                    spread(w, k).start()

        @pl.when(index == 4)
        def _():
            remote(
                fulls[2].at[across, pl.ds(pl.multiple_of(part * slices[2], 16), slices[2])],
                fulls[2].at[across, pl.ds(pl.multiple_of(part * slices[2], 16), slices[2])],
                cross_send.at[2],
                w_recv.at[2, across, part],
                (b, across),
            ).wait_recv()
            for k in range(1, QUAD):
                spread(2, k).start()

        make_scores(jnp.minimum(item + 2, count - 1), 0)
        attend(item + 1, 1)
        return carry

    lax.fori_loop(0, count // 2, pair, 0)

    for k in range(1, QUAD):
        arrived_slice(0, k).wait_recv()
    whole(0, across, far_send).start()
    load_own[0].wait()
    whole(0, sib, far_send).wait_recv()
    for k in range(1, parts):
        send_heads(t ^ k).wait_send()
        remote(
            heads_buf.at[0], heads_buf.at[parts + (t ^ k)], head_send.at[0], head_recv.at[t ^ k], (b, sib)
        ).wait_recv()
    for k in range(1, QUAD):
        arrived_slice(1, k).wait_recv()
    whole(1, across, far_send).start()
    whole(0, far, far_send).wait_recv()
    attended = heads_buf[parts : 2 * parts].reshape(parts * width, tokens)
    stream = x_ref[...].astype(F32) + tn(attended, mix_w[...].reshape(parts * width, -1))
    acc[...] = stream
    normed = root_norm(stream, gains_ref[1:2, :].astype(F32)).astype(BF16)

    def feed(index, carry):
        @pl.when(index == 0)
        def _():
            for w in (1, 2):
                load_own[w].wait()

        @pl.when(index == 1)
        def _():
            for w in (1, 2):
                whole(w, sib, far_send).wait_recv()

        @pl.when(index == 2)
        def _():
            for k in range(1, QUAD):
                arrived_slice(2, k).wait_recv()
            whole(2, across, far_send).start()

        @pl.when(index == 3)
        def _():
            for w in (1, 2):
                whole(w, far, far_send).wait_recv()

        hidden = jax.nn.gelu(nn(normed, exp_w[t ^ index])).astype(BF16)
        acc[...] += nn(hidden, red_w[t ^ index])
        return carry

    lax.fori_loop(0, parts, feed, 0)
    h_ref[...] = acc[...]
    f_ref[...] = acc[...].astype(BF16)
    for w in range(3):
        cross(w).wait_send()
        own_to_sib(w).wait_send()
        whole(w, across, far_send).wait_send()
        for k in range(1, QUAD):
            spread(w, k).wait_send()


def backbone_call(layer, x, ids, gains, qkv, mix, exp, red, parts):
    tokens, model = x.shape
    width = mix.shape[1]
    units = exp.shape[2]
    heads = width // HEAD_DIM
    vmem = pl.BlockSpec(memory_space=pltpu.VMEM)
    anywhere = pl.BlockSpec(memory_space=pl.ANY)
    dma = pltpu.SemaphoreType.DMA
    return pl.pallas_call(
        functools.partial(backbone_kernel, layer),
        out_shape=(
            jax.ShapeDtypeStruct((tokens, model), F32),
            jax.ShapeDtypeStruct((tokens, model), BF16),
            jax.ShapeDtypeStruct((parts, 8, tokens), jnp.int32),
        ),
        in_specs=[vmem] * 3 + [anywhere] * 4,
        out_specs=(vmem, vmem, vmem),
        scratch_shapes=[
            pltpu.VMEM((parts, tokens, model), BF16),
            pltpu.VMEM((parts, 8, tokens), jnp.int32),
            pltpu.VMEM((3, model, 256), BF16),
            pltpu.VMEM((parts, width, model), BF16),
            pltpu.VMEM((parts, model, units), BF16),
            pltpu.VMEM((parts, units, model), BF16),
            pltpu.VMEM((parts * tokens, 256), BF16),
            pltpu.VMEM((parts * tokens, 256), BF16),
            pltpu.VMEM((heads, HEAD_DIM + 16, parts * tokens), BF16),
            pltpu.VMEM((2, parts * tokens, tokens), F32),
            pltpu.VMEM((2 * parts, width, tokens), BF16),
            pltpu.VMEM((tokens, model), F32),
            dma((4,)),
            dma((3, 2)),
            dma((parts, 2)),
            dma((parts - 1,)),
            dma((parts,)),
            dma((parts,)),
            dma((parts,)),
            dma((3,)),
            dma((3, QUAD)),
            dma((3,)),
            dma((3,)),
            dma((3, parts, QUAD)),
        ],
        compiler_params=pltpu.CompilerParams(
            collective_id=1 + layer, has_side_effects=True, vmem_limit_bytes=60 << 20
        ),
        cost_estimate=pl.CostEstimate(flops=20_000_000_000, bytes_accessed=20_000_000, transcendentals=12_000_000),
    )(x, ids, gains, qkv, mix, exp, red)


def outer_sum(left, right):
    return lax.dot_general(
        left, right, (((0,), (0,)), ((), ())), preferred_element_type=jnp.float32
    )


def back_product(left, weight):
    return lax.dot_general(
        left, weight, (((1,), (1,)), ((), ())), preferred_element_type=jnp.float32
    )


def split_heads(values):
    return values.reshape(values.shape[0], SIDE_HEADS, SIDE_HEAD_DIM).transpose(1, 0, 2)


def join_heads(values):
    return values.transpose(1, 0, 2).reshape(values.shape[1], SIDE_HEADS * SIDE_HEAD_DIM)


def side_head(query, keys, values, row_ids, key_ids):
    scale = SIDE_HEAD_DIM ** (-0.5)
    scores = jnp.einsum("qd,kd->qk", query, keys, preferred_element_type=jnp.float32) * scale
    scores = jnp.where(row_ids[:, None] == key_ids[None, :], scores, -1e30)
    top = jnp.max(scores, axis=-1, keepdims=True)
    expo = jnp.exp(scores - top)
    denom = jnp.sum(expo, axis=-1, keepdims=True)
    probs = expo / denom
    log_total = top[:, 0] + jnp.log(denom[:, 0])
    attended = jnp.dot(probs.astype(jnp.bfloat16), values, preferred_element_type=jnp.float32)
    return (attended.astype(jnp.bfloat16), log_total)


def side_head_back(query, keys, values, grad_out, log_total, row_ids, key_ids):
    scale = SIDE_HEAD_DIM ** (-0.5)
    scores = jnp.einsum("qd,kd->qk", query, keys, preferred_element_type=jnp.float32) * scale
    scores = jnp.where(row_ids[:, None] == key_ids[None, :], scores, -1e30)
    probs = jnp.exp(scores - log_total[:, None])
    grad_probs = jnp.einsum("qd,kd->qk", grad_out, values, preferred_element_type=jnp.float32)
    grad_values = jnp.einsum(
        "qk,qd->kd", probs.astype(jnp.bfloat16), grad_out, preferred_element_type=jnp.float32
    )
    inner = jnp.sum(grad_probs * probs, axis=-1, keepdims=True)
    grad_scores = (probs * (grad_probs - inner)).astype(jnp.bfloat16)
    grad_query = (jnp.dot(grad_scores, keys, preferred_element_type=jnp.float32) * scale).astype(
        jnp.bfloat16
    )
    grad_keys = (
        jnp.einsum("qk,qd->kd", grad_scores, query, preferred_element_type=jnp.float32) * scale
    )
    return (grad_query, grad_keys, grad_values)


def side_forward(
    state, frozen, down, gate, gains, project, mixing, expand, reduce_w, row_ids, key_ids
):
    width = state.shape[1]
    lifted = jnp.dot(frozen, down, preferred_element_type=jnp.float32)
    weight = jax.nn.sigmoid(gate)
    mixed = weight * lifted + (1.0 - weight) * state
    normed = root_norm(mixed, gains[0]).astype(jnp.bfloat16)
    projected = jnp.dot(normed, project, preferred_element_type=jnp.float32).astype(jnp.bfloat16)
    query = projected[:, :width]
    all_keys, all_values = (
        lax.all_gather(projected[:, width : 2 * width], "tensor", axis=0, tiled=True),
        lax.all_gather(projected[:, 2 * width :], "tensor", axis=0, tiled=True),
    )

    def one_head(parts):
        return side_head(parts[0], parts[1], parts[2], row_ids, key_ids)

    heads_out, log_total = lax.map(
        one_head, (split_heads(query), split_heads(all_keys), split_heads(all_values))
    )
    attended = join_heads(heads_out)
    middle = mixed + jnp.dot(attended, mixing, preferred_element_type=jnp.float32)
    normed_two = root_norm(middle, gains[1]).astype(jnp.bfloat16)
    inner = jnp.dot(normed_two, expand, preferred_element_type=jnp.float32)
    activated = jax.nn.gelu(inner).astype(jnp.bfloat16)
    result = middle + jnp.dot(activated, reduce_w, preferred_element_type=jnp.float32)
    fetched = (all_keys, all_values)
    record = (
        state,
        lifted,
        mixed,
        normed,
        projected,
        fetched,
        attended,
        log_total,
        middle,
        normed_two,
        inner,
        activated,
    )
    return (record, result)


def side_backward(
    grad, record, frozen, gate, gains, project, mixing, expand, reduce_w, row_ids, key_ids
):
    (
        previous,
        lifted,
        mixed,
        normed,
        projected,
        fetched,
        attended,
        log_total,
        middle,
        normed_two,
        inner,
        activated,
    ) = record
    width = previous.shape[1]
    grad_top = grad.astype(jnp.bfloat16)
    reduce_grad = outer_sum(activated, grad_top)
    grad_act = back_product(grad_top, reduce_w)
    _, gelu_pull = jax.vjp(jax.nn.gelu, inner)
    grad_inner = gelu_pull(grad_act)[0].astype(jnp.bfloat16)
    expand_grad = outer_sum(normed_two, grad_inner)
    grad_normed_two = back_product(grad_inner, expand)
    _, norm_pull_two = jax.vjp(root_norm, middle, gains[1])
    grad_middle_norm, gain_two_grad = norm_pull_two(grad_normed_two)
    grad_middle = grad + grad_middle_norm
    grad_branch = grad_middle.astype(jnp.bfloat16)
    mixing_grad = outer_sum(attended, grad_branch)
    grad_attended = back_product(grad_branch, mixing).astype(jnp.bfloat16)
    all_keys, all_values = fetched

    def one_head(parts):
        return side_head_back(parts[0], parts[1], parts[2], parts[3], parts[4], row_ids, key_ids)

    grad_query, key_terms, value_terms = lax.map(
        one_head,
        (
            split_heads(projected[:, :width]),
            split_heads(all_keys),
            split_heads(all_values),
            split_heads(grad_attended),
            log_total,
        ),
    )
    key_grad, value_grad = (
        lax.psum_scatter(
            join_heads(key_terms).astype(jnp.bfloat16), "tensor", scatter_dimension=0, tiled=True
        ).astype(jnp.float32),
        lax.psum_scatter(
            join_heads(value_terms).astype(jnp.bfloat16), "tensor", scatter_dimension=0, tiled=True
        ).astype(jnp.float32),
    )
    grad_projected = jnp.concatenate(
        [join_heads(grad_query), key_grad.astype(jnp.bfloat16), value_grad.astype(jnp.bfloat16)],
        axis=1,
    )
    project_grad = outer_sum(normed, grad_projected)
    grad_normed = back_product(grad_projected, project)
    _, norm_pull_one = jax.vjp(root_norm, mixed, gains[0])
    grad_mixed_norm, gain_one_grad = norm_pull_one(grad_normed)
    grad_mixed = grad_middle + grad_mixed_norm
    weight = jax.nn.sigmoid(gate)
    down_grad = outer_sum(frozen, (weight * grad_mixed).astype(jnp.bfloat16))
    gate_grad = jnp.sum(grad_mixed * (lifted - previous), axis=0) * weight * (1.0 - weight)
    grad_previous = (1.0 - weight) * grad_mixed
    layer_grads = (
        down_grad,
        gate_grad,
        jnp.stack([gain_one_grad, gain_two_grad]),
        project_grad,
        mixing_grad,
        expand_grad,
        reduce_grad,
    )
    return (grad_previous, layer_grads)


def per_device(
    hidden_rows,
    side_input,
    segment_ids,
    side_cotangent,
    backbone_gains,
    backbone_project,
    backbone_mixing,
    backbone_expand,
    backbone_reduce,
    side_down,
    side_gate,
    side_gains,
    side_project,
    side_mixing,
    side_expand,
    side_reduce,
):
    parts = lax.axis_size("tensor")
    qkv = jnp.pad(
        jnp.transpose(backbone_project, (0, 2, 1, 3)),
        ((0, 0), (0, 0), (0, 0), (0, 256 - backbone_project.shape[3])),
    )
    ids_row = segment_ids.reshape(1, -1)
    key_ids = None
    stream = hidden_rows
    state = side_input.astype(jnp.float32)
    records = []
    frozen_rows = []
    for layer in range(LAYERS):
        stream, frozen, gathered = backbone_call(
            layer,
            stream,
            ids_row,
            backbone_gains[layer],
            qkv,
            backbone_mixing,
            backbone_expand,
            backbone_reduce,
            parts,
        )
        key_ids = gathered[:, 0, :].reshape(-1) if key_ids is None else key_ids
        record, state = side_forward(
            state,
            frozen,
            side_down[layer],
            side_gate[layer],
            side_gains[layer].astype(jnp.float32),
            side_project[layer],
            side_mixing[layer],
            side_expand[layer],
            side_reduce[layer],
            segment_ids,
            key_ids,
        )
        records.append(record)
        frozen_rows.append(frozen)
    grad = side_cotangent.astype(jnp.float32)
    collected = [None] * LAYERS
    for layer in reversed(range(LAYERS)):
        grad, layer_grads = side_backward(
            grad,
            records[layer],
            frozen_rows[layer],
            side_gate[layer],
            side_gains[layer].astype(jnp.float32),
            side_project[layer],
            side_mixing[layer],
            side_expand[layer],
            side_reduce[layer],
            segment_ids,
            key_ids,
        )
        collected[layer] = layer_grads
    stacked = tuple(
        (jnp.stack([collected[layer][member] for layer in range(LAYERS)]) for member in range(7))
    )
    stacked = lax.psum(
        (stacked[0], stacked[1], stacked[2], stacked[3], stacked[4], stacked[5], stacked[6]),
        ("batch", "tensor"),
    )
    return (
        frozen_rows[-1],
        state,
        grad,
        stacked[0],
        stacked[1],
        stacked[2],
        stacked[3],
        stacked[4],
        stacked[5],
        stacked[6],
    )


def solution(mesh):
    return jax.shard_map(
        per_device,
        mesh=mesh,
        in_specs=(
            P(("batch", "tensor"), None),
            P(("batch", "tensor"), None),
            P(("batch", "tensor")),
            P(("batch", "tensor"), None),
            P(),
            P(None, None, None, "tensor"),
            P(None, "tensor", None),
            P(None, None, "tensor"),
            P(None, "tensor", None),
            P(),
            P(),
            P(),
            P(),
            P(),
            P(),
            P(),
        ),
        out_specs=(
            P(("batch", "tensor"), None),
            P(("batch", "tensor"), None),
            P(("batch", "tensor"), None),
            P(),
            P(),
            P(),
            P(),
            P(),
            P(),
            P(),
        ),
        check_vma=False,
    )
```

```python
import functools
import jax
import jax.numpy as jnp
from jax import lax
from jax.experimental import pallas as pl
from jax.experimental.pallas import tpu as pltpu
from jax.sharding import PartitionSpec as P

HEAD_DIM = 64
SIDE_HEADS = 12
SIDE_HEAD_DIM = 8
LAYERS = 2
EPS = 1e-06
BIG = 2.0**100
LOG2E = 1.4426950408889634
ID_BITS = 11
QUAD = 4
MESH = pl.DeviceIdType.MESH
F32 = jnp.float32
BF16 = jnp.bfloat16


def contract(left, right, dims):
    return lax.dot_general(left, right, ((dims[:1], dims[1:]), ((), ())), preferred_element_type=F32)


def nn(left, right):
    return contract(left, right, (1, 0))


def nt(left, right):
    return contract(left, right, (1, 1))


def tn(left, right):
    return contract(left, right, (0, 0))


def lanes_of(rows, lanes):
    return lax.broadcasted_iota(jnp.int32, (rows, lanes), 1)


def segment_lanes(id_row, offset):
    width = id_row.shape[1]
    place = lax.broadcasted_iota(jnp.int32, (128, width), 0) - offset
    flipped = place >= ID_BITS
    shift = jnp.clip(jnp.where(flipped, place - ID_BITS, place), 0, ID_BITS)
    bit = lax.shift_right_logical(jnp.broadcast_to(id_row, (128, width)), shift) & 1
    bit = jnp.where(flipped, 1 - bit, bit)
    used = (place >= 0) & (place < 2 * ID_BITS)
    keys = jnp.where(used, bit, 0).astype(F32)
    queries = jnp.where(used, (bit - 1).astype(F32) * BIG, 0.0)
    return keys.T, queries.T


def root_norm(values, gain):
    return values * lax.rsqrt(jnp.mean(values * values, axis=-1, keepdims=True) + EPS) * gain


class Refs:
    def __init__(self, **refs):
        self.__dict__.update(refs)


def remote(src, dst, send, recv, target):
    return pltpu.make_async_remote_copy(
        src_ref=src, dst_ref=dst, send_sem=send, recv_sem=recv, device_id=target, device_id_type=MESH
    )


class Weights:
    def __init__(self, layer, b, t, c):
        self.layer, self.b, self.t, self.c = layer, b, t, c
        self.part = lax.rem(b, QUAD)
        self.fulls = (c.mix_w, c.exp_w, c.red_w)
        self.sources = (c.mix_hbm, c.exp_hbm, c.red_hbm)
        self.slices = tuple(w.shape[2] // QUAD for w in self.fulls)
        mix, up, down = self.slices
        self.pieces = (
            (0, 0, mix),
            (1, 0, up // 2),
            (1, up // 2, up // 2),
            (2, 0, down // 2),
            (2, down // 2, down // 2),
        )

    def rows(self, p, part):
        w, low, size = self.pieces[p]
        return pl.ds(pl.multiple_of(part * self.slices[w] + low, 16), size)

    def view(self, p, slot, part):
        return self.fulls[self.pieces[p][0]].at[self.layer, slot, self.rows(p, part)]

    def load(self, w):
        return pltpu.make_async_copy(
            self.sources[w].at[self.layer],
            self.fulls[w].at[self.layer, self.t],
            self.c.load_sem.at[self.layer, w],
        )

    def own(self, w, slot):
        c = self.c
        return remote(
            self.sources[w].at[self.layer],
            self.fulls[w].at[self.layer, slot],
            c.own_send.at[self.layer, w],
            c.own_recv.at[self.layer, w],
            (self.b, self.t ^ 1),
        )

    def cross(self, p):
        c = self.c
        return remote(
            self.sources[self.pieces[p][0]].at[self.layer, self.rows(p, self.part)],
            self.view(p, self.t, self.part),
            c.cross_send.at[self.layer, p],
            c.w_recv.at[self.layer, p, self.part],
            (self.b, self.t ^ 2),
        )

    def spread(self, p, k):
        c = self.c
        view = self.view(p, self.t ^ 2, self.part)
        return remote(
            view, view, c.spread_send.at[self.layer, p, k - 1], c.w_recv.at[self.layer, p, self.part], (self.b ^ k, self.t)
        )

    def here(self, p, k):
        c = self.c
        view = self.view(p, self.t ^ 2, self.part ^ k)
        return remote(
            view, view, c.cross_send.at[self.layer, p], c.w_recv.at[self.layer, p, self.part ^ k], (self.b, self.t ^ 2)
        )

    def forward(self, p, k, slot):
        c = self.c
        view = self.view(p, slot, self.part ^ k)
        return remote(
            view,
            view,
            c.pass_send.at[self.layer, p, k],
            c.pass_recv.at[self.layer, p, self.part ^ k],
            (self.b, self.t ^ 1),
        )

    def start_cross(self):
        for p in range(5):
            self.cross(p).start()

    def start_spread(self, p):
        self.here(p, 0).wait_recv()
        for k in range(1, QUAD):
            self.spread(p, k).start()

    def start_forward(self, p):
        for k in range(1, QUAD):
            self.here(p, k).wait_recv()
        for k in range(QUAD):
            self.forward(p, k, self.t ^ 2).start()

    def wait_far(self, p):
        for k in range(QUAD):
            self.forward(p, k, self.t ^ 3).wait_recv()

    def wait_sent(self):
        for w in range(3):
            self.own(w, self.t).wait_send()
        for p in range(5):
            self.cross(p).wait_send()
            for k in range(1, QUAD):
                self.spread(p, k).wait_send()
            for k in range(QUAD):
                self.forward(p, k, self.t ^ 2).wait_send()


class Backbone:
    def __init__(self, layer, b, t, parts, c):
        self.layer, self.b, self.t, self.parts, self.c = layer, b, t, parts, c
        self.sib, self.across, self.far = t ^ 1, t ^ 2, t ^ 3
        self.tokens = c.rows_all.shape[1]
        self.half = self.tokens // 2
        self.width = c.mix_w.shape[2]
        self.heads = self.width // HEAD_DIM
        self.weights = Weights(layer, b, t, c)

    def row_copy(self, slot, chunk, send, target):
        c = self.c
        view = c.rows_all.at[slot, pl.ds(chunk * self.half, self.half)]
        return remote(
            view,
            view,
            c.row_send.at[self.layer, send, chunk],
            c.row_recv.at[self.layer, slot, chunk],
            (self.b, target),
        )

    def send_rows(self, stream):
        c = self.c
        gain = c.gains[self.layer, 0:1, :].astype(F32)
        c.rows_all[self.t] = root_norm(stream, gain).astype(BF16)
        for chunk in range(2):
            self.row_copy(self.t, chunk, 1, self.across).start()
        for chunk in range(2):
            self.row_copy(self.t, chunk, 0, self.sib).start()

    def project(self, slot, chunk):
        c, width, half = self.c, self.width, self.half
        inside = pl.ds(pl.multiple_of(chunk * half, half), half)
        rows = c.rows_all[slot, inside, :]
        at = pl.ds(pl.multiple_of(slot * self.tokens + chunk * half, half), half)
        key_bits, query_bits = segment_lanes(c.ids_all[slot, 0:1, inside], width - 128)
        query = nt(rows, c.qkv_w[self.layer, 0]) * (HEAD_DIM**-0.5 * LOG2E)
        keys = nt(rows, c.qkv_w[self.layer, 1])
        c.q_s[at, 0:128] = query[:, 0:128].astype(BF16)
        c.q_s[at, 128:256] = (query[:, 128:256] + query_bits).astype(BF16)
        c.k_s[at, 0:128] = keys[:, 0:128].astype(BF16)
        c.k_s[at, 128:256] = (keys[:, 128:256] + key_bits).astype(BF16)
        values = nt(c.qkv_w[self.layer, 2, 0:width], rows)
        for h in range(self.heads):
            c.vt_s[h, 0:HEAD_DIM, at] = values[h * HEAD_DIM : (h + 1) * HEAD_DIM].astype(BF16)
            c.vt_s[h, HEAD_DIM:, at] = jnp.ones((16, half), BF16)

    def project_all(self, hook):
        def step(index, carry):
            for chunk in range(2):

                @pl.when(index == 2 + chunk)
                def _():
                    self.row_copy(self.sib, chunk, 0, self.sib).wait_recv()

                @pl.when(index == 4 + 2 * chunk)
                def _():
                    self.row_copy(self.across, chunk, 0, self.sib).wait_recv()
                    self.row_copy(self.across, chunk, 2, self.sib).start()

                @pl.when(index == 5 + 2 * chunk)
                def _():
                    self.row_copy(self.far, chunk, 0, self.sib).wait_recv()

            hook(index)
            early = index < 4
            k = jnp.where(early, index // 2, 2 + index % 2)
            chunk = jnp.where(early, index % 2, index // 2 - 2)
            self.project(self.t ^ k, chunk)
            return carry

        lax.fori_loop(0, 2 * self.parts, step, 0)
        for chunk in range(2):
            self.row_copy(self.t, chunk, 0, self.sib).wait_send()
            self.row_copy(self.t, chunk, 1, self.across).wait_send()
            self.row_copy(self.across, chunk, 2, self.sib).wait_send()

    def block_of(self, item):
        return self.t ^ (self.parts - 1 - item // self.heads)

    def make_scores(self, item, place):
        c = self.c
        h = lax.rem(item, self.heads)
        rows = c.q_s[pl.ds(pl.multiple_of(self.block_of(item) * self.tokens, self.tokens), self.tokens), :]
        lane = lanes_of(self.tokens, 256)
        chosen = (lane // HEAD_DIM == h) | (lane >= self.width)
        c.scores[place] = nt(c.k_s[...], jnp.where(chosen, rows, jnp.zeros_like(rows)))

    def send_heads(self, block):
        c = self.c
        return remote(
            c.heads_buf.at[block],
            c.heads_buf.at[self.parts + self.t],
            c.head_send.at[self.layer, block],
            c.head_recv.at[self.layer, self.t],
            (self.b, block),
        )

    def attend(self, item, place):
        c = self.c
        block = self.block_of(item)
        h = lax.rem(item, self.heads)
        values = c.scores[place]
        weights = jnp.exp2(values - jnp.max(values, axis=0, keepdims=True)).astype(BF16)
        out = nn(c.vt_s[h], weights)
        slot = jnp.where(block == self.t, self.parts + self.t, block)
        c.heads_buf[slot, pl.ds(pl.multiple_of(h * HEAD_DIM, HEAD_DIM), HEAD_DIM), :] = (
            out[0:HEAD_DIM] * (1.0 / out[HEAD_DIM : HEAD_DIM + 1])
        ).astype(BF16)

        @pl.when((h == self.heads - 1) & (item < (self.parts - 1) * self.heads))
        def _():
            self.send_heads(block).start()

    def attention(self, hook):
        count = self.parts * self.heads
        self.make_scores(0, 0)

        def pair(index, carry):
            item = 2 * index
            hook(index)
            self.make_scores(item + 1, 1)
            self.attend(item, 0)
            self.make_scores(jnp.minimum(item + 2, count - 1), 0)
            self.attend(item + 1, 1)
            return carry

        lax.fori_loop(0, count // 2, pair, 0)

    def wait_heads(self):
        c = self.c
        for k in range(1, self.parts):
            self.send_heads(self.t ^ k).wait_send()
            remote(
                c.heads_buf.at[0],
                c.heads_buf.at[self.parts + (self.t ^ k)],
                c.head_send.at[self.layer, 0],
                c.head_recv.at[self.layer, self.t ^ k],
                (self.b, self.sib),
            ).wait_recv()

    def feed_forward(self, stream, hook):
        c, parts, layer = self.c, self.parts, self.layer
        attended = c.heads_buf[parts : 2 * parts].reshape(parts * self.width, self.tokens)
        stream = stream + tn(attended, c.mix_w[layer].reshape(parts * self.width, -1))
        c.acc[...] = stream
        c.normed[...] = root_norm(stream, c.gains[layer, 1:2, :].astype(F32)).astype(BF16)

        def feed(index, carry):
            hook(index)
            hidden = jax.nn.gelu(nn(c.normed[...], c.exp_w[layer, self.t ^ index])).astype(BF16)
            c.acc[...] += nn(hidden, c.red_w[layer, self.t ^ index])
            return carry

        lax.fori_loop(0, parts, feed, 0)


FRONT_SCRATCH = (
    *("vectors", "rows_all", "ids_scratch", "qkv_w", "mix_w", "exp_w", "red_w", "q_s", "k_s", "vt_s", "scores"),
    *("heads_buf", "acc", "normed", "load_sem", "qkv_sem", "row_send", "row_recv", "id_send", "id_recv"),
    *("head_send", "head_recv", "cross_send", "spread_send", "pass_send", "own_send", "w_recv", "pass_recv"),
    *("own_recv", "side_vt", "kv_send", "kv_recv"),
)


def front_kernel(parts, *refs):
    refs = list(refs)

    def pop(count):
        taken, refs[:count] = refs[:count], []
        return taken

    x_ref, ids_ref, gains, qkv_hbm, mix_hbm, exp_hbm, red_hbm, side_in = pop(8)
    raw = Refs(**dict(zip(RAW, pop(7))))
    first_f, second_f, ids_all, state_one, kvt = pop(5)
    keep = Refs(**dict(zip(KEEP, pop(6))))
    prev = pop(1)[0]
    w = Refs(**dict(zip(WEIGHTS, pop(5))))
    c = Refs(**dict(zip(FRONT_SCRATCH, pop(len(FRONT_SCRATCH)))))
    c.gains, c.mix_hbm, c.exp_hbm, c.red_hbm, c.ids_all = gains, mix_hbm, exp_hbm, red_hbm, ids_all
    b = lax.axis_index("batch")
    t = lax.axis_index("tensor")
    tokens = x_ref.shape[0]
    width = c.mix_w.shape[2]
    lower, upper = Backbone(0, b, t, parts, c), Backbone(1, b, t, parts, c)
    load_qkv = [
        pltpu.make_async_copy(
            qkv_hbm.at[layer, k], c.qkv_w.at[layer, k, pl.ds(0, width)], c.qkv_sem.at[layer, k]
        )
        for layer in range(LAYERS)
        for k in range(3)
    ]
    for copy in load_qkv:
        copy.start()
    for layer in (lower, upper):
        for k in range(3):
            layer.weights.load(k).start()
    barrier = tensor_barrier(b, t, parts)
    for k in range(1, QUAD):
        pl.semaphore_signal(barrier, inc=1, device_id=(b ^ k, t), device_id_type=MESH)
    pl.semaphore_wait(barrier, parts - 1 + QUAD - 1)

    def id_copy(slot, k):
        return remote(ids_all.at[slot], ids_all.at[slot], c.id_send.at[k - 1], c.id_recv.at[slot], (b, t ^ k))

    ids_all[t] = jnp.broadcast_to(ids_ref[...], (8, tokens))
    for k in range(1, parts):
        id_copy(t, k).start()
    lower.send_rows(x_ref[...].astype(F32))
    for layer in (lower, upper):
        for k in range(3):
            layer.weights.own(k, t).start()
    c.qkv_w[:, :, width:, :] = jnp.zeros((LAYERS, 3, 256 - width, x_ref.shape[1]), BF16)
    for copy in load_qkv:
        copy.wait()
    load_side_weights(0, w, raw)
    load_vectors(c.vectors, raw)
    raw.vectors = c.vectors
    prev[...] = widened(side_in)
    for k in range(1, parts):
        id_copy(t, k).wait_send()
        id_copy(t ^ k, k).wait_recv()

    def when(index, at, act, *args):
        @pl.when(index == at)
        def _():
            act(*args)

    def lower_project(index):
        when(index, 6, lower.weights.start_cross)

    def lower_attention(index):
        for p in range(5):
            when(index, p, lower.weights.start_spread, p)
        when(index, 3, lower.weights.start_forward, 0)
        when(index, 5, lower.weights.start_forward, 1)

    def feed_hook(layer):
        def hook(index):
            weights = layer.weights

            @pl.when(index == 0)
            def _():
                for k in (1, 2):
                    weights.load(k).wait()
                if layer is lower:
                    weights.start_forward(2)

            @pl.when(index == 1)
            def _():
                for k in (1, 2):
                    weights.own(k, layer.sib).wait_recv()
                if layer is lower:
                    weights.start_forward(3)

            @pl.when(index == 2)
            def _():
                if layer is lower:
                    weights.start_forward(4)

            @pl.when(index == 3)
            def _():
                for p in range(1, 5):
                    weights.wait_far(p)

        return hook

    lower.project_all(lower_project)
    lower.attention(lower_attention)
    upper.weights.start_cross()
    lower.weights.load(0).wait()
    lower.weights.own(0, lower.sib).wait_recv()
    lower.weights.wait_far(0)
    lower.wait_heads()
    lower.feed_forward(x_ref[...].astype(F32), feed_hook(lower))
    first_f[...] = c.acc[...].astype(BF16)

    side = Refs(
        kvt=kvt, k_s=c.k_s, vt_s=c.side_vt, scores=c.scores, kv_send=c.kv_send, kv_recv=c.kv_recv
    )

    def side_hook(index):
        for p in range(5):
            when(index, p, upper.weights.start_spread, p)

    side_forward(
        0, b, t, parts, first_f, prev, w, raw, side, keep, ids_all, state_one,
        lambda: upper.send_rows(c.acc[...]), side_hook,
    )

    def upper_attention(index):
        for p in range(5):
            when(index, p + 1, upper.weights.start_forward, p)

    upper.project_all(lambda index: None)
    upper.attention(upper_attention)
    upper.weights.load(0).wait()
    upper.weights.own(0, upper.sib).wait_recv()
    upper.weights.wait_far(0)
    upper.wait_heads()
    upper.feed_forward(c.acc[...], feed_hook(upper))
    second_f[...] = c.acc[...].astype(BF16)
    lower.weights.wait_sent()
    upper.weights.wait_sent()


def front_call(x, ids, gains, qkv, mix, exp, red, side_in, raw, parts):
    tokens, model = x.shape
    width = mix.shape[1]
    units = exp.shape[2]
    heads = width // HEAD_DIM
    length = parts * tokens
    side_units = raw[5].shape[2]
    anywhere = pl.BlockSpec(memory_space=pl.ANY)
    dma = pltpu.SemaphoreType.DMA
    vmem = pltpu.VMEM
    outs = (
        ((tokens, model), BF16),
        ((tokens, model), BF16),
        ((parts, 8, tokens), jnp.int32),
        ((tokens, 128), F32),
        ((parts, 192, tokens), BF16),
        *keep_shapes(tokens),
    )
    return pl.pallas_call(
        functools.partial(front_kernel, parts),
        out_shape=tuple(jax.ShapeDtypeStruct(*o) for o in outs),
        in_specs=vmem_specs(3) + [anywhere] * 4 + vmem_specs(8),
        out_specs=tuple(vmem_specs(len(outs))),
        scratch_shapes=[
            vmem((tokens, 128), F32),
            *weight_scratch(model, side_units),
            vmem((LAYERS, 8, 128), F32),
            vmem((parts, tokens, model), BF16),
            vmem((8, 128), F32),
            vmem((LAYERS, 3, 256, model), BF16),
            vmem((LAYERS, parts, width, model), BF16),
            vmem((LAYERS, parts, model, units), BF16),
            vmem((LAYERS, parts, units, model), BF16),
            vmem((length, 256), BF16),
            vmem((length, 256), BF16),
            vmem((heads, HEAD_DIM + 16, length), BF16),
            vmem((2, length, tokens), F32),
            vmem((2 * parts, width, tokens), BF16),
            vmem((tokens, model), F32),
            vmem((tokens, model), BF16),
            dma((LAYERS, 3)),
            dma((LAYERS, 3)),
            dma((LAYERS, 3, 2)),
            dma((LAYERS, parts, 2)),
            dma((parts - 1,)),
            dma((parts,)),
            dma((LAYERS, parts)),
            dma((LAYERS, parts)),
            dma((LAYERS, 5)),
            dma((LAYERS, 5, QUAD - 1)),
            dma((LAYERS, 5, QUAD)),
            dma((LAYERS, 3)),
            dma((LAYERS, 5, QUAD)),
            dma((LAYERS, 5, QUAD)),
            dma((LAYERS, 3)),
            vmem((SIDE_HEADS, 16, length), BF16),
            dma((3,)),
            dma((parts,)),
        ],
        compiler_params=pltpu.CompilerParams(
            collective_id=1, has_side_effects=True, vmem_limit_bytes=62 << 20
        ),
    )(x, ids, gains, qkv, mix, exp, red, side_in, *raw)


LN2 = 0.6931471805599453
COLUMNS = 16
RING = 8


def side_norm(values, width):
    rstd = lax.rsqrt(jnp.sum(values * values, axis=-1, keepdims=True) * (1.0 / width) + EPS)
    return values * rstd, rstd


def gelu_parts(inner):
    root = 0.7978845608028654
    square = inner * inner
    curve = jnp.tanh(root * inner * (1.0 + 0.044715 * square))
    half = 0.5 * (1.0 + curve)
    slope = half + 0.5 * inner * (1.0 - curve * curve) * root * (1.0 + 3 * 0.044715 * square)
    return inner * half, slope


def load_side_weights(layer, w, raw):
    side = raw.mixing.shape[1]
    w.down[side:, :] = jnp.zeros_like(w.down[side:, :])
    w.down[0:side, :] = raw.down[layer]
    w.project[...] = jnp.zeros_like(w.project)
    w.project[0:side, 0 : 3 * side] = raw.project[layer]
    w.mixing[...] = jnp.zeros_like(w.mixing)
    w.mixing[0:side, 0:side] = raw.mixing[layer]
    w.expand[side:, :] = jnp.zeros_like(w.expand[side:, :])
    w.expand[0:side, :] = raw.expand[layer]
    w.reduce[side:, :] = jnp.zeros_like(w.reduce[side:, :])
    w.reduce[0:side, :] = raw.reduce[layer]


def load_vectors(vectors, raw):
    side = raw.mixing.shape[1]
    vectors[...] = jnp.zeros_like(vectors)
    for layer in range(LAYERS):
        vectors[layer, 0:1, 0:side] = raw.gate[layer : layer + 1, :]
        vectors[layer, 1:3, 0:side] = raw.gains[layer].astype(F32)


def widened(turned):
    values = turned[...].astype(F32)
    return jnp.concatenate([values, jnp.zeros((32, values.shape[1]), F32)], axis=0).T


def kv_copy(c, slot, send, target):
    return remote(c.kvt.at[slot], c.kvt.at[slot], c.kv_send.at[send], c.kv_recv.at[slot], target)


def keys_from(c, slot, ids_ref):
    tokens = c.kvt.shape[2]
    at = pl.ds(pl.multiple_of(slot * tokens, tokens), tokens)
    key_bits, _ = segment_lanes(ids_ref[slot][0:1, :], 96)
    keys = jnp.concatenate([c.kvt[slot, 0:96].astype(F32), jnp.zeros((32, tokens), F32)], axis=0)
    c.k_s[at, 0:128] = (keys.T + key_bits).astype(BF16)


def side_forward(layer, b, t, parts, f_ref, prev, w, raw, c, keep, ids_ref, result, after_send, between):
    side = raw.mixing.shape[1]
    tokens = f_ref.shape[0]
    gate = jax.nn.sigmoid(raw.vectors[layer, 0:1, :])
    lifted = nt(f_ref[...], w.down[...])
    mixed = gate * lifted + (1.0 - gate) * prev[...]
    keep.lifted[...] = lifted
    keep.mixed[...] = mixed
    normed = (side_norm(mixed, side)[0] * raw.vectors[layer, 1:2, :]).astype(BF16)
    turned = w.project[...].astype(F32).T.astype(BF16)
    c.kvt[t] = nt(turned[side : 3 * side], normed).astype(BF16)
    sib, across, far = t ^ 1, t ^ 2, t ^ 3
    kv_copy(c, t, 1, (b, across)).start()
    kv_copy(c, t, 0, (b, sib)).start()
    after_send()
    lane = lanes_of(tokens, 128)
    weight_q = jnp.where(lanes_of(128, 128) < side, w.project[:, 0:128], jnp.zeros((128, 128), BF16))
    query_bits = segment_lanes(ids_ref[t][0:1, :], 96)[1]
    keep.query[...] = (
        nn(normed, weight_q) * (SIDE_HEAD_DIM**-0.5 * LOG2E) + query_bits
    ).astype(BF16)
    keep.sums[...] = jnp.zeros_like(keep.sums)

    def take(index, carry):
        @pl.when(index == 1)
        def _():
            kv_copy(c, sib, 0, (b, sib)).wait_recv()

        @pl.when(index == 2)
        def _():
            kv_copy(c, across, 0, (b, sib)).wait_recv()
            kv_copy(c, across, 2, (b, sib)).start()

        @pl.when(index == 3)
        def _():
            kv_copy(c, far, 0, (b, sib)).wait_recv()

        slot = t ^ index
        at = pl.ds(pl.multiple_of(slot * tokens, tokens), tokens)
        keys_from(c, slot, ids_ref)
        values = c.kvt[slot, 96:192].astype(F32)
        for h in range(SIDE_HEADS):
            c.vt_s[h, :, at] = jnp.concatenate(
                [values[8 * h : 8 * h + 8], jnp.ones((8, tokens), F32)], axis=0
            ).astype(BF16)
        return carry

    lax.fori_loop(0, parts, take, 0)

    def make_scores(h, place):
        rows = keep.query[...]
        chosen = (lane // SIDE_HEAD_DIM == h) | (lane >= side)
        c.scores[place] = nt(c.k_s[:, 0:128], jnp.where(chosen, rows, jnp.zeros_like(rows)))

    def attend(h, place):
        values = c.scores[place]
        top = jnp.max(values, axis=0, keepdims=True)
        out = nn(c.vt_s[h], jnp.exp2(values - top).astype(BF16))
        total = out[8:9]
        keep.heads[pl.ds(pl.multiple_of(h * 8, 8), 8), :] = out[0:8] * (1.0 / total)
        here = lax.broadcasted_iota(jnp.int32, keep.sums.shape, 0) == h
        keep.sums[...] = jnp.where(here, top + jnp.log2(total), keep.sums[...])

    make_scores(0, 0)

    def pair(index, carry):
        h = 2 * index
        between(index)
        make_scores(h + 1, 1)
        attend(h, 0)
        make_scores(jnp.minimum(h + 2, SIDE_HEADS - 1), 0)
        attend(h + 1, 1)
        return carry

    lax.fori_loop(0, SIDE_HEADS // 2, pair, 0)
    kv_copy(c, t, 1, (b, across)).wait_send()
    kv_copy(c, t, 0, (b, sib)).wait_send()
    kv_copy(c, across, 2, (b, sib)).wait_send()
    middle = mixed + tn(keep.heads[...].astype(BF16), w.mixing[0:side, :])
    keep.middle[...] = middle
    normed_two = (side_norm(middle, side)[0] * raw.vectors[layer, 2:3, :]).astype(BF16)
    active = jax.nn.gelu(nn(normed_two, w.expand[...])).astype(BF16)
    result[...] = middle + nt(active, w.reduce[...])


def norm_back(values, gain, grad, side):
    hat, rstd = side_norm(values, side)
    gain_grad = jnp.sum(grad * hat, axis=0, keepdims=True)
    pulled = grad * gain
    mean = jnp.sum(pulled * hat, axis=-1, keepdims=True) * (1.0 / side)
    return rstd * (pulled - hat * mean), gain_grad


def pad_heads(target, rows, fill):
    for h in range(SIDE_HEADS):
        target[h] = jnp.concatenate(
            [rows[8 * h : 8 * h + 8], jnp.full((8, rows.shape[1]), fill, F32)], axis=0
        ).astype(BF16)


def side_backward(layer, b, t, parts, f_ref, prev, w, raw, c, keep, kvt, ids_ref, grad_ref, pack, between, again):
    side = raw.mixing.shape[1]
    tokens = f_ref.shape[0]
    gate = jax.nn.sigmoid(raw.vectors[layer, 0:1, :])
    lane = lanes_of(tokens, 128)
    grad = grad_ref[...]
    middle = keep.middle[...]
    gain_two = raw.vectors[layer, 2:3, :]
    normed_two = (side_norm(middle, side)[0] * gain_two).astype(BF16)
    active, slope = gelu_parts(nn(normed_two, w.expand[...]))
    top = grad.astype(BF16)
    reduce_grad = tn(top, active.astype(BF16))
    grad_inner = (slope * nn(top, w.reduce[...])).astype(BF16)
    expand_grad = tn(normed_two, grad_inner)
    for k in range(3):
        pack[6 + k] = expand_grad[0:96, 128 * k : 128 * k + 128]
        pack[9 + k] = reduce_grad[0:96, 128 * k : 128 * k + 128]
    through, gain_two_grad = norm_back(middle, gain_two, nt(grad_inner, w.expand[...]), side)
    grad_middle = grad + through
    branch = grad_middle.astype(BF16)
    heads = keep.heads[...]
    mixing_grad = nn(heads.astype(BF16), branch)
    grad_heads = nt(branch, w.mixing[...]).astype(BF16).astype(F32).T
    product = grad_heads[0:96] * heads
    group = lax.broadcasted_iota(jnp.int32, (16, 96), 1) // SIDE_HEAD_DIM
    group = (group == lax.broadcasted_iota(jnp.int32, (16, 96), 0)).astype(BF16)
    high = product.astype(BF16)
    inner = nn(group, high) + nn(group, (product - high.astype(F32)).astype(BF16))
    rows = jnp.concatenate([grad_heads[0:96], -inner, -inner], axis=0).T
    high = rows.astype(BF16)
    c.do_s[...] = jnp.where(lane < 112, high, (rows - high.astype(F32)).astype(BF16))
    pad_heads(c.dot_s, grad_heads, 0.0)
    sums = keep.sums[...]
    rows = jnp.concatenate([sums, sums, sums, jnp.zeros((80, tokens), F32)], axis=0).T
    high = rows.astype(BF16).astype(F32)
    mid = (rows - high).astype(BF16).astype(F32)
    low = rows - high - mid
    rows = jnp.where(lane < 16, high, jnp.where(lane < 32, mid, low))
    query = keep.query[...]
    c.q_s[:, 0:128] = query
    c.q_s[:, 128:256] = jnp.where(lane < 48, -rows, 0.0).astype(BF16)
    pad_heads(c.qt_s, query.astype(F32).T, 0.0)

    def take(slot, carry):
        at = pl.ds(pl.multiple_of(slot * tokens, tokens), tokens)
        if again:
            keys_from(Refs(kvt=kvt, k_s=c.k_s), slot, ids_ref)
        c.k_s[at, 128:256] = jnp.where(lane < 48, 1.0, 0.0).astype(BF16)
        values = jnp.concatenate(
            [kvt[slot, 96:192].astype(F32), jnp.ones((32, tokens), F32)], axis=0
        )
        c.v_s[at, :] = values.T.astype(BF16)
        keys = kvt[slot, 0:96].astype(F32)
        for h in range(SIDE_HEADS):
            c.kt_s[h, :, at] = jnp.concatenate(
                [keys[8 * h : 8 * h + 8], jnp.zeros((8, tokens), F32)], axis=0
            ).astype(BF16)
        return carry

    lax.fori_loop(0, parts, take, 0)
    wide = lanes_of(tokens, 256)
    query_head = jnp.where(wide < 96, wide // SIDE_HEAD_DIM, jnp.where(wide < 128, -1, (wide - 128) % 16))
    out_head = jnp.where(lane < 96, lane // SIDE_HEAD_DIM, (lane - 96) % 16)

    def one_head(h):
        rows = c.q_s[...]
        rows = jnp.where((query_head == h) | (query_head < 0), rows, jnp.zeros_like(rows))
        probs = jnp.exp2(nt(rows, c.k_s[...]))
        rows = c.do_s[...]
        rows = jnp.where(out_head == h, rows, jnp.zeros_like(rows))
        scores = (probs * nt(rows, c.v_s[...])).astype(BF16)
        keys = nn(c.qt_s[h], scores)[0:8] * LN2
        values = nn(c.dot_s[h], probs.astype(BF16))[0:8]
        queries = nt(c.kt_s[h], scores)[0:8] * SIDE_HEAD_DIM**-0.5
        return keys, values, queries

    def terms_copy(pair, k):
        return remote(
            c.terms.at[pair, t ^ k],
            c.terms_in.at[layer, pair, t],
            c.terms_send.at[layer, pair, k - 1],
            c.terms_recv.at[layer, pair, t],
            (b, t ^ k),
        )

    def terms_wait(pair, k):
        return remote(
            c.terms.at[pair, t ^ k],
            c.terms_in.at[layer, pair, t ^ k],
            c.terms_send.at[layer, pair, k - 1],
            c.terms_recv.at[layer, pair, t ^ k],
            (b, t ^ k),
        )

    def pair_of(index, carry):
        between(index)
        first = one_head(2 * index)
        second = one_head(2 * index + 1)
        keys, values, queries = (
            jnp.concatenate([left, right], axis=0).astype(BF16) for left, right in zip(first, second)
        )
        at = pl.ds(pl.multiple_of(index * 16, 16), 16)
        c.dqkv[at, :] = queries
        for slot in range(parts):
            c.terms[index, slot, 0:16] = keys[:, slot * tokens : (slot + 1) * tokens]
            c.terms[index, slot, 16:32] = values[:, slot * tokens : (slot + 1) * tokens]
        for k in range(1, parts):
            terms_copy(index, k).start()
        return carry

    pairs = SIDE_HEADS // 2
    lax.fori_loop(0, pairs, pair_of, 0)
    mixed = keep.mixed[...]
    gain_one = raw.vectors[layer, 1:2, :]
    normed = side_norm(mixed, side)[0] * gain_one
    c.dqkv[288:384, :] = jnp.zeros((96, tokens), BF16)

    def gather(index, carry):
        total = c.terms[index, t].astype(F32)
        for k in range(1, parts):
            terms_wait(index, k).wait_recv()
            total += c.terms_in[layer, index, t ^ k].astype(F32)
        total = total.astype(BF16)
        c.dqkv[pl.ds(pl.multiple_of(96 + index * 16, 16), 16), :] = total[0:16]
        c.dqkv[pl.ds(pl.multiple_of(192 + index * 16, 16), 16), :] = total[16:32]
        return carry

    lax.fori_loop(0, pairs, gather, 0)
    dqkv = c.dqkv[...]
    project_grad = nt(normed.T.astype(BF16), dqkv)
    grad_normed = nn(w.project[...], dqkv).T
    through, gain_one_grad = norm_back(mixed, gain_one, grad_normed, side)
    grad_mixed = grad_middle + through
    pack[12] = project_grad[0:96, 0:128]
    pack[13] = project_grad[0:96, 128:256]
    pack[14] = project_grad[0:96, 256:384] + pltpu.roll(mixing_grad, 32, 1)
    down_grad = nn((gate * grad_mixed).T.astype(BF16), f_ref[...])
    for k in range(6):
        pack[k] = down_grad[0:96, 128 * k : 128 * k + 128]
    gate_grad = jnp.sum(grad_mixed * (keep.lifted[...] - prev[...]), axis=0, keepdims=True)
    gate_grad = gate_grad * gate * (1.0 - gate)
    row = lax.broadcasted_iota(jnp.int32, (96, 128), 0)
    pack[15] = jnp.where(
        row == 0, gate_grad, jnp.where(row == 1, gain_one_grad, jnp.where(row == 2, gain_two_grad, 0.0))
    )
    grad_ref[...] = (1.0 - gate) * grad_mixed

    def sent(index, carry):
        for k in range(1, parts):
            terms_copy(index, k).wait_send()
        return carry

    lax.fori_loop(0, pairs, sent, 0)


class Sum:
    def __init__(self, r, b, t, parts, batch, pack, s):
        self.r, self.b, self.t, self.parts, self.batch, self.pack, self.s = r, b, t, parts, batch, pack, s
        self.place = lax.rem(b, RING)
        self.outer = batch // RING

    def across_tensor(self, k):
        r, s, t = self.r, self.s, self.t
        group = COLUMNS // self.parts
        return remote(
            s.out.at[r, pl.ds((t ^ k) * group, group)], s.one.at[r, t], s.one_send.at[r, k - 1],
            s.one_recv.at[r, t], (self.b, t ^ k),
        )

    def from_tensor(self, k):
        r, s, t = self.r, self.s, self.t
        return remote(
            s.one.at[r, t ^ k], s.one.at[r, t ^ k], s.one_send.at[r, k - 1], s.one_recv.at[r, t ^ k],
            (self.b, t ^ k),
        )

    def across_batch(self, k):
        r, s = self.r, self.s
        return remote(
            s.mid_out.at[r, self.place ^ k], s.two.at[r, self.place], s.two_send.at[r, k - 1],
            s.two_recv.at[r, self.place], (self.b ^ k, self.t),
        )

    def from_batch(self, k):
        r, s = self.r, self.s
        return remote(
            s.two.at[r, self.place ^ k], s.two.at[r, self.place ^ k], s.two_send.at[r, k - 1],
            s.two_recv.at[r, self.place ^ k], (self.b ^ k, self.t),
        )

    def across_outer(self, k):
        r, s = self.r, self.s
        mine = self.b // RING
        target = lax.rem(mine + k, self.outer) * RING + self.place
        return remote(
            s.far.at[r, mine], s.far.at[r, mine], s.far_send.at[r, k - 1], s.far_recv.at[r, mine], (target, self.t)
        )

    def from_outer(self, k):
        r, s = self.r, self.s
        other = lax.rem(self.b // RING + k, self.outer)
        return remote(
            s.far.at[r, other], s.far.at[r, other], s.far_send.at[r, k - 1], s.far_recv.at[r, other],
            (self.b ^ 1, self.t),
        )

    def back_batch(self, k, place):
        r, s = self.r, self.s
        return remote(
            s.full.at[r, self.t, place], s.full.at[r, self.t, place], s.three_send.at[r, k - 1],
            s.three_recv.at[r, place], (self.b ^ k, self.t),
        )

    def back_tensor(self, k, slot):
        r, s = self.r, self.s
        return remote(
            s.full.at[r, slot], s.full.at[r, slot], s.four_send.at[r, k - 1], s.four_recv.at[r, slot],
            (self.b, self.t ^ k),
        )

    def step_one(self):
        self.s.out[self.r] = self.pack[...].astype(BF16)
        for k in range(1, self.parts):
            self.across_tensor(k).start()

    def step_two(self):
        r, s = self.r, self.s
        group = COLUMNS // self.parts
        total = self.pack[pl.ds(self.t * group, group)]
        for k in range(1, self.parts):
            self.from_tensor(k).wait_recv()
            total += s.one[r, self.t ^ k].astype(F32)
        total = total.reshape(RING, total.shape[0] * total.shape[1] // RING, 128)
        s.mid[r] = total
        s.mid_out[r] = total.astype(BF16)
        for k in range(1, RING):
            self.across_batch(k).start()

    def step_three(self):
        r, s = self.r, self.s
        total = s.mid[r, self.place]
        for k in range(1, RING):
            self.from_batch(k).wait_recv()
            total += s.two[r, self.place ^ k].astype(F32)
        if self.outer > 1:
            s.far[r, self.b // RING] = total.astype(BF16)
            for k in range(1, self.outer):
                self.across_outer(k).start()
            for k in range(1, self.outer):
                self.from_outer(k).wait_recv()
            total = s.far[r, 0].astype(F32)
            for other in range(1, self.outer):
                total += s.far[r, other].astype(F32)
            for k in range(1, self.outer):
                self.across_outer(k).wait_send()
        s.full[r, self.t, self.place] = total.astype(BF16)
        for k in range(1, RING):
            self.back_batch(k, self.place).start()

    def step_four(self):
        for k in range(1, RING):
            self.back_batch(k, self.place ^ k).wait_recv()
        for k in range(1, self.parts):
            self.back_tensor(k, self.t).start()

    def step_five(self):
        for k in range(1, self.parts):
            self.back_tensor(k, self.t ^ k).wait_recv()
        for k in range(1, self.parts):
            self.across_tensor(k).wait_send()
            self.back_tensor(k, self.t).wait_send()
        for k in range(1, RING):
            self.across_batch(k).wait_send()
            self.back_batch(k, self.place).wait_send()


def finish_kernel(parts, frozen, state, grad, full, *refs):
    outs = Refs(**dict(zip(("frozen", "state", "grad", *OUTS), refs)))
    outs.frozen[...] = frozen[...]
    outs.state[...] = state[...].T[0:96]
    outs.grad[...] = grad[...].T[0:96]
    per = COLUMNS // parts
    for layer in range(LAYERS):

        def column(index):
            both = full[layer, index // per, 2 * (index % per) : 2 * (index % per) + 2]
            return both.astype(F32).reshape(96, 128)

        for k in range(6):
            outs.down[layer, :, 128 * k : 128 * k + 128] = column(k)
        for k in range(3):
            outs.expand[layer, :, 128 * k : 128 * k + 128] = column(6 + k)
            outs.reduce[layer, :, 128 * k : 128 * k + 128] = column(9 + k)
        outs.project[layer, :, 0:128] = column(12)
        outs.project[layer, :, 128:256] = column(13)
        last = column(14)
        outs.project[layer, :, 256:288] = last[:, 0:32]
        outs.mixing[layer] = pltpu.roll(last, 96, 1)[:, 0:96]
        small = column(15)
        outs.gate[layer : layer + 1, :] = small[0:1, 0:96]
        outs.gains[layer] = small[1:3, 0:96]


RAW = ("gate", "gains", "down", "project", "mixing", "expand", "reduce")
WEIGHTS = RAW[2:]
KEEP = ("lifted", "mixed", "query", "sums", "heads", "middle")


def keep_shapes(tokens):
    return (
        ((tokens, 128), F32),
        ((tokens, 128), F32),
        ((tokens, 128), BF16),
        ((16, tokens), F32),
        ((96, tokens), F32),
        ((tokens, 128), F32),
    )


def weight_scratch(model, units):
    return [
        pltpu.VMEM((128, model), BF16),
        pltpu.VMEM((128, 384), BF16),
        pltpu.VMEM((128, 128), BF16),
        pltpu.VMEM((128, units), BF16),
        pltpu.VMEM((128, units), BF16),
    ]


def tensor_barrier(b, t, parts):
    barrier = pltpu.get_barrier_semaphore()
    for k in range(1, parts):
        pl.semaphore_signal(barrier, inc=1, device_id=(b, t ^ k), device_id_type=MESH)
    return barrier


def vmem_specs(count):
    return [pl.BlockSpec(memory_space=pltpu.VMEM)] * count


OUTS = ("down", "gate", "gains", "project", "mixing", "expand", "reduce")
SUMS = (
    *("out", "one", "mid", "mid_out", "two", "far"),
    *("one_send", "one_recv", "two_send", "two_recv", "far_send", "far_recv"),
    *("three_send", "three_recv", "four_send", "four_recv"),
)
LOCAL = (
    *("k_s", "vt_s", "scores", "kv_send", "kv_recv", "do_s", "dot_s", "q_s", "qt_s", "v_s", "kt_s"),
    *("terms", "terms_in", "dqkv", "terms_send", "terms_recv"),
)


def side_rest_kernel(parts, batch, *refs):
    refs = list(refs)

    def pop(count):
        taken, refs[:count] = refs[:count], []
        return taken

    first_f, second_f, side_in, cotangent, ids_ref = pop(5)
    raw = Refs(**dict(zip(RAW, pop(7))))
    state_one, kvt_zero = pop(2)
    keep_zero = Refs(**dict(zip(KEEP, pop(6))))
    side_out, grad, full = pop(3)
    kvt_one, prev, pack, raw.vectors = pop(4)
    keep_one = Refs(**dict(zip(KEEP, pop(6))))
    w = Refs(**dict(zip(WEIGHTS, pop(5))))
    c = Refs(**dict(zip(LOCAL, pop(len(LOCAL)))))
    s = Refs(**dict(zip(SUMS, pop(len(SUMS)))))
    s.full = full
    c.kvt = kvt_one
    b = lax.axis_index("batch")
    t = lax.axis_index("tensor")
    barrier = tensor_barrier(b, t, parts)
    for k in range(1, RING):
        pl.semaphore_signal(barrier, inc=1, device_id=(b ^ k, t), device_id_type=MESH)
    outer = batch // RING
    for k in range(1, outer):
        other = lax.rem(b // RING + k, outer) * RING + lax.rem(b, RING)
        pl.semaphore_signal(barrier, inc=1, device_id=(other, t), device_id_type=MESH)
    load_vectors(raw.vectors, raw)
    load_side_weights(1, w, raw)
    pl.semaphore_wait(barrier, parts - 1 + RING - 1 + outer - 1)
    side_forward(
        1, b, t, parts, second_f, state_one, w, raw, c, keep_one, ids_ref, side_out,
        lambda: None, lambda index: None,
    )
    grad[...] = widened(cotangent)
    side_backward(
        1, b, t, parts, second_f, state_one, w, raw, c, keep_one, kvt_one, ids_ref, grad, pack.at[1],
        lambda index: None, False,
    )
    upper = Sum(1, b, t, parts, batch, pack.at[1], s)
    upper.step_one()
    load_side_weights(0, w, raw)
    prev[...] = widened(side_in)

    def between(index):
        pl.when(index == 1)(upper.step_two)
        pl.when(index == 3)(upper.step_three)
        pl.when(index == 4)(upper.step_four)

    side_backward(
        0, b, t, parts, first_f, prev, w, raw, c, keep_zero, kvt_zero, ids_ref, grad, pack.at[0], between, True
    )
    lower = Sum(0, b, t, parts, batch, pack.at[0], s)
    lower.step_one()
    upper.step_five()
    lower.step_two()
    lower.step_three()
    lower.step_four()
    lower.step_five()


def side_rest_call(first_f, second_f, side_in, cotangent, ids_all, raw, state_one, kvt_zero, keep_zero, parts, batch):
    tokens, model = first_f.shape
    length = parts * tokens
    units = raw[5].shape[2]
    dma = pltpu.SemaphoreType.DMA
    vmem = pltpu.VMEM
    pairs = SIDE_HEADS // 2
    group = COLUMNS // parts
    piece = group * 96 // RING
    outs = (
        ((tokens, 128), F32),
        ((tokens, 128), F32),
        ((LAYERS, parts, RING, piece, 128), BF16),
    )
    outer = max(batch // RING, 1)
    return pl.pallas_call(
        functools.partial(side_rest_kernel, parts, batch),
        out_shape=tuple(jax.ShapeDtypeStruct(*o) for o in outs),
        in_specs=vmem_specs(20),
        out_specs=tuple(vmem_specs(len(outs))),
        scratch_shapes=[
            vmem((parts, 192, tokens), BF16),
            vmem((tokens, 128), F32),
            vmem((LAYERS, COLUMNS, 96, 128), F32),
            vmem((LAYERS, 8, 128), F32),
            *[vmem(*shape) for shape in keep_shapes(tokens)],
            *weight_scratch(model, units),
            vmem((length, 256), BF16),
            vmem((SIDE_HEADS, 16, length), BF16),
            vmem((2, length, tokens), F32),
            dma((3,)),
            dma((parts,)),
            vmem((tokens, 128), BF16),
            vmem((SIDE_HEADS, 16, tokens), BF16),
            vmem((tokens, 256), BF16),
            vmem((SIDE_HEADS, 16, tokens), BF16),
            vmem((length, 128), BF16),
            vmem((SIDE_HEADS, 16, length), BF16),
            vmem((pairs, parts, 32, tokens), BF16),
            vmem((LAYERS, pairs, parts, 32, tokens), BF16),
            vmem((384, tokens), BF16),
            dma((LAYERS, pairs, parts - 1)),
            dma((LAYERS, pairs, parts)),
            vmem((LAYERS, COLUMNS, 96, 128), BF16),
            vmem((LAYERS, parts, group, 96, 128), BF16),
            vmem((LAYERS, RING, piece, 128), F32),
            vmem((LAYERS, RING, piece, 128), BF16),
            vmem((LAYERS, RING, piece, 128), BF16),
            vmem((LAYERS, outer, piece, 128), BF16),
            dma((LAYERS, parts - 1)),
            dma((LAYERS, parts)),
            dma((LAYERS, RING - 1)),
            dma((LAYERS, RING)),
            dma((LAYERS, max(outer - 1, 1))),
            dma((LAYERS, outer)),
            dma((LAYERS, RING - 1)),
            dma((LAYERS, RING)),
            dma((LAYERS, parts - 1)),
            dma((LAYERS, parts)),
        ],
        compiler_params=pltpu.CompilerParams(
            collective_id=5, has_side_effects=True, vmem_limit_bytes=60 << 20
        ),
    )(first_f, second_f, side_in, cotangent, ids_all, *raw, state_one, kvt_zero, *keep_zero)


def finish_call(frozen, state, grad, full, side, parts):
    tokens, model = frozen.shape
    units = 4 * side
    outs = (
        ((tokens, model), BF16),
        ((side, tokens), F32),
        ((side, tokens), F32),
        ((LAYERS, side, model), F32),
        ((LAYERS, side), F32),
        ((LAYERS, 2, side), F32),
        ((LAYERS, side, 3 * side), F32),
        ((LAYERS, side, side), F32),
        ((LAYERS, side, units), F32),
        ((LAYERS, side, units), F32),
    )
    frozen, state, grad, down, *others, reduce_grad = pl.pallas_call(
        functools.partial(finish_kernel, parts),
        out_shape=tuple(jax.ShapeDtypeStruct(*o) for o in outs),
        in_specs=vmem_specs(4),
        out_specs=tuple(vmem_specs(len(outs))),
        compiler_params=pltpu.CompilerParams(vmem_limit_bytes=62 << 20),
    )(frozen, state, grad, full)
    turn = (0, 2, 1)
    return (frozen, state.T, grad.T, down.transpose(turn), *others, reduce_grad.transpose(turn))


def per_device(
    hidden_rows,
    side_input,
    segment_ids,
    side_cotangent,
    backbone_gains,
    backbone_project,
    backbone_mixing,
    backbone_expand,
    backbone_reduce,
    side_down,
    side_gate,
    side_gains,
    side_project,
    side_mixing,
    side_expand,
    side_reduce,
):
    parts = lax.axis_size("tensor")
    batch = lax.axis_size("batch")
    side = side_input.shape[1]
    turn = (0, 2, 1)
    qkv = backbone_project.transpose(0, 2, 3, 1)
    raw = (
        side_gate,
        side_gains,
        side_down.transpose(turn),
        side_project,
        side_mixing,
        side_expand,
        side_reduce.transpose(turn),
    )
    side_turned, cotangent_turned = side_input.T, side_cotangent.T
    ids_row = segment_ids.reshape(1, -1)

    first_f, second_f, ids_all, state_one, kvt_zero, *keep_zero = front_call(
        hidden_rows,
        ids_row,
        backbone_gains,
        qkv,
        backbone_mixing,
        backbone_expand,
        backbone_reduce,
        side_turned,
        raw,
        parts,
    )
    state, grad, full = side_rest_call(
        first_f, second_f, side_turned, cotangent_turned, ids_all, raw, state_one, kvt_zero, keep_zero, parts, batch
    )
    return finish_call(second_f, state, grad, full, side, parts)


def solution(mesh):
    return jax.shard_map(
        per_device,
        mesh=mesh,
        in_specs=(
            P(("batch", "tensor"), None),
            P(("batch", "tensor"), None),
            P(("batch", "tensor")),
            P(("batch", "tensor"), None),
            P(),
            P(None, None, None, "tensor"),
            P(None, "tensor", None),
            P(None, None, "tensor"),
            P(None, "tensor", None),
            P(),
            P(),
            P(),
            P(),
            P(),
            P(),
            P(),
        ),
        out_specs=(
            P(("batch", "tensor"), None),
            P(("batch", "tensor"), None),
            P(("batch", "tensor"), None),
            P(),
            P(),
            P(),
            P(),
            P(),
            P(),
            P(),
        ),
        check_vma=False,
    )
```

```python
import functools
import jax
import jax.numpy as jnp
from jax import lax
from jax.experimental import pallas as pl
from jax.experimental.pallas import tpu as pltpu
from jax.sharding import PartitionSpec as P

HEAD_DIM = 64
SIDE_HEADS = 12
SIDE_HEAD_DIM = 8
LAYERS = 2
EPS = 1e-06
BIG = 2.0**100
LOG2E = 1.4426950408889634
ID_BITS = 11
QUAD = 4
MESH = pl.DeviceIdType.MESH
F32 = jnp.float32
BF16 = jnp.bfloat16


def contract(left, right, dims):
    return lax.dot_general(left, right, ((dims[:1], dims[1:]), ((), ())), preferred_element_type=F32)


def nn(left, right):
    return contract(left, right, (1, 0))


def nt(left, right):
    return contract(left, right, (1, 1))


def tn(left, right):
    return contract(left, right, (0, 0))


def lanes_of(rows, lanes):
    return lax.broadcasted_iota(jnp.int32, (rows, lanes), 1)


def segment_lanes(id_row, offset):
    width = id_row.shape[1]
    place = lax.broadcasted_iota(jnp.int32, (128, width), 0) - offset
    flipped = place >= ID_BITS
    shift = jnp.clip(jnp.where(flipped, place - ID_BITS, place), 0, ID_BITS)
    bit = lax.shift_right_logical(jnp.broadcast_to(id_row, (128, width)), shift) & 1
    bit = jnp.where(flipped, 1 - bit, bit)
    used = (place >= 0) & (place < 2 * ID_BITS)
    keys = jnp.where(used, bit, 0).astype(F32)
    queries = jnp.where(used, (bit - 1).astype(F32) * BIG, 0.0)
    return keys.T, queries.T


def root_norm(values, gain):
    return values * lax.rsqrt(jnp.mean(values * values, axis=-1, keepdims=True) + EPS) * gain


class Refs:
    def __init__(self, **refs):
        self.__dict__.update(refs)


def remote(src, dst, send, recv, target):
    return pltpu.make_async_remote_copy(
        src_ref=src, dst_ref=dst, send_sem=send, recv_sem=recv, device_id=target, device_id_type=MESH
    )


class Weights:
    def __init__(self, layer, b, t, c):
        self.layer, self.b, self.t, self.c = layer, b, t, c
        self.part = lax.rem(b, QUAD)
        self.fulls = (c.mix_w, c.exp_w, c.red_w)
        self.sources = (c.mix_hbm, c.exp_hbm, c.red_hbm)
        self.slices = tuple(w.shape[2] // QUAD for w in self.fulls)
        mix, up, down = self.slices
        self.pieces = (
            (0, 0, mix),
            (1, 0, up // 2),
            (1, up // 2, up // 2),
            (2, 0, down // 2),
            (2, down // 2, down // 2),
        )

    def rows(self, p, part):
        w, low, size = self.pieces[p]
        return pl.ds(pl.multiple_of(part * self.slices[w] + low, 16), size)

    def view(self, p, slot, part):
        return self.fulls[self.pieces[p][0]].at[self.layer, slot, self.rows(p, part)]

    def load(self, w):
        return pltpu.make_async_copy(
            self.sources[w].at[self.layer],
            self.fulls[w].at[self.layer, self.t],
            self.c.load_sem.at[self.layer, w],
        )

    def own(self, w, slot):
        c = self.c
        return remote(
            self.sources[w].at[self.layer],
            self.fulls[w].at[self.layer, slot],
            c.own_send.at[self.layer, w],
            c.own_recv.at[self.layer, w],
            (self.b, self.t ^ 1),
        )

    def cross(self, p):
        c = self.c
        return remote(
            self.sources[self.pieces[p][0]].at[self.layer, self.rows(p, self.part)],
            self.view(p, self.t, self.part),
            c.cross_send.at[self.layer, p],
            c.w_recv.at[self.layer, p, self.part],
            (self.b, self.t ^ 2),
        )

    def spread(self, p, k):
        c = self.c
        view = self.view(p, self.t ^ 2, self.part)
        return remote(
            view, view, c.spread_send.at[self.layer, p, k - 1], c.w_recv.at[self.layer, p, self.part], (self.b ^ k, self.t)
        )

    def here(self, p, k):
        c = self.c
        view = self.view(p, self.t ^ 2, self.part ^ k)
        return remote(
            view, view, c.cross_send.at[self.layer, p], c.w_recv.at[self.layer, p, self.part ^ k], (self.b, self.t ^ 2)
        )

    def forward(self, p, k, slot):
        c = self.c
        view = self.view(p, slot, self.part ^ k)
        return remote(
            view,
            view,
            c.pass_send.at[self.layer, p, k],
            c.pass_recv.at[self.layer, p, self.part ^ k],
            (self.b, self.t ^ 1),
        )

    def start_cross(self):
        for p in range(5):
            self.cross(p).start()

    def start_spread(self, p):
        self.here(p, 0).wait_recv()
        for k in range(1, QUAD):
            self.spread(p, k).start()

    def start_forward(self, p):
        for k in range(1, QUAD):
            self.here(p, k).wait_recv()
        for k in range(QUAD):
            self.forward(p, k, self.t ^ 2).start()

    def wait_far(self, p):
        for k in range(QUAD):
            self.forward(p, k, self.t ^ 3).wait_recv()

    def wait_sent(self):
        for w in range(3):
            self.own(w, self.t).wait_send()
        for p in range(5):
            self.cross(p).wait_send()
            for k in range(1, QUAD):
                self.spread(p, k).wait_send()
            for k in range(QUAD):
                self.forward(p, k, self.t ^ 2).wait_send()


class Backbone:
    def __init__(self, layer, b, t, parts, c):
        self.layer, self.b, self.t, self.parts, self.c = layer, b, t, parts, c
        self.sib, self.across, self.far = t ^ 1, t ^ 2, t ^ 3
        self.tokens = c.rows_all.shape[1]
        self.half = self.tokens // 2
        self.width = c.mix_w.shape[2]
        self.heads = self.width // HEAD_DIM
        self.weights = Weights(layer, b, t, c)

    def row_copy(self, slot, chunk, send, target):
        c = self.c
        view = c.rows_all.at[slot, pl.ds(chunk * self.half, self.half)]
        return remote(
            view,
            view,
            c.row_send.at[self.layer, send, chunk],
            c.row_recv.at[self.layer, slot, chunk],
            (self.b, target),
        )

    def norm_rows(self, stream):
        c = self.c
        gain = c.gains[self.layer, 0:1, :].astype(F32)
        c.rows_all[self.t] = root_norm(stream, gain).astype(BF16)

    def send_rows(self):
        for chunk in range(2):
            self.row_copy(self.t, chunk, 1, self.across).start()
        for chunk in range(2):
            self.row_copy(self.t, chunk, 0, self.sib).start()

    def project(self, slot, chunk):
        c, width, half = self.c, self.width, self.half
        inside = pl.ds(pl.multiple_of(chunk * half, half), half)
        rows = c.rows_all[slot, inside, :]
        at = pl.ds(pl.multiple_of(slot * self.tokens + chunk * half, half), half)
        key_bits, query_bits = segment_lanes(c.ids_all[slot, 0:1, inside], width - 128)
        query = nt(rows, c.qkv_w[self.layer, 0]) * (HEAD_DIM**-0.5 * LOG2E)
        keys = nt(rows, c.qkv_w[self.layer, 1])
        c.q_s[at, 0:128] = query[:, 0:128].astype(BF16)
        c.q_s[at, 128:256] = (query[:, 128:256] + query_bits).astype(BF16)
        c.k_s[at, 0:128] = keys[:, 0:128].astype(BF16)
        c.k_s[at, 128:256] = (keys[:, 128:256] + key_bits).astype(BF16)
        values = nt(c.qkv_w[self.layer, 2, 0:width], rows)
        for h in range(self.heads):
            c.vt_s[h, 0:HEAD_DIM, at] = values[h * HEAD_DIM : (h + 1) * HEAD_DIM].astype(BF16)
            c.vt_s[h, HEAD_DIM:, at] = jnp.ones((16, half), BF16)

    def project_all(self, first, last, hook):
        def step(index, carry):
            for chunk in range(2):

                @pl.when(index == 2 + chunk)
                def _():
                    self.row_copy(self.sib, chunk, 0, self.sib).wait_recv()

                @pl.when(index == 4 + 2 * chunk)
                def _():
                    self.row_copy(self.across, chunk, 0, self.sib).wait_recv()
                    self.row_copy(self.across, chunk, 2, self.sib).start()

                @pl.when(index == 5 + 2 * chunk)
                def _():
                    self.row_copy(self.far, chunk, 0, self.sib).wait_recv()

            hook(index)
            early = index < 4
            k = jnp.where(early, index // 2, 2 + index % 2)
            chunk = jnp.where(early, index % 2, index // 2 - 2)
            self.project(self.t ^ k, chunk)
            return carry

        lax.fori_loop(first, last, step, 0)

    def wait_rows(self):
        for chunk in range(2):
            self.row_copy(self.t, chunk, 0, self.sib).wait_send()
            self.row_copy(self.t, chunk, 1, self.across).wait_send()
            self.row_copy(self.across, chunk, 2, self.sib).wait_send()

    def block_of(self, item):
        return self.t ^ (self.parts - 1 - item // self.heads)

    def make_scores(self, item, place):
        c = self.c
        h = lax.rem(item, self.heads)
        rows = c.q_s[pl.ds(pl.multiple_of(self.block_of(item) * self.tokens, self.tokens), self.tokens), :]
        lane = lanes_of(self.tokens, 256)
        chosen = (lane // HEAD_DIM == h) | (lane >= self.width)
        c.scores[place] = nt(c.k_s[...], jnp.where(chosen, rows, jnp.zeros_like(rows)))

    def send_heads(self, block):
        c = self.c
        return remote(
            c.heads_buf.at[block],
            c.heads_buf.at[self.parts + self.t],
            c.head_send.at[self.layer, block],
            c.head_recv.at[self.layer, self.t],
            (self.b, block),
        )

    def attend(self, item, place):
        c = self.c
        block = self.block_of(item)
        h = lax.rem(item, self.heads)
        values = c.scores[place]
        weights = jnp.exp2(values - jnp.max(values, axis=0, keepdims=True)).astype(BF16)
        out = nn(c.vt_s[h], weights)
        slot = jnp.where(block == self.t, self.parts + self.t, block)
        c.heads_buf[slot, pl.ds(pl.multiple_of(h * HEAD_DIM, HEAD_DIM), HEAD_DIM), :] = (
            out[0:HEAD_DIM] * (1.0 / out[HEAD_DIM : HEAD_DIM + 1])
        ).astype(BF16)

        @pl.when((h == self.heads - 1) & (item < (self.parts - 1) * self.heads))
        def _():
            self.send_heads(block).start()

    def attention(self, hook):
        count = self.parts * self.heads
        self.make_scores(0, 0)

        def pair(index, carry):
            item = 2 * index
            hook(index)
            self.make_scores(item + 1, 1)
            self.attend(item, 0)
            self.make_scores(jnp.minimum(item + 2, count - 1), 0)
            self.attend(item + 1, 1)
            return carry

        lax.fori_loop(0, count // 2, pair, 0)

    def wait_heads(self):
        c = self.c
        for k in range(1, self.parts):
            self.send_heads(self.t ^ k).wait_send()
            remote(
                c.heads_buf.at[0],
                c.heads_buf.at[self.parts + (self.t ^ k)],
                c.head_send.at[self.layer, 0],
                c.head_recv.at[self.layer, self.t ^ k],
                (self.b, self.sib),
            ).wait_recv()

    def feed_forward(self, stream, hook):
        c, parts, layer = self.c, self.parts, self.layer
        attended = c.heads_buf[parts : 2 * parts].reshape(parts * self.width, self.tokens)
        stream = stream + tn(attended, c.mix_w[layer].reshape(parts * self.width, -1))
        c.acc[...] = stream
        c.normed[...] = root_norm(stream, c.gains[layer, 1:2, :].astype(F32)).astype(BF16)

        def feed(index, carry):
            hook(index)
            hidden = jax.nn.gelu(nn(c.normed[...], c.exp_w[layer, self.t ^ index])).astype(BF16)
            c.acc[...] += nn(hidden, c.red_w[layer, self.t ^ index])
            return carry

        lax.fori_loop(0, parts, feed, 0)


FRONT_SCRATCH = (
    *("vectors", "rows_all", "ids_scratch", "qkv_w", "mix_w", "exp_w", "red_w", "q_s", "k_s", "vt_s", "scores"),
    *("heads_buf", "acc", "normed", "load_sem", "qkv_sem", "row_send", "row_recv", "id_send", "id_recv"),
    *("head_send", "head_recv", "cross_send", "spread_send", "pass_send", "own_send", "w_recv", "pass_recv"),
    *("own_recv", "side_k", "side_vt", "kv_send", "kv_recv"),
)


def front_kernel(parts, *refs):
    refs = list(refs)

    def pop(count):
        taken, refs[:count] = refs[:count], []
        return taken

    x_ref, ids_ref, gains, qkv_hbm, mix_hbm, exp_hbm, red_hbm, side_in = pop(8)
    raw = Refs(**dict(zip(RAW, pop(7))))
    first_f, second_f, ids_all, state_one, kvt = pop(5)
    keep = Refs(**dict(zip(KEEP, pop(6))))
    prev = pop(1)[0]
    w = Refs(**dict(zip(WEIGHTS, pop(5))))
    c = Refs(**dict(zip(FRONT_SCRATCH, pop(len(FRONT_SCRATCH)))))
    c.gains, c.mix_hbm, c.exp_hbm, c.red_hbm, c.ids_all = gains, mix_hbm, exp_hbm, red_hbm, ids_all
    b = lax.axis_index("batch")
    t = lax.axis_index("tensor")
    tokens = x_ref.shape[0]
    width = c.mix_w.shape[2]
    lower, upper = Backbone(0, b, t, parts, c), Backbone(1, b, t, parts, c)
    load_qkv = [
        pltpu.make_async_copy(
            qkv_hbm.at[layer, k], c.qkv_w.at[layer, k, pl.ds(0, width)], c.qkv_sem.at[layer, k]
        )
        for layer in range(LAYERS)
        for k in range(3)
    ]
    for copy in load_qkv:
        copy.start()
    for layer in (lower, upper):
        for k in range(3):
            layer.weights.load(k).start()
    barrier = tensor_barrier(b, t, parts)
    for k in range(1, QUAD):
        pl.semaphore_signal(barrier, inc=1, device_id=(b ^ k, t), device_id_type=MESH)
    lower.norm_rows(x_ref[...].astype(F32))
    ids_all[t] = jnp.broadcast_to(ids_ref[...], (8, tokens))
    pl.semaphore_wait(barrier, parts - 1 + QUAD - 1)

    def id_copy(slot, k):
        return remote(ids_all.at[slot], ids_all.at[slot], c.id_send.at[k - 1], c.id_recv.at[slot], (b, t ^ k))

    for k in range(1, parts):
        id_copy(t, k).start()
    lower.weights.cross(1).start()
    lower.send_rows()
    for layer in (lower, upper):
        for k in range(3):
            layer.weights.own(k, t).start()
    c.qkv_w[:, :, width:, :] = jnp.zeros((LAYERS, 3, 256 - width, x_ref.shape[1]), BF16)
    for copy in load_qkv:
        copy.wait()
    load_side_weights(0, w, raw)
    load_vectors(c.vectors, raw)
    raw.vectors = c.vectors
    prev[...] = widened(side_in)
    for k in range(1, parts):
        id_copy(t, k).wait_send()
        id_copy(t ^ k, k).wait_recv()

    def when(index, at, act, *args):
        @pl.when(index == at)
        def _():
            act(*args)

    def lower_project(index):
        when(index, 4, lower.weights.start_spread, 1)
        for p in (0, 2, 3, 4):
            when(index, 6, lambda p: lower.weights.cross(p).start(), p)

    def lower_attention(index):
        for at, p in ((1, 0), (2, 2), (3, 3), (5, 4)):
            when(index, at, lower.weights.start_spread, p)
        for at, p in ((4, 1), (5, 0)):
            when(index, at, lower.weights.start_forward, p)

    def feed_hook(layer):
        def hook(index):
            weights = layer.weights

            @pl.when(index == 0)
            def _():
                for k in (1, 2):
                    weights.load(k).wait()
                if layer is lower:
                    weights.start_forward(2)

            @pl.when(index == 1)
            def _():
                for k in (1, 2):
                    weights.own(k, layer.sib).wait_recv()
                if layer is lower:
                    weights.start_forward(3)

            @pl.when(index == 2)
            def _():
                if layer is lower:
                    weights.start_forward(4)

            @pl.when(index == 3)
            def _():
                for p in range(1, 5):
                    weights.wait_far(p)

        return hook

    lower.project_all(0, 2 * parts, lower_project)
    lower.wait_rows()
    lower.attention(lower_attention)
    upper.weights.start_cross()
    lower.weights.load(0).wait()
    lower.weights.own(0, lower.sib).wait_recv()
    lower.weights.wait_far(0)
    lower.wait_heads()
    lower.feed_forward(x_ref[...].astype(F32), feed_hook(lower))
    first_f[...] = c.acc[...].astype(BF16)

    side = Refs(
        kvt=kvt, k_s=c.side_k, vt_s=c.side_vt, scores=c.scores, kv_send=c.kv_send, kv_recv=c.kv_recv
    )

    def send_upper():
        upper.norm_rows(c.acc[...])
        upper.send_rows()

    def side_hook(index):
        for p in range(5):
            when(index, p, upper.weights.start_spread, p)

    side_forward(
        0, b, t, parts, first_f, prev, w, raw, side, keep, ids_all, state_one,
        send_upper, lambda: upper.project_all(0, parts, lambda index: None), side_hook,
    )

    def upper_attention(index):
        for p in range(5):
            when(index, p + 1, upper.weights.start_forward, p)

    upper.project_all(parts, 2 * parts, lambda index: None)
    upper.wait_rows()
    upper.attention(upper_attention)
    upper.weights.load(0).wait()
    upper.weights.own(0, upper.sib).wait_recv()
    upper.weights.wait_far(0)
    upper.wait_heads()
    upper.feed_forward(c.acc[...], feed_hook(upper))
    second_f[...] = c.acc[...].astype(BF16)
    lower.weights.wait_sent()
    upper.weights.wait_sent()


def front_call(x, ids, gains, qkv, mix, exp, red, side_in, raw, parts):
    tokens, model = x.shape
    width = mix.shape[1]
    units = exp.shape[2]
    heads = width // HEAD_DIM
    length = parts * tokens
    side_units = raw[5].shape[2]
    anywhere = pl.BlockSpec(memory_space=pl.ANY)
    dma = pltpu.SemaphoreType.DMA
    vmem = pltpu.VMEM
    outs = (
        ((tokens, model), BF16),
        ((tokens, model), BF16),
        ((parts, 8, tokens), jnp.int32),
        ((tokens, 128), F32),
        ((parts, 192, tokens), BF16),
        *keep_shapes(tokens),
    )
    return pl.pallas_call(
        functools.partial(front_kernel, parts),
        out_shape=tuple(jax.ShapeDtypeStruct(*o) for o in outs),
        in_specs=vmem_specs(3) + [anywhere] * 4 + vmem_specs(8),
        out_specs=tuple(vmem_specs(len(outs))),
        scratch_shapes=[
            vmem((tokens, 128), F32),
            *weight_scratch(model, side_units),
            vmem((LAYERS, 8, 128), F32),
            vmem((parts, tokens, model), BF16),
            vmem((8, 128), F32),
            vmem((LAYERS, 3, 256, model), BF16),
            vmem((LAYERS, parts, width, model), BF16),
            vmem((LAYERS, parts, model, units), BF16),
            vmem((LAYERS, parts, units, model), BF16),
            vmem((length, 256), BF16),
            vmem((length, 256), BF16),
            vmem((heads, HEAD_DIM + 16, length), BF16),
            vmem((2, length, tokens), F32),
            vmem((2 * parts, width, tokens), BF16),
            vmem((tokens, model), F32),
            vmem((tokens, model), BF16),
            dma((LAYERS, 3)),
            dma((LAYERS, 3)),
            dma((LAYERS, 3, 2)),
            dma((LAYERS, parts, 2)),
            dma((parts - 1,)),
            dma((parts,)),
            dma((LAYERS, parts)),
            dma((LAYERS, parts)),
            dma((LAYERS, 5)),
            dma((LAYERS, 5, QUAD - 1)),
            dma((LAYERS, 5, QUAD)),
            dma((LAYERS, 3)),
            dma((LAYERS, 5, QUAD)),
            dma((LAYERS, 5, QUAD)),
            dma((LAYERS, 3)),
            vmem((length, 128), BF16),
            vmem((SIDE_HEADS, 16, length), BF16),
            dma((3,)),
            dma((parts,)),
        ],
        compiler_params=pltpu.CompilerParams(
            collective_id=1, has_side_effects=True, vmem_limit_bytes=62 << 20
        ),
    )(x, ids, gains, qkv, mix, exp, red, side_in, *raw)


LN2 = 0.6931471805599453
COLUMNS = 16
EARLY = (6, 7, 8, 9, 10, 11, 12, 13)
LATE = (0, 1, 2, 3, 4, 5, 14, 15)


def place_of(column):
    order, low = (EARLY, 0) if column in EARLY else (LATE, 2)
    index = order.index(column)
    return index // 2 * 4 + low + index % 2


RING = 8


def side_norm(values, width):
    rstd = lax.rsqrt(jnp.sum(values * values, axis=-1, keepdims=True) * (1.0 / width) + EPS)
    return values * rstd, rstd


def gelu_parts(inner):
    root = 0.7978845608028654
    square = inner * inner
    curve = jnp.tanh(root * inner * (1.0 + 0.044715 * square))
    half = 0.5 * (1.0 + curve)
    slope = half + 0.5 * inner * (1.0 - curve * curve) * root * (1.0 + 3 * 0.044715 * square)
    return inner * half, slope


def load_side_weights(layer, w, raw):
    side = raw.mixing.shape[1]
    w.down[side:, :] = jnp.zeros_like(w.down[side:, :])
    w.down[0:side, :] = raw.down[layer]
    w.project[...] = jnp.zeros_like(w.project)
    w.project[0:side, 0 : 3 * side] = raw.project[layer]
    w.mixing[...] = jnp.zeros_like(w.mixing)
    w.mixing[0:side, 0:side] = raw.mixing[layer]
    w.expand[side:, :] = jnp.zeros_like(w.expand[side:, :])
    w.expand[0:side, :] = raw.expand[layer]
    w.reduce[side:, :] = jnp.zeros_like(w.reduce[side:, :])
    w.reduce[0:side, :] = raw.reduce[layer]


def load_vectors(vectors, raw):
    side = raw.mixing.shape[1]
    vectors[...] = jnp.zeros_like(vectors)
    for layer in range(LAYERS):
        vectors[layer, 0:1, 0:side] = raw.gate[layer : layer + 1, :]
        vectors[layer, 1:3, 0:side] = raw.gains[layer].astype(F32)


def widened(turned):
    values = turned[...].astype(F32)
    return jnp.concatenate([values, jnp.zeros((32, values.shape[1]), F32)], axis=0).T


def kv_copy(c, slot, send, target):
    return remote(c.kvt.at[slot], c.kvt.at[slot], c.kv_send.at[send], c.kv_recv.at[slot], target)


def keys_from(c, slot, ids_ref):
    tokens = c.kvt.shape[2]
    at = pl.ds(pl.multiple_of(slot * tokens, tokens), tokens)
    key_bits, _ = segment_lanes(ids_ref[slot][0:1, :], 96)
    keys = jnp.concatenate([c.kvt[slot, 0:96].astype(F32), jnp.zeros((32, tokens), F32)], axis=0)
    c.k_s[at, 0:128] = (keys.T + key_bits).astype(BF16)


def side_forward(layer, b, t, parts, f_ref, prev, w, raw, c, keep, ids_ref, result, after_send, meanwhile, between):
    side = raw.mixing.shape[1]
    tokens = f_ref.shape[0]
    gate = jax.nn.sigmoid(raw.vectors[layer, 0:1, :])
    lifted = nt(f_ref[...], w.down[...])
    mixed = gate * lifted + (1.0 - gate) * prev[...]
    keep.lifted[...] = lifted
    keep.mixed[...] = mixed
    normed = (side_norm(mixed, side)[0] * raw.vectors[layer, 1:2, :]).astype(BF16)
    turned = w.project[...].astype(F32).T.astype(BF16)
    c.kvt[t] = nt(turned[side : 3 * side], normed).astype(BF16)
    sib, across, far = t ^ 1, t ^ 2, t ^ 3
    kv_copy(c, t, 1, (b, across)).start()
    kv_copy(c, t, 0, (b, sib)).start()
    after_send()
    lane = lanes_of(tokens, 128)
    weight_q = jnp.where(lanes_of(128, 128) < side, w.project[:, 0:128], jnp.zeros((128, 128), BF16))
    query_bits = segment_lanes(ids_ref[t][0:1, :], 96)[1]
    keep.query[...] = (
        nn(normed, weight_q) * (SIDE_HEAD_DIM**-0.5 * LOG2E) + query_bits
    ).astype(BF16)
    keep.sums[...] = jnp.zeros_like(keep.sums)

    def take(index, carry):
        @pl.when(index == 1)
        def _():
            kv_copy(c, sib, 0, (b, sib)).wait_recv()

        @pl.when(index == 2)
        def _():
            meanwhile()
            kv_copy(c, across, 0, (b, sib)).wait_recv()
            kv_copy(c, across, 2, (b, sib)).start()

        @pl.when(index == 3)
        def _():
            kv_copy(c, far, 0, (b, sib)).wait_recv()

        slot = t ^ index
        at = pl.ds(pl.multiple_of(slot * tokens, tokens), tokens)
        keys_from(c, slot, ids_ref)
        values = c.kvt[slot, 96:192].astype(F32)
        for h in range(SIDE_HEADS):
            c.vt_s[h, :, at] = jnp.concatenate(
                [values[8 * h : 8 * h + 8], jnp.ones((8, tokens), F32)], axis=0
            ).astype(BF16)
        return carry

    lax.fori_loop(0, parts, take, 0)

    def make_scores(h, place):
        rows = keep.query[...]
        chosen = (lane // SIDE_HEAD_DIM == h) | (lane >= side)
        c.scores[place] = nt(c.k_s[:, 0:128], jnp.where(chosen, rows, jnp.zeros_like(rows)))

    def attend(h, place):
        values = c.scores[place]
        top = jnp.max(values, axis=0, keepdims=True)
        out = nn(c.vt_s[h], jnp.exp2(values - top).astype(BF16))
        total = out[8:9]
        keep.heads[pl.ds(pl.multiple_of(h * 8, 8), 8), :] = out[0:8] * (1.0 / total)
        here = lax.broadcasted_iota(jnp.int32, keep.sums.shape, 0) == h
        keep.sums[...] = jnp.where(here, top + jnp.log2(total), keep.sums[...])

    make_scores(0, 0)

    def pair(index, carry):
        h = 2 * index
        between(index)
        make_scores(h + 1, 1)
        attend(h, 0)
        make_scores(jnp.minimum(h + 2, SIDE_HEADS - 1), 0)
        attend(h + 1, 1)
        return carry

    lax.fori_loop(0, SIDE_HEADS // 2, pair, 0)
    kv_copy(c, t, 1, (b, across)).wait_send()
    kv_copy(c, t, 0, (b, sib)).wait_send()
    kv_copy(c, across, 2, (b, sib)).wait_send()
    middle = mixed + tn(keep.heads[...].astype(BF16), w.mixing[0:side, :])
    keep.middle[...] = middle
    normed_two = (side_norm(middle, side)[0] * raw.vectors[layer, 2:3, :]).astype(BF16)
    active = jax.nn.gelu(nn(normed_two, w.expand[...])).astype(BF16)
    result[...] = middle + nt(active, w.reduce[...])


def norm_back(values, gain, grad, side):
    hat, rstd = side_norm(values, side)
    gain_grad = jnp.sum(grad * hat, axis=0, keepdims=True)
    pulled = grad * gain
    mean = jnp.sum(pulled * hat, axis=-1, keepdims=True) * (1.0 / side)
    return rstd * (pulled - hat * mean), gain_grad


def pad_heads(target, rows, fill):
    for h in range(SIDE_HEADS):
        target[h] = jnp.concatenate(
            [rows[8 * h : 8 * h + 8], jnp.full((8, rows.shape[1]), fill, F32)], axis=0
        ).astype(BF16)


def side_prepare(layer, parts, w, raw, c, keep, kvt, ids_ref, again):
    side = raw.mixing.shape[1]
    tokens = c.q_s.shape[1]
    lane = lanes_of(tokens, 128)
    normed_two = side_norm(keep.middle[...], side)[0] * raw.vectors[layer, 2:3, :]
    active, slope = gelu_parts(nn(normed_two.astype(BF16), w.expand[...]))
    c.active[layer] = active.astype(BF16)
    c.slope[layer] = slope
    sums = keep.sums[...]
    rows = jnp.concatenate([sums, sums, sums, jnp.zeros((80, tokens), F32)], axis=0).T
    high = rows.astype(BF16).astype(F32)
    mid = (rows - high).astype(BF16).astype(F32)
    low = rows - high - mid
    rows = jnp.where(lane < 16, high, jnp.where(lane < 32, mid, low))
    query = keep.query[...]
    c.q_s[layer, :, 0:128] = query
    c.q_s[layer, :, 128:256] = jnp.where(lane < 48, -rows, 0.0).astype(BF16)
    pad_heads(c.qt_s.at[layer], query.astype(F32).T, 0.0)

    def take(slot, carry):
        at = pl.ds(pl.multiple_of(slot * tokens, tokens), tokens)
        if again:
            keys_from(Refs(kvt=kvt, k_s=c.k_s.at[layer]), slot, ids_ref)
        c.k_s[layer, at, 128:256] = jnp.where(lane < 48, 1.0, 0.0).astype(BF16)
        values = jnp.concatenate([kvt[slot, 96:192].astype(F32), jnp.ones((32, tokens), F32)], axis=0)
        c.v_s[layer, at, :] = values.T.astype(BF16)
        keys = kvt[slot, 0:96].astype(F32)
        for h in range(SIDE_HEADS):
            c.kt_s[layer, h, :, at] = jnp.concatenate(
                [keys[8 * h : 8 * h + 8], jnp.zeros((8, tokens), F32)], axis=0
            ).astype(BF16)
        return carry

    lax.fori_loop(0, parts, take, 0)


def side_backward(layer, b, t, parts, f_ref, prev, w, raw, c, keep, grad_ref, pack, between, early):
    side = raw.mixing.shape[1]
    tokens = f_ref.shape[0]
    gate = jax.nn.sigmoid(raw.vectors[layer, 0:1, :])
    lane = lanes_of(tokens, 128)
    grad = grad_ref[...]
    middle = keep.middle[...]
    gain_two = raw.vectors[layer, 2:3, :]
    normed_two = (side_norm(middle, side)[0] * gain_two).astype(BF16)
    top = grad.astype(BF16)
    reduce_grad = tn(top, c.active[layer])
    grad_inner = (c.slope[layer] * nn(top, w.reduce[...])).astype(BF16)
    expand_grad = tn(normed_two, grad_inner)
    for k in range(3):
        pack[place_of(6 + k)] = expand_grad[0:96, 128 * k : 128 * k + 128]
        pack[place_of(9 + k)] = reduce_grad[0:96, 128 * k : 128 * k + 128]
    through, gain_two_grad = norm_back(middle, gain_two, nt(grad_inner, w.expand[...]), side)
    grad_middle = grad + through
    branch = grad_middle.astype(BF16)
    heads = keep.heads[...]
    mixing_grad = nn(heads.astype(BF16), branch)
    grad_heads = nt(branch, w.mixing[...]).astype(BF16).astype(F32).T
    product = grad_heads[0:96] * heads
    group = lax.broadcasted_iota(jnp.int32, (16, 96), 1) // SIDE_HEAD_DIM
    group = (group == lax.broadcasted_iota(jnp.int32, (16, 96), 0)).astype(BF16)
    high = product.astype(BF16)
    inner = nn(group, high) + nn(group, (product - high.astype(F32)).astype(BF16))
    rows = jnp.concatenate([grad_heads[0:96], -inner, -inner], axis=0).T
    high = rows.astype(BF16)
    c.do_s[...] = jnp.where(lane < 112, high, (rows - high.astype(F32)).astype(BF16))
    pad_heads(c.dot_s, grad_heads, 0.0)
    wide = lanes_of(tokens, 256)
    query_head = jnp.where(wide < 96, wide // SIDE_HEAD_DIM, jnp.where(wide < 128, -1, (wide - 128) % 16))
    out_head = jnp.where(lane < 96, lane // SIDE_HEAD_DIM, (lane - 96) % 16)

    count = parts * tokens // 2

    def one_head(h, keys):
        rows = c.q_s[layer]
        rows = jnp.where((query_head == h) | (query_head < 0), rows, jnp.zeros_like(rows))
        probs = jnp.exp2(nt(rows, c.k_s[layer, keys, :]))
        rows = c.do_s[...]
        rows = jnp.where(out_head == h, rows, jnp.zeros_like(rows))
        scores = (probs * nt(rows, c.v_s[layer, keys, :])).astype(BF16)
        by_keys = nn(c.qt_s[layer, h], scores)[0:8] * LN2
        by_values = nn(c.dot_s[h], probs.astype(BF16))[0:8]
        return by_keys, by_values, nt(c.kt_s[layer, h, :, keys], scores)[0:8] * SIDE_HEAD_DIM**-0.5

    def terms_copy(pair, k):
        return remote(
            c.terms.at[pair, t ^ k],
            c.terms_in.at[layer, pair, t],
            c.terms_send.at[layer, pair, k - 1],
            c.terms_recv.at[layer, pair, t],
            (b, t ^ k),
        )

    def terms_wait(pair, k):
        return remote(
            c.terms.at[pair, t ^ k],
            c.terms_in.at[layer, pair, t ^ k],
            c.terms_send.at[layer, pair, k - 1],
            c.terms_recv.at[layer, pair, t ^ k],
            (b, t ^ k),
        )

    def pair_of(index, carry):
        between(index)
        queries = jnp.zeros((16, tokens), F32)
        for near in range(2):
            chip = t // 2 if near else (t // 2) ^ 1
            keys = pl.ds(pl.multiple_of(chip * count, count), count)
            first, second = one_head(2 * index, keys), one_head(2 * index + 1, keys)
            by_keys, by_values, by_queries = (
                jnp.concatenate([left, right], axis=0) for left, right in zip(first, second)
            )
            queries += by_queries
            for place in range(parts // 2):
                at = slice(place * tokens, (place + 1) * tokens)
                c.terms[index, chip * (parts // 2) + place, 0:16] = by_keys[:, at].astype(BF16)
                c.terms[index, chip * (parts // 2) + place, 16:32] = by_values[:, at].astype(BF16)
            for k in (1,) if near else (2, 3):
                terms_copy(index, k).start()
        c.dqkv[pl.ds(pl.multiple_of(index * 16, 16), 16), :] = queries.astype(BF16)
        return carry

    pairs = SIDE_HEADS // 2
    lax.fori_loop(0, pairs, pair_of, 0)
    mixed = keep.mixed[...]
    gain_one = raw.vectors[layer, 1:2, :]
    normed = side_norm(mixed, side)[0] * gain_one
    c.dqkv[288:384, :] = jnp.zeros((96, tokens), BF16)

    def gather(index, carry):
        total = c.terms[index, t].astype(F32)
        for k in range(1, parts):
            terms_wait(index, k).wait_recv()
            total += c.terms_in[layer, index, t ^ k].astype(F32)
        total = total.astype(BF16)
        c.dqkv[pl.ds(pl.multiple_of(96 + index * 16, 16), 16), :] = total[0:16]
        c.dqkv[pl.ds(pl.multiple_of(192 + index * 16, 16), 16), :] = total[16:32]
        return carry

    lax.fori_loop(0, pairs, gather, 0)
    dqkv = c.dqkv[...]
    project_grad = nt(normed.T.astype(BF16), dqkv)
    pack[place_of(12)] = project_grad[0:96, 0:128]
    pack[place_of(13)] = project_grad[0:96, 128:256]
    pack[place_of(14)] = project_grad[0:96, 256:384] + pltpu.roll(mixing_grad, 32, 1)
    early()
    grad_normed = nn(w.project[...], dqkv).T
    through, gain_one_grad = norm_back(mixed, gain_one, grad_normed, side)
    grad_mixed = grad_middle + through
    down_grad = nn((gate * grad_mixed).T.astype(BF16), f_ref[...])
    for k in range(6):
        pack[place_of(k)] = down_grad[0:96, 128 * k : 128 * k + 128]
    gate_grad = jnp.sum(grad_mixed * (keep.lifted[...] - prev[...]), axis=0, keepdims=True)
    gate_grad = gate_grad * gate * (1.0 - gate)
    row = lax.broadcasted_iota(jnp.int32, (96, 128), 0)
    pack[place_of(15)] = jnp.where(
        row == 0, gate_grad, jnp.where(row == 1, gain_one_grad, jnp.where(row == 2, gain_two_grad, 0.0))
    )
    grad_ref[...] = (1.0 - gate) * grad_mixed

    def sent(index, carry):
        for k in range(1, parts):
            terms_copy(index, k).wait_send()
        return carry

    lax.fori_loop(0, pairs, sent, 0)


class Sum:
    def __init__(self, r, b, t, parts, batch, pack, s):
        self.r, self.b, self.t, self.parts, self.batch, self.pack, self.s = r, b, t, parts, batch, pack, s
        self.place = lax.rem(b, RING)
        self.outer = batch // RING

    def across_tensor(self, half, k):
        r, s, t = self.r, self.s, self.t
        group = COLUMNS // self.parts
        return remote(
            s.out.at[r, pl.ds((t ^ k) * group + half * (group // 2), group // 2)],
            s.one.at[r, t, pl.ds(half * (group // 2), group // 2)],
            s.one_send.at[r, half, k - 1],
            s.one_recv.at[r, half, t],
            (self.b, t ^ k),
        )

    def from_tensor(self, half, k):
        r, s, t = self.r, self.s, self.t
        group = COLUMNS // self.parts
        view = s.one.at[r, t ^ k, pl.ds(half * (group // 2), group // 2)]
        return remote(view, view, s.one_send.at[r, half, k - 1], s.one_recv.at[r, half, t ^ k], (self.b, t ^ k))

    def across_batch(self, k):
        r, s = self.r, self.s
        return remote(
            s.mid_out.at[r, self.place ^ k], s.two.at[r, self.place], s.two_send.at[r, k - 1],
            s.two_recv.at[r, self.place], (self.b ^ k, self.t),
        )

    def from_batch(self, k):
        r, s = self.r, self.s
        return remote(
            s.two.at[r, self.place ^ k], s.two.at[r, self.place ^ k], s.two_send.at[r, k - 1],
            s.two_recv.at[r, self.place ^ k], (self.b ^ k, self.t),
        )

    def across_outer(self, k):
        r, s = self.r, self.s
        mine = self.b // RING
        target = lax.rem(mine + k, self.outer) * RING + self.place
        return remote(
            s.far.at[r, mine], s.far.at[r, mine], s.far_send.at[r, k - 1], s.far_recv.at[r, mine], (target, self.t)
        )

    def from_outer(self, k):
        r, s = self.r, self.s
        other = lax.rem(self.b // RING + k, self.outer)
        return remote(
            s.far.at[r, other], s.far.at[r, other], s.far_send.at[r, k - 1], s.far_recv.at[r, other],
            (self.b ^ 1, self.t),
        )

    def back_batch(self, k, place):
        r, s = self.r, self.s
        return remote(
            s.full.at[r, self.t, place], s.full.at[r, self.t, place], s.three_send.at[r, k - 1],
            s.three_recv.at[r, place], (self.b ^ k, self.t),
        )

    def back_tensor(self, k, slot, place):
        r, s = self.r, self.s
        view = s.full.at[r, slot, place]
        return remote(view, view, s.four_send.at[r, k - 1, place], s.four_recv.at[r, slot, place], (self.b, self.t ^ k))

    def pass_piece(self, place):
        for k in (2, 3, 1):
            self.back_tensor(k, self.t, place).start()

    def step_one(self, half):
        group = COLUMNS // self.parts
        for slot in range(self.parts):
            at = slot * group + half * (group // 2)
            self.s.out[self.r, at : at + group // 2] = self.pack[at : at + group // 2].astype(BF16)
        for k in (2, 3, 1):
            self.across_tensor(half, k).start()

    def step_two(self):
        r, s = self.r, self.s
        group = COLUMNS // self.parts
        total = self.pack[pl.ds(self.t * group, group)]
        for k in range(1, self.parts):
            for half in range(2):
                self.from_tensor(half, k).wait_recv()
            total += s.one[r, self.t ^ k].astype(F32)
        total = total.reshape(RING, total.shape[0] * total.shape[1] // RING, 128)
        s.mid[r] = total
        s.mid_out[r] = total.astype(BF16)
        for k in range(1, RING):
            self.across_batch(k).start()

    def step_three(self):
        r, s = self.r, self.s
        total = s.mid[r, self.place]
        for k in range(1, RING):
            self.from_batch(k).wait_recv()
            total += s.two[r, self.place ^ k].astype(F32)
        if self.outer > 1:
            s.far[r, self.b // RING] = total.astype(BF16)
            for k in range(1, self.outer):
                self.across_outer(k).start()
            for k in range(1, self.outer):
                self.from_outer(k).wait_recv()
            total = s.far[r, 0].astype(F32)
            for other in range(1, self.outer):
                total += s.far[r, other].astype(F32)
            for k in range(1, self.outer):
                self.across_outer(k).wait_send()
        s.full[r, self.t, self.place] = total.astype(BF16)
        for k in range(1, RING):
            self.back_batch(k, self.place).start()
        self.pass_piece(self.place)

    def step_four(self):
        for k in range(1, RING):
            self.back_batch(k, self.place ^ k).wait_recv()
            self.pass_piece(self.place ^ k)

    def step_five(self):
        for k in range(1, self.parts):
            for place in range(RING):
                self.back_tensor(k, self.t ^ k, place).wait_recv()
        for k in range(1, self.parts):
            for half in range(2):
                self.across_tensor(half, k).wait_send()
            for place in range(RING):
                self.back_tensor(k, self.t, place).wait_send()
        for k in range(1, RING):
            self.across_batch(k).wait_send()
            self.back_batch(k, self.place).wait_send()


def finish_kernel(parts, frozen, state, grad, full, *refs):
    outs = Refs(**dict(zip(("frozen", "state", "grad", *OUTS), refs)))
    outs.frozen[...] = frozen[...]
    outs.state[...] = state[...].T[0:96]
    outs.grad[...] = grad[...].T[0:96]
    per = COLUMNS // parts
    for layer in range(LAYERS):

        def column(index):
            at = place_of(index)
            both = full[layer, at // per, 2 * (at % per) : 2 * (at % per) + 2]
            return both.astype(F32).reshape(96, 128)

        for k in range(6):
            outs.down[layer, :, 128 * k : 128 * k + 128] = column(k)
        for k in range(3):
            outs.expand[layer, :, 128 * k : 128 * k + 128] = column(6 + k)
            outs.reduce[layer, :, 128 * k : 128 * k + 128] = column(9 + k)
        outs.project[layer, :, 0:128] = column(12)
        outs.project[layer, :, 128:256] = column(13)
        last = column(14)
        outs.project[layer, :, 256:288] = last[:, 0:32]
        outs.mixing[layer] = pltpu.roll(last, 96, 1)[:, 0:96]
        small = column(15)
        outs.gate[layer : layer + 1, :] = small[0:1, 0:96]
        outs.gains[layer] = small[1:3, 0:96]


RAW = ("gate", "gains", "down", "project", "mixing", "expand", "reduce")
WEIGHTS = RAW[2:]
KEEP = ("lifted", "mixed", "query", "sums", "heads", "middle")


def keep_shapes(tokens):
    return (
        ((tokens, 128), F32),
        ((tokens, 128), F32),
        ((tokens, 128), BF16),
        ((16, tokens), F32),
        ((96, tokens), F32),
        ((tokens, 128), F32),
    )


def weight_scratch(model, units):
    return [
        pltpu.VMEM((128, model), BF16),
        pltpu.VMEM((128, 384), BF16),
        pltpu.VMEM((128, 128), BF16),
        pltpu.VMEM((128, units), BF16),
        pltpu.VMEM((128, units), BF16),
    ]


def tensor_barrier(b, t, parts):
    barrier = pltpu.get_barrier_semaphore()
    for k in range(1, parts):
        pl.semaphore_signal(barrier, inc=1, device_id=(b, t ^ k), device_id_type=MESH)
    return barrier


def vmem_specs(count):
    return [pl.BlockSpec(memory_space=pltpu.VMEM)] * count


OUTS = ("down", "gate", "gains", "project", "mixing", "expand", "reduce")
SUMS = (
    *("out", "one", "mid", "mid_out", "two", "far"),
    *("one_send", "one_recv", "two_send", "two_recv", "far_send", "far_recv"),
    *("three_send", "three_recv", "four_send", "four_recv"),
)
LOCAL = (
    *("k_s", "vt_s", "scores", "kv_send", "kv_recv", "do_s", "dot_s", "q_s", "qt_s", "v_s", "kt_s"),
    *("active", "slope"),
    *("terms", "terms_in", "dqkv", "terms_send", "terms_recv"),
)


def side_rest_kernel(parts, batch, *refs):
    refs = list(refs)

    def pop(count):
        taken, refs[:count] = refs[:count], []
        return taken

    first_f, second_f, side_in, cotangent, ids_ref = pop(5)
    raw = Refs(**dict(zip(RAW, pop(7))))
    state_one, kvt_zero = pop(2)
    keep_zero = Refs(**dict(zip(KEEP, pop(6))))
    side_out, grad, full = pop(3)
    kvt_one, prev, pack, raw.vectors = pop(4)
    keep_one = Refs(**dict(zip(KEEP, pop(6))))
    w_one = Refs(**dict(zip(WEIGHTS, pop(5))))
    w_zero = Refs(**dict(zip(WEIGHTS, pop(5))))
    c = Refs(**dict(zip(LOCAL, pop(len(LOCAL)))))
    s = Refs(**dict(zip(SUMS, pop(len(SUMS)))))
    s.full = full
    b = lax.axis_index("batch")
    t = lax.axis_index("tensor")
    barrier = tensor_barrier(b, t, parts)
    for k in range(1, RING):
        pl.semaphore_signal(barrier, inc=1, device_id=(b ^ k, t), device_id_type=MESH)
    outer = batch // RING
    for k in range(1, outer):
        other = lax.rem(b // RING + k, outer) * RING + lax.rem(b, RING)
        pl.semaphore_signal(barrier, inc=1, device_id=(other, t), device_id_type=MESH)
    load_vectors(raw.vectors, raw)
    load_side_weights(1, w_one, raw)
    load_side_weights(0, w_zero, raw)
    grad[...] = widened(cotangent)
    prev[...] = widened(side_in)
    pl.semaphore_wait(barrier, parts - 1 + RING - 1 + outer - 1)
    first = Refs(
        kvt=kvt_one, k_s=c.k_s.at[1], vt_s=c.vt_s, scores=c.scores, kv_send=c.kv_send, kv_recv=c.kv_recv
    )
    side_forward(
        1, b, t, parts, second_f, state_one, w_one, raw, first, keep_one, ids_ref, side_out,
        lambda: None, lambda: side_prepare(0, parts, w_zero, raw, c, keep_zero, kvt_zero, ids_ref, True),
        lambda index: None,
    )
    side_prepare(1, parts, w_one, raw, c, keep_one, kvt_one, ids_ref, False)
    upper = Sum(1, b, t, parts, batch, pack.at[1], s)
    lower = Sum(0, b, t, parts, batch, pack.at[0], s)
    side_backward(
        1, b, t, parts, second_f, state_one, w_one, raw, c, keep_one, grad, pack.at[1],
        lambda index: None, lambda: upper.step_one(0),
    )
    upper.step_one(1)

    def between(index):
        pl.when(index == 2)(upper.step_two)
        pl.when(index == 4)(upper.step_three)
        pl.when(index == 5)(upper.step_four)

    side_backward(
        0, b, t, parts, first_f, prev, w_zero, raw, c, keep_zero, grad, pack.at[0],
        between, lambda: lower.step_one(0),
    )
    lower.step_one(1)
    upper.step_five()
    lower.step_two()
    lower.step_three()
    lower.step_four()
    lower.step_five()


def side_rest_call(first_f, second_f, side_in, cotangent, ids_all, raw, state_one, kvt_zero, keep_zero, parts, batch):
    tokens, model = first_f.shape
    length = parts * tokens
    units = raw[5].shape[2]
    dma = pltpu.SemaphoreType.DMA
    vmem = pltpu.VMEM
    pairs = SIDE_HEADS // 2
    group = COLUMNS // parts
    piece = group * 96 // RING
    outs = (
        ((tokens, 128), F32),
        ((tokens, 128), F32),
        ((LAYERS, parts, RING, piece, 128), BF16),
    )
    outer = max(batch // RING, 1)
    return pl.pallas_call(
        functools.partial(side_rest_kernel, parts, batch),
        out_shape=tuple(jax.ShapeDtypeStruct(*o) for o in outs),
        in_specs=vmem_specs(20),
        out_specs=tuple(vmem_specs(len(outs))),
        scratch_shapes=[
            vmem((parts, 192, tokens), BF16),
            vmem((tokens, 128), F32),
            vmem((LAYERS, COLUMNS, 96, 128), F32),
            vmem((LAYERS, 8, 128), F32),
            *[vmem(*shape) for shape in keep_shapes(tokens)],
            *weight_scratch(model, units),
            *weight_scratch(model, units),
            vmem((LAYERS, length, 256), BF16),
            vmem((SIDE_HEADS, 16, length), BF16),
            vmem((2, length, tokens), F32),
            dma((3,)),
            dma((parts,)),
            vmem((tokens, 128), BF16),
            vmem((SIDE_HEADS, 16, tokens), BF16),
            vmem((LAYERS, tokens, 256), BF16),
            vmem((LAYERS, SIDE_HEADS, 16, tokens), BF16),
            vmem((LAYERS, length, 128), BF16),
            vmem((LAYERS, SIDE_HEADS, 16, length), BF16),
            vmem((LAYERS, tokens, units), BF16),
            vmem((LAYERS, tokens, units), F32),
            vmem((pairs, parts, 32, tokens), BF16),
            vmem((LAYERS, pairs, parts, 32, tokens), BF16),
            vmem((384, tokens), BF16),
            dma((LAYERS, pairs, parts - 1)),
            dma((LAYERS, pairs, parts)),
            vmem((LAYERS, COLUMNS, 96, 128), BF16),
            vmem((LAYERS, parts, group, 96, 128), BF16),
            vmem((LAYERS, RING, piece, 128), F32),
            vmem((LAYERS, RING, piece, 128), BF16),
            vmem((LAYERS, RING, piece, 128), BF16),
            vmem((LAYERS, outer, piece, 128), BF16),
            dma((LAYERS, 2, parts - 1)),
            dma((LAYERS, 2, parts)),
            dma((LAYERS, RING - 1)),
            dma((LAYERS, RING)),
            dma((LAYERS, max(outer - 1, 1))),
            dma((LAYERS, outer)),
            dma((LAYERS, RING - 1)),
            dma((LAYERS, RING)),
            dma((LAYERS, parts - 1, RING)),
            dma((LAYERS, parts, RING)),
        ],
        compiler_params=pltpu.CompilerParams(
            collective_id=5, has_side_effects=True, vmem_limit_bytes=62 << 20
        ),
    )(first_f, second_f, side_in, cotangent, ids_all, *raw, state_one, kvt_zero, *keep_zero)


def finish_call(frozen, state, grad, full, side, parts):
    tokens, model = frozen.shape
    units = 4 * side
    outs = (
        ((tokens, model), BF16),
        ((side, tokens), F32),
        ((side, tokens), F32),
        ((LAYERS, side, model), F32),
        ((LAYERS, side), F32),
        ((LAYERS, 2, side), F32),
        ((LAYERS, side, 3 * side), F32),
        ((LAYERS, side, side), F32),
        ((LAYERS, side, units), F32),
        ((LAYERS, side, units), F32),
    )
    frozen, state, grad, down, *others, reduce_grad = pl.pallas_call(
        functools.partial(finish_kernel, parts),
        out_shape=tuple(jax.ShapeDtypeStruct(*o) for o in outs),
        in_specs=vmem_specs(4),
        out_specs=tuple(vmem_specs(len(outs))),
        compiler_params=pltpu.CompilerParams(vmem_limit_bytes=62 << 20),
    )(frozen, state, grad, full)
    turn = (0, 2, 1)
    return (frozen, state.T, grad.T, down.transpose(turn), *others, reduce_grad.transpose(turn))


def per_device(
    hidden_rows,
    side_input,
    segment_ids,
    side_cotangent,
    backbone_gains,
    backbone_project,
    backbone_mixing,
    backbone_expand,
    backbone_reduce,
    side_down,
    side_gate,
    side_gains,
    side_project,
    side_mixing,
    side_expand,
    side_reduce,
):
    parts = lax.axis_size("tensor")
    batch = lax.axis_size("batch")
    side = side_input.shape[1]
    turn = (0, 2, 1)
    qkv = backbone_project.transpose(0, 2, 3, 1)
    raw = (
        side_gate,
        side_gains,
        side_down.transpose(turn),
        side_project,
        side_mixing,
        side_expand,
        side_reduce.transpose(turn),
    )
    side_turned, cotangent_turned = side_input.T, side_cotangent.T
    ids_row = segment_ids.reshape(1, -1)

    first_f, second_f, ids_all, state_one, kvt_zero, *keep_zero = front_call(
        hidden_rows,
        ids_row,
        backbone_gains,
        qkv,
        backbone_mixing,
        backbone_expand,
        backbone_reduce,
        side_turned,
        raw,
        parts,
    )
    state, grad, full = side_rest_call(
        first_f, second_f, side_turned, cotangent_turned, ids_all, raw, state_one, kvt_zero, keep_zero, parts, batch
    )
    return finish_call(second_f, state, grad, full, side, parts)


def solution(mesh):
    return jax.shard_map(
        per_device,
        mesh=mesh,
        in_specs=(
            P(("batch", "tensor"), None),
            P(("batch", "tensor"), None),
            P(("batch", "tensor")),
            P(("batch", "tensor"), None),
            P(),
            P(None, None, None, "tensor"),
            P(None, "tensor", None),
            P(None, None, "tensor"),
            P(None, "tensor", None),
            P(),
            P(),
            P(),
            P(),
            P(),
            P(),
            P(),
        ),
        out_specs=(
            P(("batch", "tensor"), None),
            P(("batch", "tensor"), None),
            P(("batch", "tensor"), None),
            P(),
            P(),
            P(),
            P(),
            P(),
            P(),
            P(),
        ),
        check_vma=False,
    )
```

```python
import functools
import jax
import jax.numpy as jnp
from jax import lax
from jax.experimental import pallas as pl
from jax.experimental.pallas import tpu as pltpu
from jax.sharding import PartitionSpec as P

HEAD_DIM = 64
SIDE_HEADS = 12
SIDE_HEAD_DIM = 8
LAYERS = 2
EPS = 1e-06
BIG = 2.0**100
LOG2E = 1.4426950408889634
ID_BITS = 11
QUAD = 4
MESH = pl.DeviceIdType.MESH
F32 = jnp.float32
BF16 = jnp.bfloat16


def contract(left, right, dims):
    return lax.dot_general(left, right, ((dims[:1], dims[1:]), ((), ())), preferred_element_type=F32)


def nn(left, right):
    return contract(left, right, (1, 0))


def nt(left, right):
    return contract(left, right, (1, 1))


def tn(left, right):
    return contract(left, right, (0, 0))


def lanes_of(rows, lanes):
    return lax.broadcasted_iota(jnp.int32, (rows, lanes), 1)


def segment_lanes(id_row, offset):
    width = id_row.shape[1]
    place = lax.broadcasted_iota(jnp.int32, (128, width), 0) - offset
    flipped = place >= ID_BITS
    shift = jnp.clip(jnp.where(flipped, place - ID_BITS, place), 0, ID_BITS)
    bit = lax.shift_right_logical(jnp.broadcast_to(id_row, (128, width)), shift) & 1
    bit = jnp.where(flipped, 1 - bit, bit)
    used = (place >= 0) & (place < 2 * ID_BITS)
    keys = jnp.where(used, bit, 0).astype(F32)
    queries = jnp.where(used, (bit - 1).astype(F32) * BIG, 0.0)
    return keys.T, queries.T


def root_norm(values, gain):
    return values * lax.rsqrt(jnp.mean(values * values, axis=-1, keepdims=True) + EPS) * gain


class Refs:
    def __init__(self, **refs):
        self.__dict__.update(refs)


def remote(src, dst, send, recv, target):
    return pltpu.make_async_remote_copy(
        src_ref=src, dst_ref=dst, send_sem=send, recv_sem=recv, device_id=target, device_id_type=MESH
    )


class Weights:
    def __init__(self, layer, b, t, c):
        self.layer, self.b, self.t, self.c = layer, b, t, c
        self.part = lax.rem(b, QUAD)
        self.fulls = (c.mix_w, c.exp_w, c.red_w)
        self.sources = (c.mix_hbm, c.exp_hbm, c.red_hbm)
        self.slices = tuple(w.shape[2] // QUAD for w in self.fulls)
        mix, up, down = self.slices
        self.pieces = (
            (0, 0, mix),
            (1, 0, up // 2),
            (1, up // 2, up // 2),
            (2, 0, down // 2),
            (2, down // 2, down // 2),
        )

    def rows(self, p, part):
        w, low, size = self.pieces[p]
        return pl.ds(pl.multiple_of(part * self.slices[w] + low, 16), size)

    def view(self, p, slot, part):
        return self.fulls[self.pieces[p][0]].at[self.layer, slot, self.rows(p, part)]

    def load(self, w):
        return pltpu.make_async_copy(
            self.sources[w].at[self.layer],
            self.fulls[w].at[self.layer, self.t],
            self.c.load_sem.at[self.layer, w],
        )

    def own(self, w, slot):
        c = self.c
        return remote(
            self.sources[w].at[self.layer],
            self.fulls[w].at[self.layer, slot],
            c.own_send.at[self.layer, w],
            c.own_recv.at[self.layer, w],
            (self.b, self.t ^ 1),
        )

    def cross(self, p):
        c = self.c
        return remote(
            self.sources[self.pieces[p][0]].at[self.layer, self.rows(p, self.part)],
            self.view(p, self.t, self.part),
            c.cross_send.at[self.layer, p],
            c.w_recv.at[self.layer, p, self.part],
            (self.b, self.t ^ 2),
        )

    def spread(self, p, k):
        c = self.c
        view = self.view(p, self.t ^ 2, self.part)
        return remote(
            view, view, c.spread_send.at[self.layer, p, k - 1], c.w_recv.at[self.layer, p, self.part], (self.b ^ k, self.t)
        )

    def here(self, p, k):
        c = self.c
        view = self.view(p, self.t ^ 2, self.part ^ k)
        return remote(
            view, view, c.cross_send.at[self.layer, p], c.w_recv.at[self.layer, p, self.part ^ k], (self.b, self.t ^ 2)
        )

    def forward(self, p, k, slot):
        c = self.c
        view = self.view(p, slot, self.part ^ k)
        return remote(
            view,
            view,
            c.pass_send.at[self.layer, p, k],
            c.pass_recv.at[self.layer, p, self.part ^ k],
            (self.b, self.t ^ 1),
        )

    def start_cross(self):
        for p in range(5):
            self.cross(p).start()

    def start_spread(self, p):
        self.here(p, 0).wait_recv()
        for k in range(1, QUAD):
            self.spread(p, k).start()

    def start_forward(self, p):
        for k in range(1, QUAD):
            self.here(p, k).wait_recv()
        for k in range(QUAD):
            self.forward(p, k, self.t ^ 2).start()

    def wait_far(self, p):
        for k in range(QUAD):
            self.forward(p, k, self.t ^ 3).wait_recv()

    def wait_sent(self):
        for w in range(3):
            self.own(w, self.t).wait_send()
        for p in range(5):
            self.cross(p).wait_send()
            for k in range(1, QUAD):
                self.spread(p, k).wait_send()
            for k in range(QUAD):
                self.forward(p, k, self.t ^ 2).wait_send()


class Backbone:
    def __init__(self, layer, b, t, parts, c):
        self.layer, self.b, self.t, self.parts, self.c = layer, b, t, parts, c
        self.sib, self.across, self.far = t ^ 1, t ^ 2, t ^ 3
        self.tokens = c.rows_all.shape[1]
        self.half = self.tokens // 2
        self.width = c.mix_w.shape[2]
        self.heads = self.width // HEAD_DIM
        self.weights = Weights(layer, b, t, c)

    def row_copy(self, slot, chunk, send, target):
        c = self.c
        view = c.rows_all.at[slot, pl.ds(chunk * self.half, self.half)]
        return remote(
            view,
            view,
            c.row_send.at[self.layer, send, chunk],
            c.row_recv.at[self.layer, slot, chunk],
            (self.b, target),
        )

    def norm_rows(self, stream):
        c = self.c
        gain = c.gains[self.layer, 0:1, :].astype(F32)
        c.rows_all[self.t] = root_norm(stream, gain).astype(BF16)

    def send_rows(self):
        for chunk in range(2):
            self.row_copy(self.t, chunk, 1, self.across).start()
        for chunk in range(2):
            self.row_copy(self.t, chunk, 0, self.sib).start()

    def project(self, slot, chunk):
        c, width, half = self.c, self.width, self.half
        inside = pl.ds(pl.multiple_of(chunk * half, half), half)
        rows = c.rows_all[slot, inside, :]
        at = pl.ds(pl.multiple_of(slot * self.tokens + chunk * half, half), half)
        lane = lanes_of(half, 128)
        query = nt(rows, c.qkv_w[self.layer, 0]) * (HEAD_DIM**-0.5 * LOG2E)
        keys = nt(rows, c.qkv_w[self.layer, 1])
        bits = segment_lanes(c.ids_all[slot, 0:1, inside], HEAD_DIM)
        for target, columns, high in ((c.k_s, keys, bits[0]), (c.q_s, query, bits[1])):
            low = pltpu.roll(high, HEAD_DIM, 1)
            for h in range(self.heads):
                own = columns[:, h // 2 * 128 : h // 2 * 128 + 128]
                inner = jnp.where(lane < HEAD_DIM, own, high) if h % 2 == 0 else jnp.where(lane < HEAD_DIM, low, own)
                target[h, at] = inner.astype(BF16)
        values = nt(c.qkv_w[self.layer, 2, 0:width], rows)
        for h in range(self.heads):
            c.vt_s[h, 0:HEAD_DIM, at] = values[h * HEAD_DIM : (h + 1) * HEAD_DIM].astype(BF16)
            c.vt_s[h, HEAD_DIM:, at] = jnp.ones((16, half), BF16)

    def project_all(self, first, last, hook):
        def step(index, carry):
            for chunk in range(2):

                @pl.when(index == 2 + chunk)
                def _():
                    self.row_copy(self.sib, chunk, 0, self.sib).wait_recv()

                @pl.when(index == 4 + 2 * chunk)
                def _():
                    self.row_copy(self.across, chunk, 0, self.sib).wait_recv()
                    self.row_copy(self.across, chunk, 2, self.sib).start()

                @pl.when(index == 5 + 2 * chunk)
                def _():
                    self.row_copy(self.far, chunk, 0, self.sib).wait_recv()

            hook(index)
            early = index < 4
            k = jnp.where(early, index // 2, 2 + index % 2)
            chunk = jnp.where(early, index % 2, index // 2 - 2)
            self.project(self.t ^ k, chunk)
            return carry

        lax.fori_loop(first, last, step, 0)

    def wait_rows(self):
        for chunk in range(2):
            self.row_copy(self.t, chunk, 0, self.sib).wait_send()
            self.row_copy(self.t, chunk, 1, self.across).wait_send()
            self.row_copy(self.across, chunk, 2, self.sib).wait_send()

    def block_of(self, item):
        return self.t ^ (self.parts - 1 - item // self.heads)

    def make_scores(self, item, place):
        c = self.c
        h = lax.rem(item, self.heads)
        at = pl.ds(pl.multiple_of(self.block_of(item) * self.tokens, self.tokens), self.tokens)
        c.scores[place] = nt(c.k_s[h], c.q_s[h, at])

    def send_heads(self, block):
        c = self.c
        return remote(
            c.heads_buf.at[block],
            c.heads_buf.at[self.parts + self.t],
            c.head_send.at[self.layer, block],
            c.head_recv.at[self.layer, self.t],
            (self.b, block),
        )

    def attend(self, item, place):
        c = self.c
        block = self.block_of(item)
        h = lax.rem(item, self.heads)
        values = c.scores[place]
        weights = jnp.exp2(values - jnp.max(values, axis=0, keepdims=True)).astype(BF16)
        out = nn(c.vt_s[h], weights)
        slot = jnp.where(block == self.t, self.parts + self.t, block)
        c.heads_buf[slot, pl.ds(pl.multiple_of(h * HEAD_DIM, HEAD_DIM), HEAD_DIM), :] = (
            out[0:HEAD_DIM] * (1.0 / out[HEAD_DIM : HEAD_DIM + 1])
        ).astype(BF16)

        @pl.when((h == self.heads - 1) & (item < (self.parts - 1) * self.heads))
        def _():
            self.send_heads(block).start()

    def attention(self, hook):
        count = self.parts * self.heads
        self.make_scores(0, 0)

        def pair(index, carry):
            item = 2 * index
            hook(index)
            self.make_scores(item + 1, 1)
            self.attend(item, 0)
            self.make_scores(jnp.minimum(item + 2, count - 1), 0)
            self.attend(item + 1, 1)
            return carry

        lax.fori_loop(0, count // 2, pair, 0)

    def wait_heads(self):
        c = self.c
        for k in range(1, self.parts):
            self.send_heads(self.t ^ k).wait_send()
            remote(
                c.heads_buf.at[0],
                c.heads_buf.at[self.parts + (self.t ^ k)],
                c.head_send.at[self.layer, 0],
                c.head_recv.at[self.layer, self.t ^ k],
                (self.b, self.sib),
            ).wait_recv()

    def feed_forward(self, stream, own_chip, far_up, near_down, far_down):
        c, parts, layer = self.c, self.parts, self.layer
        attended = c.heads_buf[parts : 2 * parts].reshape(parts * self.width, self.tokens)
        stream = stream + tn(attended, c.mix_w[layer].reshape(parts * self.width, -1))
        c.acc[...] = stream
        c.normed[...] = root_norm(stream, c.gains[layer, 1:2, :].astype(F32)).astype(BF16)

        def hidden(slot):
            return jax.nn.gelu(nn(c.normed[...], c.exp_w[layer, slot])).astype(BF16)

        def feed(index, carry):
            own_chip(index)
            c.acc[...] += nn(hidden(self.t ^ index), c.red_w[layer, self.t ^ index])
            return carry

        lax.fori_loop(0, 2, feed, 0)
        c.rows_all[self.t] = hidden(self.across)
        far_up()
        c.spare[...] = hidden(self.far)
        near_down()
        c.acc[...] += nn(c.rows_all[self.t], c.red_w[layer, self.across])
        far_down()
        c.acc[...] += nn(c.spare[...], c.red_w[layer, self.far])


FRONT_SCRATCH = (
    *("vectors", "rows_all", "ids_scratch", "qkv_w", "mix_w", "exp_w", "red_w", "q_s", "k_s", "vt_s", "scores"),
    *("heads_buf", "acc", "normed", "load_sem", "qkv_sem", "row_send", "row_recv", "id_send", "id_recv"),
    *("head_send", "head_recv", "cross_send", "spread_send", "pass_send", "own_send", "w_recv", "pass_recv"),
    *("own_recv", "side_k", "side_vt", "kv_send", "kv_recv"),
)


def front_kernel(parts, *refs):
    refs = list(refs)

    def pop(count):
        taken, refs[:count] = refs[:count], []
        return taken

    x_ref, ids_ref, gains, qkv_hbm, mix_hbm, exp_hbm, red_hbm, side_in = pop(8)
    raw = Refs(**dict(zip(RAW, pop(7))))
    second_f, *handed = pop(11)
    local = pop(10)
    first_f, ids_all, state_one, kvt = local[0:4]
    keep = Refs(**dict(zip(KEEP, local[4:])))
    hand_sem = pop(1)[0]
    hand = [pltpu.make_async_copy(*pair, hand_sem.at[k]) for k, pair in enumerate(zip(local, handed))]
    prev = pop(1)[0]
    w = Refs(**dict(zip(WEIGHTS, pop(5))))
    c = Refs(**dict(zip(FRONT_SCRATCH, pop(len(FRONT_SCRATCH)))))
    c.spare = second_f
    c.gains, c.mix_hbm, c.exp_hbm, c.red_hbm, c.ids_all = gains, mix_hbm, exp_hbm, red_hbm, ids_all
    b = lax.axis_index("batch")
    t = lax.axis_index("tensor")
    tokens = x_ref.shape[0]
    width = c.mix_w.shape[2]
    lower, upper = Backbone(0, b, t, parts, c), Backbone(1, b, t, parts, c)
    load_qkv = [
        pltpu.make_async_copy(
            qkv_hbm.at[layer, k], c.qkv_w.at[layer, k, pl.ds(0, width)], c.qkv_sem.at[layer, k]
        )
        for layer in range(LAYERS)
        for k in range(3)
    ]
    for copy in load_qkv:
        copy.start()
    for layer in (lower, upper):
        for k in range(3):
            layer.weights.load(k).start()
    barrier = tensor_barrier(b, t, parts)
    for k in range(1, QUAD):
        pl.semaphore_signal(barrier, inc=1, device_id=(b ^ k, t), device_id_type=MESH)
    lower.norm_rows(x_ref[...].astype(F32))
    ids_all[t] = jnp.broadcast_to(ids_ref[...], (8, tokens))
    pl.semaphore_wait(barrier, parts - 1 + QUAD - 1)

    def id_copy(slot, k):
        return remote(ids_all.at[slot], ids_all.at[slot], c.id_send.at[k - 1], c.id_recv.at[slot], (b, t ^ k))

    for k in range(1, parts):
        id_copy(t, k).start()
    lower.weights.cross(1).start()
    lower.send_rows()
    for k in range(3):
        lower.weights.own(k, t).start()
    c.qkv_w[:, :, width:, :] = jnp.zeros((LAYERS, 3, 256 - width, x_ref.shape[1]), BF16)
    for copy in load_qkv:
        copy.wait()
    load_side_weights(0, w, raw)
    load_vectors(c.vectors, raw)
    raw.vectors = c.vectors
    prev[...] = widened(side_in)
    for k in range(1, parts):
        id_copy(t, k).wait_send()
        id_copy(t ^ k, k).wait_recv()

    def when(index, at, act, *args):
        @pl.when(index == at)
        def _():
            act(*args)

    def lower_project(index):
        when(index, 4, lower.weights.start_spread, 1)
        for p in (0, 2, 3, 4):
            when(index, 6, lambda p: lower.weights.cross(p).start(), p)

    def lower_attention(index):
        for at, p in ((1, 0), (2, 2), (3, 3), (5, 4)):
            when(index, at, lower.weights.start_spread, p)
        for at, p in ((4, 1), (5, 0)):
            when(index, at, lower.weights.start_forward, p)

    def feed_hooks(layer):
        weights = layer.weights

        def own_chip(index):
            @pl.when(index == 0)
            def _():
                for k in (1, 2):
                    weights.load(k).wait()
                if layer is lower:
                    weights.start_forward(2)

            @pl.when(index == 1)
            def _():
                for k in (1, 2):
                    weights.own(k, layer.sib).wait_recv()

        def far_up():
            for p in (1, 2):
                weights.wait_far(p)

        def near_down():
            if layer is lower:
                for p in (3, 4):
                    weights.start_forward(p)

        def far_down():
            for p in (3, 4):
                weights.wait_far(p)

        return own_chip, far_up, near_down, far_down

    lower.project_all(0, 2 * parts, lower_project)
    lower.wait_rows()
    lower.attention(lower_attention)
    upper.weights.start_cross()
    for k in range(3):
        upper.weights.own(k, t).start()
    lower.weights.load(0).wait()
    lower.weights.own(0, lower.sib).wait_recv()
    lower.weights.wait_far(0)
    lower.wait_heads()
    lower.feed_forward(x_ref[...].astype(F32), *feed_hooks(lower))
    first_f[...] = c.acc[...].astype(BF16)

    side = Refs(
        kvt=kvt, k_s=c.side_k, vt_s=c.side_vt, scores=c.scores, kv_send=c.kv_send, kv_recv=c.kv_recv
    )

    def send_upper():
        upper.norm_rows(c.acc[...])
        upper.send_rows()

    def side_hook(index):
        for p in range(5):
            when(index, p, upper.weights.start_spread, p)

    side_forward(
        0, b, t, parts, first_f, prev, w, raw, side, keep, ids_all, state_one,
        send_upper, lambda: upper.project_all(0, parts, lambda index: None), side_hook,
    )

    for copy in hand:
        copy.start()

    def upper_attention(index):
        for p in range(5):
            when(index, p + 1, upper.weights.start_forward, p)

    upper.project_all(parts, 2 * parts, lambda index: None)
    upper.wait_rows()
    upper.attention(upper_attention)
    upper.weights.load(0).wait()
    upper.weights.own(0, upper.sib).wait_recv()
    upper.weights.wait_far(0)
    upper.wait_heads()
    upper.feed_forward(c.acc[...], *feed_hooks(upper))
    second_f[...] = c.acc[...].astype(BF16)
    for copy in hand:
        copy.wait()
    lower.weights.wait_sent()
    upper.weights.wait_sent()


def front_call(x, ids, gains, qkv, mix, exp, red, side_in, raw, parts):
    tokens, model = x.shape
    width = mix.shape[1]
    units = exp.shape[2]
    heads = width // HEAD_DIM
    length = parts * tokens
    side_units = raw[5].shape[2]
    anywhere = pl.BlockSpec(memory_space=pl.ANY)
    dma = pltpu.SemaphoreType.DMA
    vmem = pltpu.VMEM
    outs = (
        ((tokens, model), BF16),
        ((tokens, model), BF16),
        ((parts, 8, tokens), jnp.int32),
        ((tokens, 128), F32),
        ((parts, 192, tokens), BF16),
        *keep_shapes(tokens),
    )
    return pl.pallas_call(
        functools.partial(front_kernel, parts),
        out_shape=tuple(jax.ShapeDtypeStruct(*o) for o in outs),
        in_specs=vmem_specs(3) + [anywhere] * 4 + vmem_specs(8),
        out_specs=(*vmem_specs(1), *[anywhere] * 10),
        scratch_shapes=[
            *[vmem(*out) for out in outs[1:]],
            dma((10,)),
            vmem((tokens, 128), F32),
            *weight_scratch(model, side_units),
            vmem((LAYERS, 8, 128), F32),
            vmem((parts, tokens, model), BF16),
            vmem((8, 128), F32),
            vmem((LAYERS, 3, 256, model), BF16),
            vmem((LAYERS, parts, width, model), BF16),
            vmem((LAYERS, parts, model, units), BF16),
            vmem((LAYERS, parts, units, model), BF16),
            vmem((heads, length, 128), BF16),
            vmem((heads, length, 128), BF16),
            vmem((heads, HEAD_DIM + 16, length), BF16),
            vmem((2, length, tokens), F32),
            vmem((2 * parts, width, tokens), BF16),
            vmem((tokens, model), F32),
            vmem((tokens, model), BF16),
            dma((LAYERS, 3)),
            dma((LAYERS, 3)),
            dma((LAYERS, 3, 2)),
            dma((LAYERS, parts, 2)),
            dma((parts - 1,)),
            dma((parts,)),
            dma((LAYERS, parts)),
            dma((LAYERS, parts)),
            dma((LAYERS, 5)),
            dma((LAYERS, 5, QUAD - 1)),
            dma((LAYERS, 5, QUAD)),
            dma((LAYERS, 3)),
            dma((LAYERS, 5, QUAD)),
            dma((LAYERS, 5, QUAD)),
            dma((LAYERS, 3)),
            vmem((length, 128), BF16),
            vmem((SIDE_HEADS, 16, length), BF16),
            dma((3,)),
            dma((parts,)),
        ],
        compiler_params=pltpu.CompilerParams(
            collective_id=1, has_side_effects=True, vmem_limit_bytes=62 << 20
        ),
    )(x, ids, gains, qkv, mix, exp, red, side_in, *raw)


LN2 = 0.6931471805599453
COLUMNS = 16
EARLY = (6, 7, 8, 9, 10, 11, 12, 13)
LATE = (0, 1, 2, 3, 4, 5, 14, 15)


def place_of(column):
    order, low = (EARLY, 0) if column in EARLY else (LATE, 2)
    index = order.index(column)
    return index // 2 * 4 + low + index % 2


RING = 8


def side_norm(values, width):
    rstd = lax.rsqrt(jnp.sum(values * values, axis=-1, keepdims=True) * (1.0 / width) + EPS)
    return values * rstd, rstd


def gelu_parts(inner):
    root = 0.7978845608028654
    square = inner * inner
    curve = jnp.tanh(root * inner * (1.0 + 0.044715 * square))
    half = 0.5 * (1.0 + curve)
    slope = half + 0.5 * inner * (1.0 - curve * curve) * root * (1.0 + 3 * 0.044715 * square)
    return inner * half, slope


def load_side_weights(layer, w, raw):
    side = raw.mixing.shape[1]
    w.down[side:, :] = jnp.zeros_like(w.down[side:, :])
    w.down[0:side, :] = raw.down[layer]
    w.project[...] = jnp.zeros_like(w.project)
    w.project[0:side, 0 : 3 * side] = raw.project[layer]
    w.mixing[...] = jnp.zeros_like(w.mixing)
    w.mixing[0:side, 0:side] = raw.mixing[layer]
    w.expand[side:, :] = jnp.zeros_like(w.expand[side:, :])
    w.expand[0:side, :] = raw.expand[layer]
    w.reduce[side:, :] = jnp.zeros_like(w.reduce[side:, :])
    w.reduce[0:side, :] = raw.reduce[layer]


def load_vectors(vectors, raw):
    side = raw.mixing.shape[1]
    vectors[...] = jnp.zeros_like(vectors)
    for layer in range(LAYERS):
        vectors[layer, 0:1, 0:side] = raw.gate[layer : layer + 1, :]
        vectors[layer, 1:3, 0:side] = raw.gains[layer].astype(F32)


def widened(turned):
    values = turned[...].astype(F32)
    return jnp.concatenate([values, jnp.zeros((32, values.shape[1]), F32)], axis=0).T


def kv_copy(c, slot, send, target):
    return remote(c.kvt.at[slot], c.kvt.at[slot], c.kv_send.at[send], c.kv_recv.at[slot], target)


def keys_from(c, slot, ids_ref):
    tokens = c.kvt.shape[2]
    at = pl.ds(pl.multiple_of(slot * tokens, tokens), tokens)
    key_bits, _ = segment_lanes(ids_ref[slot][0:1, :], 96)
    keys = jnp.concatenate([c.kvt[slot, 0:96].astype(F32), jnp.zeros((32, tokens), F32)], axis=0)
    c.k_s[at, 0:128] = (keys.T + key_bits).astype(BF16)


def side_forward(layer, b, t, parts, f_ref, prev, w, raw, c, keep, ids_ref, result, after_send, meanwhile, between):
    side = raw.mixing.shape[1]
    tokens = f_ref.shape[0]
    gate = jax.nn.sigmoid(raw.vectors[layer, 0:1, :])
    lifted = nt(f_ref[...], w.down[...])
    mixed = gate * lifted + (1.0 - gate) * prev[...]
    keep.lifted[...] = lifted
    keep.mixed[...] = mixed
    normed = (side_norm(mixed, side)[0] * raw.vectors[layer, 1:2, :]).astype(BF16)
    turned = w.project[...].astype(F32).T.astype(BF16)
    c.kvt[t] = nt(turned[side : 3 * side], normed).astype(BF16)
    sib, across, far = t ^ 1, t ^ 2, t ^ 3
    kv_copy(c, t, 1, (b, across)).start()
    kv_copy(c, t, 0, (b, sib)).start()
    after_send()
    lane = lanes_of(tokens, 128)
    weight_q = jnp.where(lanes_of(128, 128) < side, w.project[:, 0:128], jnp.zeros((128, 128), BF16))
    query_bits = segment_lanes(ids_ref[t][0:1, :], 96)[1]
    keep.query[...] = (
        nn(normed, weight_q) * (SIDE_HEAD_DIM**-0.5 * LOG2E) + query_bits
    ).astype(BF16)
    keep.sums[...] = jnp.zeros_like(keep.sums)

    def take(index, carry):
        @pl.when(index == 1)
        def _():
            kv_copy(c, sib, 0, (b, sib)).wait_recv()

        @pl.when(index == 2)
        def _():
            meanwhile()
            kv_copy(c, across, 0, (b, sib)).wait_recv()
            kv_copy(c, across, 2, (b, sib)).start()

        @pl.when(index == 3)
        def _():
            kv_copy(c, far, 0, (b, sib)).wait_recv()

        slot = t ^ index
        at = pl.ds(pl.multiple_of(slot * tokens, tokens), tokens)
        keys_from(c, slot, ids_ref)
        values = c.kvt[slot, 96:192].astype(F32)
        for h in range(SIDE_HEADS):
            c.vt_s[h, :, at] = jnp.concatenate(
                [values[8 * h : 8 * h + 8], jnp.ones((8, tokens), F32)], axis=0
            ).astype(BF16)
        return carry

    lax.fori_loop(0, parts, take, 0)

    def make_scores(h, place):
        rows = keep.query[...]
        chosen = (lane // SIDE_HEAD_DIM == h) | (lane >= side)
        c.scores[place] = nt(c.k_s[:, 0:128], jnp.where(chosen, rows, jnp.zeros_like(rows)))

    def attend(h, place):
        values = c.scores[place]
        top = jnp.max(values, axis=0, keepdims=True)
        out = nn(c.vt_s[h], jnp.exp2(values - top).astype(BF16))
        total = out[8:9]
        keep.heads[pl.ds(pl.multiple_of(h * 8, 8), 8), :] = out[0:8] * (1.0 / total)
        here = lax.broadcasted_iota(jnp.int32, keep.sums.shape, 0) == h
        keep.sums[...] = jnp.where(here, top + jnp.log2(total), keep.sums[...])

    make_scores(0, 0)

    def pair(index, carry):
        h = 2 * index
        between(index)
        make_scores(h + 1, 1)
        attend(h, 0)
        make_scores(jnp.minimum(h + 2, SIDE_HEADS - 1), 0)
        attend(h + 1, 1)
        return carry

    lax.fori_loop(0, SIDE_HEADS // 2, pair, 0)
    kv_copy(c, t, 1, (b, across)).wait_send()
    kv_copy(c, t, 0, (b, sib)).wait_send()
    kv_copy(c, across, 2, (b, sib)).wait_send()
    middle = mixed + tn(keep.heads[...].astype(BF16), w.mixing[0:side, :])
    keep.middle[...] = middle
    normed_two = (side_norm(middle, side)[0] * raw.vectors[layer, 2:3, :]).astype(BF16)
    active = jax.nn.gelu(nn(normed_two, w.expand[...])).astype(BF16)
    result[...] = middle + nt(active, w.reduce[...])


def norm_back(values, gain, grad, side):
    hat, rstd = side_norm(values, side)
    gain_grad = jnp.sum(grad * hat, axis=0, keepdims=True)
    pulled = grad * gain
    mean = jnp.sum(pulled * hat, axis=-1, keepdims=True) * (1.0 / side)
    return rstd * (pulled - hat * mean), gain_grad


def pad_heads(target, rows, fill):
    for h in range(SIDE_HEADS):
        target[h] = jnp.concatenate(
            [rows[8 * h : 8 * h + 8], jnp.full((8, rows.shape[1]), fill, F32)], axis=0
        ).astype(BF16)


def side_prepare(layer, parts, w, raw, c, keep, kvt, ids_ref, again):
    side = raw.mixing.shape[1]
    tokens = c.q_s.shape[1]
    lane = lanes_of(tokens, 128)
    normed_two = side_norm(keep.middle[...], side)[0] * raw.vectors[layer, 2:3, :]
    active, slope = gelu_parts(nn(normed_two.astype(BF16), w.expand[...]))
    c.active[layer] = active.astype(BF16)
    c.slope[layer] = slope
    sums = keep.sums[...]
    rows = jnp.concatenate([sums, sums, sums, jnp.zeros((80, tokens), F32)], axis=0).T
    high = rows.astype(BF16).astype(F32)
    mid = (rows - high).astype(BF16).astype(F32)
    low = rows - high - mid
    rows = jnp.where(lane < 16, high, jnp.where(lane < 32, mid, low))
    query = keep.query[...]
    c.q_s[layer, :, 0:128] = query
    c.q_s[layer, :, 128:256] = jnp.where(lane < 48, -rows, 0.0).astype(BF16)
    pad_heads(c.qt_s.at[layer], query.astype(F32).T, 0.0)

    def take(slot, carry):
        at = pl.ds(pl.multiple_of(slot * tokens, tokens), tokens)
        if again:
            keys_from(Refs(kvt=kvt, k_s=c.k_s.at[layer]), slot, ids_ref)
        c.k_s[layer, at, 128:256] = jnp.where(lane < 48, 1.0, 0.0).astype(BF16)
        values = jnp.concatenate([kvt[slot, 96:192].astype(F32), jnp.ones((32, tokens), F32)], axis=0)
        c.v_s[layer, at, :] = values.T.astype(BF16)
        keys = kvt[slot, 0:96].astype(F32)
        for h in range(SIDE_HEADS):
            c.kt_s[layer, h, :, at] = jnp.concatenate(
                [keys[8 * h : 8 * h + 8], jnp.zeros((8, tokens), F32)], axis=0
            ).astype(BF16)
        return carry

    lax.fori_loop(0, parts, take, 0)


def side_backward(layer, b, t, parts, f_ref, prev, w, raw, c, keep, grad_ref, pack, between, early):
    side = raw.mixing.shape[1]
    tokens = f_ref.shape[0]
    gate = jax.nn.sigmoid(raw.vectors[layer, 0:1, :])
    lane = lanes_of(tokens, 128)
    grad = grad_ref[...]
    middle = keep.middle[...]
    gain_two = raw.vectors[layer, 2:3, :]
    normed_two = (side_norm(middle, side)[0] * gain_two).astype(BF16)
    top = grad.astype(BF16)
    reduce_grad = tn(top, c.active[layer])
    grad_inner = (c.slope[layer] * nn(top, w.reduce[...])).astype(BF16)
    expand_grad = tn(normed_two, grad_inner)
    for k in range(3):
        pack[place_of(6 + k)] = expand_grad[0:96, 128 * k : 128 * k + 128]
        pack[place_of(9 + k)] = reduce_grad[0:96, 128 * k : 128 * k + 128]
    through, gain_two_grad = norm_back(middle, gain_two, nt(grad_inner, w.expand[...]), side)
    grad_middle = grad + through
    branch = grad_middle.astype(BF16)
    heads = keep.heads[...]
    mixing_grad = nn(heads.astype(BF16), branch)
    grad_heads = nt(branch, w.mixing[...]).astype(BF16).astype(F32).T
    product = grad_heads[0:96] * heads
    group = lax.broadcasted_iota(jnp.int32, (16, 96), 1) // SIDE_HEAD_DIM
    group = (group == lax.broadcasted_iota(jnp.int32, (16, 96), 0)).astype(BF16)
    high = product.astype(BF16)
    inner = nn(group, high) + nn(group, (product - high.astype(F32)).astype(BF16))
    rows = jnp.concatenate([grad_heads[0:96], -inner, -inner], axis=0).T
    high = rows.astype(BF16)
    c.do_s[...] = jnp.where(lane < 112, high, (rows - high.astype(F32)).astype(BF16))
    pad_heads(c.dot_s, grad_heads, 0.0)
    wide = lanes_of(tokens, 256)
    query_head = jnp.where(wide < 96, wide // SIDE_HEAD_DIM, jnp.where(wide < 128, -1, (wide - 128) % 16))
    out_head = jnp.where(lane < 96, lane // SIDE_HEAD_DIM, (lane - 96) % 16)

    count = parts * tokens // 2

    def one_head(h, keys):
        rows = c.q_s[layer]
        rows = jnp.where((query_head == h) | (query_head < 0), rows, jnp.zeros_like(rows))
        probs = jnp.exp2(nt(rows, c.k_s[layer, keys, :]))
        rows = c.do_s[...]
        rows = jnp.where(out_head == h, rows, jnp.zeros_like(rows))
        scores = (probs * nt(rows, c.v_s[layer, keys, :])).astype(BF16)
        by_keys = nn(c.qt_s[layer, h], scores)[0:8] * LN2
        by_values = nn(c.dot_s[h], probs.astype(BF16))[0:8]
        return by_keys, by_values, nt(c.kt_s[layer, h, :, keys], scores)[0:8] * SIDE_HEAD_DIM**-0.5

    def terms_copy(pair, k):
        return remote(
            c.terms.at[pair, t ^ k],
            c.terms_in.at[layer, pair, t],
            c.terms_send.at[layer, pair, k - 1],
            c.terms_recv.at[layer, pair, t],
            (b, t ^ k),
        )

    def terms_wait(pair, k):
        return remote(
            c.terms.at[pair, t ^ k],
            c.terms_in.at[layer, pair, t ^ k],
            c.terms_send.at[layer, pair, k - 1],
            c.terms_recv.at[layer, pair, t ^ k],
            (b, t ^ k),
        )

    def pair_of(index, carry):
        between(index)
        queries = jnp.zeros((16, tokens), F32)
        for near in range(2):
            chip = t // 2 if near else (t // 2) ^ 1
            keys = pl.ds(pl.multiple_of(chip * count, count), count)
            first, second = one_head(2 * index, keys), one_head(2 * index + 1, keys)
            by_keys, by_values, by_queries = (
                jnp.concatenate([left, right], axis=0) for left, right in zip(first, second)
            )
            queries += by_queries
            for place in range(parts // 2):
                at = slice(place * tokens, (place + 1) * tokens)
                c.terms[index, chip * (parts // 2) + place, 0:16] = by_keys[:, at].astype(BF16)
                c.terms[index, chip * (parts // 2) + place, 16:32] = by_values[:, at].astype(BF16)
            for k in (1,) if near else (2, 3):
                terms_copy(index, k).start()
        c.dqkv[pl.ds(pl.multiple_of(index * 16, 16), 16), :] = queries.astype(BF16)
        return carry

    pairs = SIDE_HEADS // 2
    lax.fori_loop(0, pairs, pair_of, 0)
    mixed = keep.mixed[...]
    gain_one = raw.vectors[layer, 1:2, :]
    normed = side_norm(mixed, side)[0] * gain_one
    c.dqkv[288:384, :] = jnp.zeros((96, tokens), BF16)

    def gather(index, carry):
        total = c.terms[index, t].astype(F32)
        for k in range(1, parts):
            terms_wait(index, k).wait_recv()
            total += c.terms_in[layer, index, t ^ k].astype(F32)
        total = total.astype(BF16)
        c.dqkv[pl.ds(pl.multiple_of(96 + index * 16, 16), 16), :] = total[0:16]
        c.dqkv[pl.ds(pl.multiple_of(192 + index * 16, 16), 16), :] = total[16:32]
        return carry

    lax.fori_loop(0, pairs, gather, 0)
    dqkv = c.dqkv[...]
    project_grad = nt(normed.T.astype(BF16), dqkv)
    pack[place_of(12)] = project_grad[0:96, 0:128]
    pack[place_of(13)] = project_grad[0:96, 128:256]
    pack[place_of(14)] = project_grad[0:96, 256:384] + pltpu.roll(mixing_grad, 32, 1)
    early()
    grad_normed = nn(w.project[...], dqkv).T
    through, gain_one_grad = norm_back(mixed, gain_one, grad_normed, side)
    grad_mixed = grad_middle + through
    down_grad = nn((gate * grad_mixed).T.astype(BF16), f_ref[...])
    for k in range(6):
        pack[place_of(k)] = down_grad[0:96, 128 * k : 128 * k + 128]
    gate_grad = jnp.sum(grad_mixed * (keep.lifted[...] - prev[...]), axis=0, keepdims=True)
    gate_grad = gate_grad * gate * (1.0 - gate)
    row = lax.broadcasted_iota(jnp.int32, (96, 128), 0)
    pack[place_of(15)] = jnp.where(
        row == 0, gate_grad, jnp.where(row == 1, gain_one_grad, jnp.where(row == 2, gain_two_grad, 0.0))
    )
    grad_ref[...] = (1.0 - gate) * grad_mixed

    def sent(index, carry):
        for k in range(1, parts):
            terms_copy(index, k).wait_send()
        return carry

    lax.fori_loop(0, pairs, sent, 0)


class Sum:
    def __init__(self, r, b, t, parts, batch, pack, s):
        self.r, self.b, self.t, self.parts, self.batch, self.pack, self.s = r, b, t, parts, batch, pack, s
        self.place = lax.rem(b, RING)
        self.outer = batch // RING

    def across_tensor(self, half, k):
        r, s, t = self.r, self.s, self.t
        group = COLUMNS // self.parts
        return remote(
            s.out.at[r, pl.ds((t ^ k) * group + half * (group // 2), group // 2)],
            s.one.at[r, t, pl.ds(half * (group // 2), group // 2)],
            s.one_send.at[r, half, k - 1],
            s.one_recv.at[r, half, t],
            (self.b, t ^ k),
        )

    def from_tensor(self, half, k):
        r, s, t = self.r, self.s, self.t
        group = COLUMNS // self.parts
        view = s.one.at[r, t ^ k, pl.ds(half * (group // 2), group // 2)]
        return remote(view, view, s.one_send.at[r, half, k - 1], s.one_recv.at[r, half, t ^ k], (self.b, t ^ k))

    def across_batch(self, k):
        r, s = self.r, self.s
        return remote(
            s.mid_out.at[r, self.place ^ k], s.two.at[r, self.place], s.two_send.at[r, k - 1],
            s.two_recv.at[r, self.place], (self.b ^ k, self.t),
        )

    def from_batch(self, k):
        r, s = self.r, self.s
        return remote(
            s.two.at[r, self.place ^ k], s.two.at[r, self.place ^ k], s.two_send.at[r, k - 1],
            s.two_recv.at[r, self.place ^ k], (self.b ^ k, self.t),
        )

    def across_outer(self, k):
        r, s = self.r, self.s
        mine = self.b // RING
        target = lax.rem(mine + k, self.outer) * RING + self.place
        return remote(
            s.far.at[r, mine], s.far.at[r, mine], s.far_send.at[r, k - 1], s.far_recv.at[r, mine], (target, self.t)
        )

    def from_outer(self, k):
        r, s = self.r, self.s
        other = lax.rem(self.b // RING + k, self.outer)
        return remote(
            s.far.at[r, other], s.far.at[r, other], s.far_send.at[r, k - 1], s.far_recv.at[r, other],
            (self.b ^ 1, self.t),
        )

    def back_batch(self, k, place):
        r, s = self.r, self.s
        return remote(
            s.full.at[r, self.t, place], s.full.at[r, self.t, place], s.three_send.at[r, k - 1],
            s.three_recv.at[r, place], (self.b ^ k, self.t),
        )

    def back_tensor(self, k, slot, place):
        r, s = self.r, self.s
        view = s.full.at[r, slot, place]
        return remote(view, view, s.four_send.at[r, k - 1, place], s.four_recv.at[r, slot, place], (self.b, self.t ^ k))

    def pass_piece(self, place):
        for k in (2, 3, 1):
            self.back_tensor(k, self.t, place).start()

    def step_one(self, half):
        group = COLUMNS // self.parts
        for slot in range(self.parts):
            at = slot * group + half * (group // 2)
            self.s.out[self.r, at : at + group // 2] = self.pack[at : at + group // 2].astype(BF16)
        for k in (2, 3, 1):
            self.across_tensor(half, k).start()

    def step_two(self):
        r, s = self.r, self.s
        group = COLUMNS // self.parts
        total = self.pack[pl.ds(self.t * group, group)]
        for k in range(1, self.parts):
            for half in range(2):
                self.from_tensor(half, k).wait_recv()
            total += s.one[r, self.t ^ k].astype(F32)
        total = total.reshape(RING, total.shape[0] * total.shape[1] // RING, 128)
        s.mid[r] = total
        s.mid_out[r] = total.astype(BF16)
        for k in range(1, RING):
            self.across_batch(k).start()

    def step_three(self):
        r, s = self.r, self.s
        total = s.mid[r, self.place]
        for k in range(1, RING):
            self.from_batch(k).wait_recv()
            total += s.two[r, self.place ^ k].astype(F32)
        if self.outer > 1:
            s.far[r, self.b // RING] = total.astype(BF16)
            for k in range(1, self.outer):
                self.across_outer(k).start()
            for k in range(1, self.outer):
                self.from_outer(k).wait_recv()
            total = s.far[r, 0].astype(F32)
            for other in range(1, self.outer):
                total += s.far[r, other].astype(F32)
            for k in range(1, self.outer):
                self.across_outer(k).wait_send()
        s.full[r, self.t, self.place] = total.astype(BF16)
        for k in range(1, RING):
            self.back_batch(k, self.place).start()
        self.pass_piece(self.place)

    def step_four(self):
        for k in range(1, RING):
            self.back_batch(k, self.place ^ k).wait_recv()
            self.pass_piece(self.place ^ k)

    def step_five(self):
        for k in range(1, self.parts):
            for place in range(RING):
                self.back_tensor(k, self.t ^ k, place).wait_recv()
        for k in range(1, self.parts):
            for half in range(2):
                self.across_tensor(half, k).wait_send()
            for place in range(RING):
                self.back_tensor(k, self.t, place).wait_send()
        for k in range(1, RING):
            self.across_batch(k).wait_send()
            self.back_batch(k, self.place).wait_send()


def finish_kernel(parts, frozen, state, grad, full, *refs):
    outs = Refs(**dict(zip(("frozen", "state", "grad", *OUTS), refs)))
    outs.frozen[...] = frozen[...]
    outs.state[...] = state[...].T[0:96]
    outs.grad[...] = grad[...].T[0:96]
    per = COLUMNS // parts
    for layer in range(LAYERS):

        def column(index):
            at = place_of(index)
            both = full[layer, at // per, 2 * (at % per) : 2 * (at % per) + 2]
            return both.astype(F32).reshape(96, 128)

        for k in range(6):
            outs.down[layer, :, 128 * k : 128 * k + 128] = column(k)
        for k in range(3):
            outs.expand[layer, :, 128 * k : 128 * k + 128] = column(6 + k)
            outs.reduce[layer, :, 128 * k : 128 * k + 128] = column(9 + k)
        outs.project[layer, :, 0:128] = column(12)
        outs.project[layer, :, 128:256] = column(13)
        last = column(14)
        outs.project[layer, :, 256:288] = last[:, 0:32]
        outs.mixing[layer] = pltpu.roll(last, 96, 1)[:, 0:96]
        small = column(15)
        outs.gate[layer : layer + 1, :] = small[0:1, 0:96]
        outs.gains[layer] = small[1:3, 0:96]


RAW = ("gate", "gains", "down", "project", "mixing", "expand", "reduce")
WEIGHTS = RAW[2:]
KEEP = ("lifted", "mixed", "query", "sums", "heads", "middle")


def keep_shapes(tokens):
    return (
        ((tokens, 128), F32),
        ((tokens, 128), F32),
        ((tokens, 128), BF16),
        ((16, tokens), F32),
        ((96, tokens), F32),
        ((tokens, 128), F32),
    )


def weight_scratch(model, units):
    return [
        pltpu.VMEM((128, model), BF16),
        pltpu.VMEM((128, 384), BF16),
        pltpu.VMEM((128, 128), BF16),
        pltpu.VMEM((128, units), BF16),
        pltpu.VMEM((128, units), BF16),
    ]


def tensor_barrier(b, t, parts):
    barrier = pltpu.get_barrier_semaphore()
    for k in range(1, parts):
        pl.semaphore_signal(barrier, inc=1, device_id=(b, t ^ k), device_id_type=MESH)
    return barrier


def vmem_specs(count):
    return [pl.BlockSpec(memory_space=pltpu.VMEM)] * count


OUTS = ("down", "gate", "gains", "project", "mixing", "expand", "reduce")
SUMS = (
    *("out", "one", "mid", "mid_out", "two", "far"),
    *("one_send", "one_recv", "two_send", "two_recv", "far_send", "far_recv"),
    *("three_send", "three_recv", "four_send", "four_recv"),
)
LOCAL = (
    *("k_s", "vt_s", "scores", "kv_send", "kv_recv", "do_s", "dot_s", "q_s", "qt_s", "v_s", "kt_s"),
    *("active", "slope"),
    *("terms", "terms_in", "dqkv", "terms_send", "terms_recv"),
)


def side_rest_kernel(parts, batch, *refs):
    refs = list(refs)

    def pop(count):
        taken, refs[:count] = refs[:count], []
        return taken

    second_f, side_in, cotangent, ids_ref = pop(4)
    raw = Refs(**dict(zip(RAW, pop(7))))
    state_one, *handed = pop(9)
    side_out, grad, full = pop(3)
    local = pop(8)
    first_f, kvt_zero = local[0:2]
    keep_zero = Refs(**dict(zip(KEEP, local[2:])))
    hand_sem = pop(1)[0]
    hand = [pltpu.make_async_copy(*pair, hand_sem.at[k]) for k, pair in enumerate(zip(handed, local))]
    for copy in hand:
        copy.start()
    kvt_one, prev, pack, raw.vectors = pop(4)
    keep_one = Refs(**dict(zip(KEEP, pop(6))))
    w_one = Refs(**dict(zip(WEIGHTS, pop(5))))
    w_zero = Refs(**dict(zip(WEIGHTS, pop(5))))
    c = Refs(**dict(zip(LOCAL, pop(len(LOCAL)))))
    s = Refs(**dict(zip(SUMS, pop(len(SUMS)))))
    s.full = full
    b = lax.axis_index("batch")
    t = lax.axis_index("tensor")
    barrier = tensor_barrier(b, t, parts)
    for k in range(1, RING):
        pl.semaphore_signal(barrier, inc=1, device_id=(b ^ k, t), device_id_type=MESH)
    outer = batch // RING
    for k in range(1, outer):
        other = lax.rem(b // RING + k, outer) * RING + lax.rem(b, RING)
        pl.semaphore_signal(barrier, inc=1, device_id=(other, t), device_id_type=MESH)
    load_vectors(raw.vectors, raw)
    load_side_weights(1, w_one, raw)
    load_side_weights(0, w_zero, raw)
    grad[...] = widened(cotangent)
    prev[...] = widened(side_in)
    pl.semaphore_wait(barrier, parts - 1 + RING - 1 + outer - 1)

    def prepare_lower():
        for copy in hand:
            copy.wait()
        side_prepare(0, parts, w_zero, raw, c, keep_zero, kvt_zero, ids_ref, True)

    first = Refs(
        kvt=kvt_one, k_s=c.k_s.at[1], vt_s=c.vt_s, scores=c.scores, kv_send=c.kv_send, kv_recv=c.kv_recv
    )
    side_forward(
        1, b, t, parts, second_f, state_one, w_one, raw, first, keep_one, ids_ref, side_out,
        lambda: None, prepare_lower, lambda index: None,
    )
    side_prepare(1, parts, w_one, raw, c, keep_one, kvt_one, ids_ref, False)
    upper = Sum(1, b, t, parts, batch, pack.at[1], s)
    lower = Sum(0, b, t, parts, batch, pack.at[0], s)
    side_backward(
        1, b, t, parts, second_f, state_one, w_one, raw, c, keep_one, grad, pack.at[1],
        lambda index: None, lambda: upper.step_one(0),
    )
    upper.step_one(1)

    def between(index):
        pl.when(index == 2)(upper.step_two)
        pl.when(index == 4)(upper.step_three)
        pl.when(index == 5)(upper.step_four)

    side_backward(
        0, b, t, parts, first_f, prev, w_zero, raw, c, keep_zero, grad, pack.at[0],
        between, lambda: lower.step_one(0),
    )
    lower.step_one(1)
    upper.step_five()
    lower.step_two()
    lower.step_three()
    lower.step_four()
    lower.step_five()


def side_rest_call(first_f, second_f, side_in, cotangent, ids_all, raw, state_one, kvt_zero, keep_zero, parts, batch):
    tokens, model = first_f.shape
    length = parts * tokens
    units = raw[5].shape[2]
    dma = pltpu.SemaphoreType.DMA
    vmem = pltpu.VMEM
    pairs = SIDE_HEADS // 2
    group = COLUMNS // parts
    piece = group * 96 // RING
    outs = (
        ((tokens, 128), F32),
        ((tokens, 128), F32),
        ((LAYERS, parts, RING, piece, 128), BF16),
    )
    outer = max(batch // RING, 1)
    return pl.pallas_call(
        functools.partial(side_rest_kernel, parts, batch),
        out_shape=tuple(jax.ShapeDtypeStruct(*o) for o in outs),
        in_specs=vmem_specs(12) + [pl.BlockSpec(memory_space=pl.ANY)] * 8,
        out_specs=tuple(vmem_specs(len(outs))),
        scratch_shapes=[
            vmem((tokens, model), BF16),
            vmem((parts, 192, tokens), BF16),
            *[vmem(*shape) for shape in keep_shapes(tokens)],
            dma((8,)),
            vmem((parts, 192, tokens), BF16),
            vmem((tokens, 128), F32),
            vmem((LAYERS, COLUMNS, 96, 128), F32),
            vmem((LAYERS, 8, 128), F32),
            *[vmem(*shape) for shape in keep_shapes(tokens)],
            *weight_scratch(model, units),
            *weight_scratch(model, units),
            vmem((LAYERS, length, 256), BF16),
            vmem((SIDE_HEADS, 16, length), BF16),
            vmem((2, length, tokens), F32),
            dma((3,)),
            dma((parts,)),
            vmem((tokens, 128), BF16),
            vmem((SIDE_HEADS, 16, tokens), BF16),
            vmem((LAYERS, tokens, 256), BF16),
            vmem((LAYERS, SIDE_HEADS, 16, tokens), BF16),
            vmem((LAYERS, length, 128), BF16),
            vmem((LAYERS, SIDE_HEADS, 16, length), BF16),
            vmem((LAYERS, tokens, units), BF16),
            vmem((LAYERS, tokens, units), F32),
            vmem((pairs, parts, 32, tokens), BF16),
            vmem((LAYERS, pairs, parts, 32, tokens), BF16),
            vmem((384, tokens), BF16),
            dma((LAYERS, pairs, parts - 1)),
            dma((LAYERS, pairs, parts)),
            vmem((LAYERS, COLUMNS, 96, 128), BF16),
            vmem((LAYERS, parts, group, 96, 128), BF16),
            vmem((LAYERS, RING, piece, 128), F32),
            vmem((LAYERS, RING, piece, 128), BF16),
            vmem((LAYERS, RING, piece, 128), BF16),
            vmem((LAYERS, outer, piece, 128), BF16),
            dma((LAYERS, 2, parts - 1)),
            dma((LAYERS, 2, parts)),
            dma((LAYERS, RING - 1)),
            dma((LAYERS, RING)),
            dma((LAYERS, max(outer - 1, 1))),
            dma((LAYERS, outer)),
            dma((LAYERS, RING - 1)),
            dma((LAYERS, RING)),
            dma((LAYERS, parts - 1, RING)),
            dma((LAYERS, parts, RING)),
        ],
        compiler_params=pltpu.CompilerParams(
            collective_id=5, has_side_effects=True, vmem_limit_bytes=62 << 20
        ),
    )(second_f, side_in, cotangent, ids_all, *raw, state_one, first_f, kvt_zero, *keep_zero)


def finish_call(frozen, state, grad, full, side, parts):
    tokens, model = frozen.shape
    units = 4 * side
    outs = (
        ((tokens, model), BF16),
        ((side, tokens), F32),
        ((side, tokens), F32),
        ((LAYERS, side, model), F32),
        ((LAYERS, side), F32),
        ((LAYERS, 2, side), F32),
        ((LAYERS, side, 3 * side), F32),
        ((LAYERS, side, side), F32),
        ((LAYERS, side, units), F32),
        ((LAYERS, side, units), F32),
    )
    frozen, state, grad, down, *others, reduce_grad = pl.pallas_call(
        functools.partial(finish_kernel, parts),
        out_shape=tuple(jax.ShapeDtypeStruct(*o) for o in outs),
        in_specs=vmem_specs(4),
        out_specs=tuple(vmem_specs(len(outs))),
        compiler_params=pltpu.CompilerParams(vmem_limit_bytes=62 << 20),
    )(frozen, state, grad, full)
    turn = (0, 2, 1)
    return (frozen, state.T, grad.T, down.transpose(turn), *others, reduce_grad.transpose(turn))


def per_device(
    hidden_rows,
    side_input,
    segment_ids,
    side_cotangent,
    backbone_gains,
    backbone_project,
    backbone_mixing,
    backbone_expand,
    backbone_reduce,
    side_down,
    side_gate,
    side_gains,
    side_project,
    side_mixing,
    side_expand,
    side_reduce,
):
    parts = lax.axis_size("tensor")
    batch = lax.axis_size("batch")
    side = side_input.shape[1]
    turn = (0, 2, 1)
    qkv = backbone_project.transpose(0, 2, 3, 1)
    raw = (
        side_gate,
        side_gains,
        side_down.transpose(turn),
        side_project,
        side_mixing,
        side_expand,
        side_reduce.transpose(turn),
    )
    side_turned, cotangent_turned = side_input.T, side_cotangent.T
    ids_row = segment_ids.reshape(1, -1)

    second_f, first_f, ids_all, state_one, kvt_zero, *keep_zero = front_call(
        hidden_rows,
        ids_row,
        backbone_gains,
        qkv,
        backbone_mixing,
        backbone_expand,
        backbone_reduce,
        side_turned,
        raw,
        parts,
    )
    state, grad, full = side_rest_call(
        first_f, second_f, side_turned, cotangent_turned, ids_all, raw, state_one, kvt_zero, keep_zero, parts, batch
    )
    return finish_call(second_f, state, grad, full, side, parts)


def solution(mesh):
    return jax.shard_map(
        per_device,
        mesh=mesh,
        in_specs=(
            P(("batch", "tensor"), None),
            P(("batch", "tensor"), None),
            P(("batch", "tensor")),
            P(("batch", "tensor"), None),
            P(),
            P(None, None, None, "tensor"),
            P(None, "tensor", None),
            P(None, None, "tensor"),
            P(None, "tensor", None),
            P(),
            P(),
            P(),
            P(),
            P(),
            P(),
            P(),
        ),
        out_specs=(
            P(("batch", "tensor"), None),
            P(("batch", "tensor"), None),
            P(("batch", "tensor"), None),
            P(),
            P(),
            P(),
            P(),
            P(),
            P(),
            P(),
        ),
        check_vma=False,
    )
```

```python
import functools
import jax
import jax.numpy as jnp
from jax import lax
from jax.experimental import pallas as pl
from jax.experimental.pallas import tpu as pltpu
from jax.sharding import PartitionSpec as P

HEAD_DIM = 64
SIDE_HEADS = 12
SIDE_HEAD_DIM = 8
LAYERS = 2
EPS = 1e-06
BIG = 2.0**100
LOG2E = 1.4426950408889634
ID_BITS = 11
QUAD = 4
MESH = pl.DeviceIdType.MESH
F32 = jnp.float32
BF16 = jnp.bfloat16


def contract(left, right, dims):
    return lax.dot_general(left, right, ((dims[:1], dims[1:]), ((), ())), preferred_element_type=F32)


def nn(left, right):
    return contract(left, right, (1, 0))


def nt(left, right):
    return contract(left, right, (1, 1))


def tn(left, right):
    return contract(left, right, (0, 0))


def lanes_of(rows, lanes):
    return lax.broadcasted_iota(jnp.int32, (rows, lanes), 1)


def segment_lanes(id_row, offset):
    width = id_row.shape[1]
    place = lax.broadcasted_iota(jnp.int32, (128, width), 0) - offset
    flipped = place >= ID_BITS
    shift = jnp.clip(jnp.where(flipped, place - ID_BITS, place), 0, ID_BITS)
    bit = lax.shift_right_logical(jnp.broadcast_to(id_row, (128, width)), shift) & 1
    bit = jnp.where(flipped, 1 - bit, bit)
    used = (place >= 0) & (place < 2 * ID_BITS)
    keys = jnp.where(used, bit, 0).astype(F32)
    queries = jnp.where(used, (bit - 1).astype(F32) * BIG, 0.0)
    return keys.T, queries.T


def root_norm(values, gain):
    return values * lax.rsqrt(jnp.mean(values * values, axis=-1, keepdims=True) + EPS) * gain


class Refs:
    def __init__(self, **refs):
        self.__dict__.update(refs)


def remote(src, dst, send, recv, target):
    return pltpu.make_async_remote_copy(
        src_ref=src, dst_ref=dst, send_sem=send, recv_sem=recv, device_id=target, device_id_type=MESH
    )


class Weights:
    def __init__(self, layer, b, t, c):
        self.layer, self.b, self.t, self.c = layer, b, t, c
        self.part = lax.rem(b, QUAD)
        self.fulls = (c.mix_w, c.exp_w, c.red_w)
        self.sources = (c.mix_hbm, c.exp_hbm, c.red_hbm)
        self.slices = tuple(w.shape[2] // QUAD for w in self.fulls)
        mix, up, down = self.slices
        self.pieces = (
            (0, 0, mix),
            (1, 0, up // 2),
            (1, up // 2, up // 2),
            (2, 0, down // 2),
            (2, down // 2, down // 2),
        )

    def rows(self, p, part):
        w, low, size = self.pieces[p]
        return pl.ds(pl.multiple_of(part * self.slices[w] + low, 16), size)

    def view(self, p, slot, part):
        return self.fulls[self.pieces[p][0]].at[self.layer, slot, self.rows(p, part)]

    def load(self, w):
        return pltpu.make_async_copy(
            self.sources[w].at[self.layer],
            self.fulls[w].at[self.layer, self.t],
            self.c.load_sem.at[self.layer, w],
        )

    def own(self, w, slot):
        c = self.c
        return remote(
            self.sources[w].at[self.layer],
            self.fulls[w].at[self.layer, slot],
            c.own_send.at[self.layer, w],
            c.own_recv.at[self.layer, w],
            (self.b, self.t ^ 1),
        )

    def cross(self, p):
        c = self.c
        return remote(
            self.sources[self.pieces[p][0]].at[self.layer, self.rows(p, self.part)],
            self.view(p, self.t, self.part),
            c.cross_send.at[self.layer, p],
            c.w_recv.at[self.layer, p, self.part],
            (self.b, self.t ^ 2),
        )

    def spread(self, p, k):
        c = self.c
        view = self.view(p, self.t ^ 2, self.part)
        return remote(
            view, view, c.spread_send.at[self.layer, p, k - 1], c.w_recv.at[self.layer, p, self.part], (self.b ^ k, self.t)
        )

    def here(self, p, k):
        c = self.c
        view = self.view(p, self.t ^ 2, self.part ^ k)
        return remote(
            view, view, c.cross_send.at[self.layer, p], c.w_recv.at[self.layer, p, self.part ^ k], (self.b, self.t ^ 2)
        )

    def forward(self, p, k, slot):
        c = self.c
        view = self.view(p, slot, self.part ^ k)
        return remote(
            view,
            view,
            c.pass_send.at[self.layer, p, k],
            c.pass_recv.at[self.layer, p, self.part ^ k],
            (self.b, self.t ^ 1),
        )

    def start_cross(self):
        for p in range(5):
            self.cross(p).start()

    def start_spread(self, p):
        self.here(p, 0).wait_recv()
        for k in range(1, QUAD):
            self.spread(p, k).start()

    def start_forward(self, p):
        for k in range(1, QUAD):
            self.here(p, k).wait_recv()
        for k in range(QUAD):
            self.forward(p, k, self.t ^ 2).start()

    def wait_far(self, p):
        for k in range(QUAD):
            self.forward(p, k, self.t ^ 3).wait_recv()

    def wait_sent(self):
        for w in range(3):
            self.own(w, self.t).wait_send()
        for p in range(5):
            self.cross(p).wait_send()
            for k in range(1, QUAD):
                self.spread(p, k).wait_send()
            for k in range(QUAD):
                self.forward(p, k, self.t ^ 2).wait_send()


class Backbone:
    def __init__(self, layer, b, t, parts, c):
        self.layer, self.b, self.t, self.parts, self.c = layer, b, t, parts, c
        self.sib, self.across, self.far = t ^ 1, t ^ 2, t ^ 3
        self.tokens = c.rows_all.shape[1]
        self.half = self.tokens // 2
        self.width = c.mix_w.shape[2]
        self.heads = self.width // HEAD_DIM
        self.weights = Weights(layer, b, t, c)

    def row_copy(self, slot, chunk, send, target):
        c = self.c
        view = c.rows_all.at[slot, pl.ds(chunk * self.half, self.half)]
        return remote(
            view,
            view,
            c.row_send.at[self.layer, send, chunk],
            c.row_recv.at[self.layer, slot, chunk],
            (self.b, target),
        )

    def norm_rows(self, stream):
        c = self.c
        gain = c.gains[self.layer, 0:1, :].astype(F32)
        c.rows_all[self.t] = root_norm(stream, gain).astype(BF16)

    def send_rows(self):
        for chunk in range(2):
            self.row_copy(self.t, chunk, 1, self.across).start()
        for chunk in range(2):
            self.row_copy(self.t, chunk, 0, self.sib).start()

    def project(self, slot, chunk):
        c, width, half = self.c, self.width, self.half
        inside = pl.ds(pl.multiple_of(chunk * half, half), half)
        rows = c.rows_all[slot, inside, :]
        at = pl.ds(pl.multiple_of(slot * self.tokens + chunk * half, half), half)
        lane = lanes_of(half, 128)
        query = nt(rows, c.qkv_w[self.layer, 0]) * (HEAD_DIM**-0.5 * LOG2E)
        keys = nt(rows, c.qkv_w[self.layer, 1])
        bits = segment_lanes(c.ids_all[slot, 0:1, inside], HEAD_DIM)
        for target, columns, high in ((c.k_s, keys, bits[0]), (c.q_s, query, bits[1])):
            low = pltpu.roll(high, HEAD_DIM, 1)
            for h in range(self.heads):
                own = columns[:, h // 2 * 128 : h // 2 * 128 + 128]
                inner = jnp.where(lane < HEAD_DIM, own, high) if h % 2 == 0 else jnp.where(lane < HEAD_DIM, low, own)
                target[h, at] = inner.astype(BF16)
        values = nt(c.qkv_w[self.layer, 2, 0:width], rows)
        for h in range(self.heads):
            c.vt_s[h, 0:HEAD_DIM, at] = values[h * HEAD_DIM : (h + 1) * HEAD_DIM].astype(BF16)
            c.vt_s[h, HEAD_DIM:, at] = jnp.ones((16, half), BF16)

    def project_all(self, first, last, hook):
        def step(index, carry):
            for chunk in range(2):

                @pl.when(index == 2 + chunk)
                def _():
                    self.row_copy(self.sib, chunk, 0, self.sib).wait_recv()

                @pl.when(index == 4 + 2 * chunk)
                def _():
                    self.row_copy(self.across, chunk, 0, self.sib).wait_recv()
                    self.row_copy(self.across, chunk, 2, self.sib).start()

                @pl.when(index == 5 + 2 * chunk)
                def _():
                    self.row_copy(self.far, chunk, 0, self.sib).wait_recv()

            hook(index)
            early = index < 4
            k = jnp.where(early, index // 2, 2 + index % 2)
            chunk = jnp.where(early, index % 2, index // 2 - 2)
            self.project(self.t ^ k, chunk)
            return carry

        lax.fori_loop(first, last, step, 0)

    def wait_rows(self):
        for chunk in range(2):
            self.row_copy(self.t, chunk, 0, self.sib).wait_send()
            self.row_copy(self.t, chunk, 1, self.across).wait_send()
            self.row_copy(self.across, chunk, 2, self.sib).wait_send()

    def block_of(self, item):
        return self.t ^ (self.parts - 1 - item // self.heads)

    def make_scores(self, item, place):
        c = self.c
        h = lax.rem(item, self.heads)
        at = pl.ds(pl.multiple_of(self.block_of(item) * self.tokens, self.tokens), self.tokens)
        c.scores[place] = nt(c.k_s[h], c.q_s[h, at])

    def send_heads(self, block):
        c = self.c
        return remote(
            c.heads_buf.at[block],
            c.heads_buf.at[self.parts + self.t],
            c.head_send.at[self.layer, block],
            c.head_recv.at[self.layer, self.t],
            (self.b, block),
        )

    def attend(self, item, place):
        c = self.c
        block = self.block_of(item)
        h = lax.rem(item, self.heads)
        values = c.scores[place]
        weights = jnp.exp2(values - jnp.max(values, axis=0, keepdims=True)).astype(BF16)
        out = nn(c.vt_s[h], weights)
        slot = jnp.where(block == self.t, self.parts + self.t, block)
        c.heads_buf[slot, pl.ds(pl.multiple_of(h * HEAD_DIM, HEAD_DIM), HEAD_DIM), :] = (
            out[0:HEAD_DIM] * (1.0 / out[HEAD_DIM : HEAD_DIM + 1])
        ).astype(BF16)

        @pl.when((h == self.heads - 1) & (item < (self.parts - 1) * self.heads))
        def _():
            self.send_heads(block).start()

    def attention(self, hook):
        count = self.parts * self.heads
        self.make_scores(0, 0)

        def pair(index, carry):
            item = 2 * index
            hook(index)
            self.make_scores(item + 1, 1)
            self.attend(item, 0)
            self.make_scores(jnp.minimum(item + 2, count - 1), 0)
            self.attend(item + 1, 1)
            return carry

        lax.fori_loop(0, count // 2, pair, 0)

    def wait_heads(self):
        c = self.c
        for k in range(1, self.parts):
            self.send_heads(self.t ^ k).wait_send()
            remote(
                c.heads_buf.at[0],
                c.heads_buf.at[self.parts + (self.t ^ k)],
                c.head_send.at[self.layer, 0],
                c.head_recv.at[self.layer, self.t ^ k],
                (self.b, self.sib),
            ).wait_recv()

    def feed_forward(self, stream, hook):
        c, parts, layer = self.c, self.parts, self.layer
        attended = c.heads_buf[parts : 2 * parts].reshape(parts * self.width, self.tokens)
        stream = stream + tn(attended, c.mix_w[layer].reshape(parts * self.width, -1))
        c.acc[...] = stream
        c.normed[...] = root_norm(stream, c.gains[layer, 1:2, :].astype(F32)).astype(BF16)

        def feed(index, carry):
            hook(index)
            hidden = jax.nn.gelu(nn(c.normed[...], c.exp_w[layer, self.t ^ index])).astype(BF16)
            c.acc[...] += nn(hidden, c.red_w[layer, self.t ^ index])
            return carry

        lax.fori_loop(0, parts, feed, 0)


FRONT_SCRATCH = (
    *("vectors", "rows_all", "ids_scratch", "qkv_w", "mix_w", "exp_w", "red_w", "q_s", "k_s", "vt_s", "scores"),
    *("heads_buf", "acc", "normed", "load_sem", "qkv_sem", "row_send", "row_recv", "id_send", "id_recv"),
    *("head_send", "head_recv", "cross_send", "spread_send", "pass_send", "own_send", "w_recv", "pass_recv"),
    *("own_recv", "side_k", "side_vt", "kv_send", "kv_recv"),
)


def front_kernel(parts, *refs):
    refs = list(refs)

    def pop(count):
        taken, refs[:count] = refs[:count], []
        return taken

    x_ref, ids_ref, gains, qkv_hbm, mix_hbm, exp_hbm, red_hbm, side_in = pop(8)
    raw = Refs(**dict(zip(RAW, pop(7))))
    second_f, *handed = pop(11)
    local = pop(10)
    first_f, ids_all, state_one, kvt = local[0:4]
    keep = Refs(**dict(zip(KEEP, local[4:])))
    hand_sem = pop(1)[0]
    hand = [pltpu.make_async_copy(*pair, hand_sem.at[k]) for k, pair in enumerate(zip(local, handed))]
    prev = pop(1)[0]
    w = Refs(**dict(zip(WEIGHTS, pop(5))))
    c = Refs(**dict(zip(FRONT_SCRATCH, pop(len(FRONT_SCRATCH)))))
    c.gains, c.mix_hbm, c.exp_hbm, c.red_hbm, c.ids_all = gains, mix_hbm, exp_hbm, red_hbm, ids_all
    b = lax.axis_index("batch")
    t = lax.axis_index("tensor")
    tokens = x_ref.shape[0]
    width = c.mix_w.shape[2]
    lower, upper = Backbone(0, b, t, parts, c), Backbone(1, b, t, parts, c)
    load_qkv = [
        pltpu.make_async_copy(
            qkv_hbm.at[layer, k], c.qkv_w.at[layer, k, pl.ds(0, width)], c.qkv_sem.at[layer, k]
        )
        for layer in range(LAYERS)
        for k in range(3)
    ]
    for copy in load_qkv:
        copy.start()
    for layer in (lower, upper):
        for k in range(3):
            layer.weights.load(k).start()
    barrier = tensor_barrier(b, t, parts)
    for k in range(1, QUAD):
        pl.semaphore_signal(barrier, inc=1, device_id=(b ^ k, t), device_id_type=MESH)
    lower.norm_rows(x_ref[...].astype(F32))
    ids_all[t] = jnp.broadcast_to(ids_ref[...], (8, tokens))
    pl.semaphore_wait(barrier, parts - 1 + QUAD - 1)

    def id_copy(slot, k):
        return remote(ids_all.at[slot], ids_all.at[slot], c.id_send.at[k - 1], c.id_recv.at[slot], (b, t ^ k))

    for k in range(1, parts):
        id_copy(t, k).start()
    lower.weights.cross(1).start()
    lower.send_rows()
    for k in range(3):
        lower.weights.own(k, t).start()
    c.qkv_w[:, :, width:, :] = jnp.zeros((LAYERS, 3, 256 - width, x_ref.shape[1]), BF16)
    for copy in load_qkv:
        copy.wait()
    load_side_weights(0, w, raw)
    load_vectors(c.vectors, raw)
    raw.vectors = c.vectors
    prev[...] = widened(side_in)
    for k in range(1, parts):
        id_copy(t, k).wait_send()
        id_copy(t ^ k, k).wait_recv()

    def when(index, at, act, *args):
        @pl.when(index == at)
        def _():
            act(*args)

    def lower_project(index):
        when(index, 4, lower.weights.start_spread, 1)
        for p in (0, 2, 3, 4):
            when(index, 6, lambda p: lower.weights.cross(p).start(), p)

    def lower_attention(index):
        for at, p in ((1, 0), (2, 2), (3, 3), (5, 4)):
            when(index, at, lower.weights.start_spread, p)
        for at, p in ((4, 1), (5, 0)):
            when(index, at, lower.weights.start_forward, p)

    def feed_hook(layer):
        def hook(index):
            weights = layer.weights

            @pl.when(index == 0)
            def _():
                for k in (1, 2):
                    weights.load(k).wait()
                if layer is lower:
                    weights.start_forward(2)

            @pl.when(index == 1)
            def _():
                for k in (1, 2):
                    weights.own(k, layer.sib).wait_recv()
                if layer is lower:
                    weights.start_forward(3)

            @pl.when(index == 2)
            def _():
                if layer is lower:
                    weights.start_forward(4)

            @pl.when(index == 3)
            def _():
                for p in range(1, 5):
                    weights.wait_far(p)

        return hook

    lower.project_all(0, 2 * parts, lower_project)
    lower.wait_rows()
    lower.attention(lower_attention)
    upper.weights.start_cross()
    for k in range(3):
        upper.weights.own(k, t).start()
    lower.weights.load(0).wait()
    lower.weights.own(0, lower.sib).wait_recv()
    lower.weights.wait_far(0)
    lower.wait_heads()
    lower.feed_forward(x_ref[...].astype(F32), feed_hook(lower))
    first_f[...] = c.acc[...].astype(BF16)

    side = Refs(
        kvt=kvt, k_s=c.side_k, vt_s=c.side_vt, scores=c.scores, kv_send=c.kv_send, kv_recv=c.kv_recv
    )

    def send_upper():
        upper.norm_rows(c.acc[...])
        upper.send_rows()

    def side_hook(index):
        for p in range(5):
            when(index, p, upper.weights.start_spread, p)

    side_forward(
        0, b, t, parts, first_f, prev, w, raw, side, keep, ids_all, state_one,
        send_upper, lambda: upper.project_all(0, parts, lambda index: None), side_hook,
    )

    for copy in hand:
        copy.start()

    def upper_attention(index):
        for p in range(5):
            when(index, p + 1, upper.weights.start_forward, p)

    upper.project_all(parts, 2 * parts, lambda index: None)
    upper.wait_rows()
    upper.attention(upper_attention)
    upper.weights.load(0).wait()
    upper.weights.own(0, upper.sib).wait_recv()
    upper.weights.wait_far(0)
    upper.wait_heads()
    upper.feed_forward(c.acc[...], feed_hook(upper))
    second_f[...] = c.acc[...].astype(BF16)
    for copy in hand:
        copy.wait()
    lower.weights.wait_sent()
    upper.weights.wait_sent()


def front_call(x, ids, gains, qkv, mix, exp, red, side_in, raw, parts):
    tokens, model = x.shape
    width = mix.shape[1]
    units = exp.shape[2]
    heads = width // HEAD_DIM
    length = parts * tokens
    side_units = raw[5].shape[2]
    anywhere = pl.BlockSpec(memory_space=pl.ANY)
    dma = pltpu.SemaphoreType.DMA
    vmem = pltpu.VMEM
    outs = (
        ((tokens, model), BF16),
        ((tokens, model), BF16),
        ((parts, 8, tokens), jnp.int32),
        ((tokens, 128), F32),
        ((parts, 192, tokens), BF16),
        *keep_shapes(tokens),
    )
    return pl.pallas_call(
        functools.partial(front_kernel, parts),
        out_shape=tuple(jax.ShapeDtypeStruct(*o) for o in outs),
        in_specs=vmem_specs(3) + [anywhere] * 4 + vmem_specs(8),
        out_specs=(*vmem_specs(1), *[anywhere] * 10),
        scratch_shapes=[
            *[vmem(*out) for out in outs[1:]],
            dma((10,)),
            vmem((tokens, 128), F32),
            *weight_scratch(model, side_units),
            vmem((LAYERS, 8, 128), F32),
            vmem((parts, tokens, model), BF16),
            vmem((8, 128), F32),
            vmem((LAYERS, 3, 256, model), BF16),
            vmem((LAYERS, parts, width, model), BF16),
            vmem((LAYERS, parts, model, units), BF16),
            vmem((LAYERS, parts, units, model), BF16),
            vmem((heads, length, 128), BF16),
            vmem((heads, length, 128), BF16),
            vmem((heads, HEAD_DIM + 16, length), BF16),
            vmem((2, length, tokens), F32),
            vmem((2 * parts, width, tokens), BF16),
            vmem((tokens, model), F32),
            vmem((tokens, model), BF16),
            dma((LAYERS, 3)),
            dma((LAYERS, 3)),
            dma((LAYERS, 3, 2)),
            dma((LAYERS, parts, 2)),
            dma((parts - 1,)),
            dma((parts,)),
            dma((LAYERS, parts)),
            dma((LAYERS, parts)),
            dma((LAYERS, 5)),
            dma((LAYERS, 5, QUAD - 1)),
            dma((LAYERS, 5, QUAD)),
            dma((LAYERS, 3)),
            dma((LAYERS, 5, QUAD)),
            dma((LAYERS, 5, QUAD)),
            dma((LAYERS, 3)),
            vmem((length, 128), BF16),
            vmem((SIDE_HEADS, 16, length), BF16),
            dma((3,)),
            dma((parts,)),
        ],
        compiler_params=pltpu.CompilerParams(
            collective_id=1, has_side_effects=True, vmem_limit_bytes=62 << 20
        ),
    )(x, ids, gains, qkv, mix, exp, red, side_in, *raw)


LN2 = 0.6931471805599453
COLUMNS = 16
EARLY = (6, 7, 8, 9, 10, 11, 12, 13)
LATE = (0, 1, 2, 3, 4, 5, 14, 15)


def place_of(column):
    order, low = (EARLY, 0) if column in EARLY else (LATE, 2)
    index = order.index(column)
    return index // 2 * 4 + low + index % 2


RING = 8


def side_norm(values, width):
    rstd = lax.rsqrt(jnp.sum(values * values, axis=-1, keepdims=True) * (1.0 / width) + EPS)
    return values * rstd, rstd


def gelu_parts(inner):
    root = 0.7978845608028654
    square = inner * inner
    curve = jnp.tanh(root * inner * (1.0 + 0.044715 * square))
    half = 0.5 * (1.0 + curve)
    slope = half + 0.5 * inner * (1.0 - curve * curve) * root * (1.0 + 3 * 0.044715 * square)
    return inner * half, slope


def load_side_weights(layer, w, raw):
    side = raw.mixing.shape[1]
    w.down[side:, :] = jnp.zeros_like(w.down[side:, :])
    w.down[0:side, :] = raw.down[layer]
    w.project[...] = jnp.zeros_like(w.project)
    w.project[0:side, 0 : 3 * side] = raw.project[layer]
    w.mixing[...] = jnp.zeros_like(w.mixing)
    w.mixing[0:side, 0:side] = raw.mixing[layer]
    w.expand[side:, :] = jnp.zeros_like(w.expand[side:, :])
    w.expand[0:side, :] = raw.expand[layer]
    w.reduce[side:, :] = jnp.zeros_like(w.reduce[side:, :])
    w.reduce[0:side, :] = raw.reduce[layer]


def load_vectors(vectors, raw):
    side = raw.mixing.shape[1]
    vectors[...] = jnp.zeros_like(vectors)
    for layer in range(LAYERS):
        vectors[layer, 0:1, 0:side] = raw.gate[layer : layer + 1, :]
        vectors[layer, 1:3, 0:side] = raw.gains[layer].astype(F32)


def widened(turned):
    values = turned[...].astype(F32)
    return jnp.concatenate([values, jnp.zeros((32, values.shape[1]), F32)], axis=0).T


def kv_copy(c, slot, send, target):
    return remote(c.kvt.at[slot], c.kvt.at[slot], c.kv_send.at[send], c.kv_recv.at[slot], target)


def keys_from(c, slot, ids_ref):
    tokens = c.kvt.shape[2]
    at = pl.ds(pl.multiple_of(slot * tokens, tokens), tokens)
    key_bits, _ = segment_lanes(ids_ref[slot][0:1, :], 96)
    keys = jnp.concatenate([c.kvt[slot, 0:96].astype(F32), jnp.zeros((32, tokens), F32)], axis=0)
    c.k_s[at, 0:128] = (keys.T + key_bits).astype(BF16)


def side_forward(layer, b, t, parts, f_ref, prev, w, raw, c, keep, ids_ref, result, after_send, meanwhile, between):
    side = raw.mixing.shape[1]
    tokens = f_ref.shape[0]
    gate = jax.nn.sigmoid(raw.vectors[layer, 0:1, :])
    lifted = nt(f_ref[...], w.down[...])
    mixed = gate * lifted + (1.0 - gate) * prev[...]
    keep.lifted[...] = lifted
    keep.mixed[...] = mixed
    normed = (side_norm(mixed, side)[0] * raw.vectors[layer, 1:2, :]).astype(BF16)
    turned = w.project[...].astype(F32).T.astype(BF16)
    c.kvt[t] = nt(turned[side : 3 * side], normed).astype(BF16)
    sib, across, far = t ^ 1, t ^ 2, t ^ 3
    kv_copy(c, t, 1, (b, across)).start()
    kv_copy(c, t, 0, (b, sib)).start()
    after_send()
    lane = lanes_of(tokens, 128)
    weight_q = jnp.where(lanes_of(128, 128) < side, w.project[:, 0:128], jnp.zeros((128, 128), BF16))
    query_bits = segment_lanes(ids_ref[t][0:1, :], 96)[1]
    keep.query[...] = (
        nn(normed, weight_q) * (SIDE_HEAD_DIM**-0.5 * LOG2E) + query_bits
    ).astype(BF16)
    keep.sums[...] = jnp.zeros_like(keep.sums)

    def take(index, carry):
        @pl.when(index == 1)
        def _():
            kv_copy(c, sib, 0, (b, sib)).wait_recv()

        @pl.when(index == 2)
        def _():
            meanwhile()
            kv_copy(c, across, 0, (b, sib)).wait_recv()
            kv_copy(c, across, 2, (b, sib)).start()

        @pl.when(index == 3)
        def _():
            kv_copy(c, far, 0, (b, sib)).wait_recv()

        slot = t ^ index
        at = pl.ds(pl.multiple_of(slot * tokens, tokens), tokens)
        keys_from(c, slot, ids_ref)
        values = c.kvt[slot, 96:192].astype(F32)
        for h in range(SIDE_HEADS):
            c.vt_s[h, :, at] = jnp.concatenate(
                [values[8 * h : 8 * h + 8], jnp.ones((8, tokens), F32)], axis=0
            ).astype(BF16)
        return carry

    lax.fori_loop(0, parts, take, 0)

    def make_scores(h, place):
        rows = keep.query[...]
        chosen = (lane // SIDE_HEAD_DIM == h) | (lane >= side)
        c.scores[place] = nt(c.k_s[:, 0:128], jnp.where(chosen, rows, jnp.zeros_like(rows)))

    def attend(h, place):
        values = c.scores[place]
        top = jnp.max(values, axis=0, keepdims=True)
        out = nn(c.vt_s[h], jnp.exp2(values - top).astype(BF16))
        total = out[8:9]
        keep.heads[pl.ds(pl.multiple_of(h * 8, 8), 8), :] = out[0:8] * (1.0 / total)
        here = lax.broadcasted_iota(jnp.int32, keep.sums.shape, 0) == h
        keep.sums[...] = jnp.where(here, top + jnp.log2(total), keep.sums[...])

    make_scores(0, 0)

    def pair(index, carry):
        h = 2 * index
        between(index)
        make_scores(h + 1, 1)
        attend(h, 0)
        make_scores(jnp.minimum(h + 2, SIDE_HEADS - 1), 0)
        attend(h + 1, 1)
        return carry

    lax.fori_loop(0, SIDE_HEADS // 2, pair, 0)
    kv_copy(c, t, 1, (b, across)).wait_send()
    kv_copy(c, t, 0, (b, sib)).wait_send()
    kv_copy(c, across, 2, (b, sib)).wait_send()
    middle = mixed + tn(keep.heads[...].astype(BF16), w.mixing[0:side, :])
    keep.middle[...] = middle
    normed_two = (side_norm(middle, side)[0] * raw.vectors[layer, 2:3, :]).astype(BF16)
    active = jax.nn.gelu(nn(normed_two, w.expand[...])).astype(BF16)
    result[...] = middle + nt(active, w.reduce[...])


def norm_back(values, gain, grad, side):
    hat, rstd = side_norm(values, side)
    gain_grad = jnp.sum(grad * hat, axis=0, keepdims=True)
    pulled = grad * gain
    mean = jnp.sum(pulled * hat, axis=-1, keepdims=True) * (1.0 / side)
    return rstd * (pulled - hat * mean), gain_grad


def pad_heads(target, rows, fill):
    for h in range(SIDE_HEADS):
        target[h] = jnp.concatenate(
            [rows[8 * h : 8 * h + 8], jnp.full((8, rows.shape[1]), fill, F32)], axis=0
        ).astype(BF16)


def side_prepare(layer, parts, w, raw, c, keep, kvt, ids_ref, again):
    side = raw.mixing.shape[1]
    tokens = c.q_s.shape[1]
    lane = lanes_of(tokens, 128)
    normed_two = side_norm(keep.middle[...], side)[0] * raw.vectors[layer, 2:3, :]
    active, slope = gelu_parts(nn(normed_two.astype(BF16), w.expand[...]))
    c.active[layer] = active.astype(BF16)
    c.slope[layer] = slope
    sums = keep.sums[...]
    rows = jnp.concatenate([sums, sums, sums, jnp.zeros((80, tokens), F32)], axis=0).T
    high = rows.astype(BF16).astype(F32)
    mid = (rows - high).astype(BF16).astype(F32)
    low = rows - high - mid
    rows = jnp.where(lane < 16, high, jnp.where(lane < 32, mid, low))
    query = keep.query[...]
    c.q_s[layer, :, 0:128] = query
    c.q_s[layer, :, 128:256] = jnp.where(lane < 48, -rows, 0.0).astype(BF16)
    pad_heads(c.qt_s.at[layer], query.astype(F32).T, 0.0)

    def take(slot, carry):
        at = pl.ds(pl.multiple_of(slot * tokens, tokens), tokens)
        if again:
            keys_from(Refs(kvt=kvt, k_s=c.k_s.at[layer]), slot, ids_ref)
        c.k_s[layer, at, 128:256] = jnp.where(lane < 48, 1.0, 0.0).astype(BF16)
        values = jnp.concatenate([kvt[slot, 96:192].astype(F32), jnp.ones((32, tokens), F32)], axis=0)
        c.v_s[layer, at, :] = values.T.astype(BF16)
        keys = kvt[slot, 0:96].astype(F32)
        for h in range(SIDE_HEADS):
            c.kt_s[layer, h, :, at] = jnp.concatenate(
                [keys[8 * h : 8 * h + 8], jnp.zeros((8, tokens), F32)], axis=0
            ).astype(BF16)
        return carry

    lax.fori_loop(0, parts, take, 0)


def side_backward(layer, b, t, parts, f_ref, prev, w, raw, c, keep, grad_ref, pack, between, early):
    side = raw.mixing.shape[1]
    tokens = f_ref.shape[0]
    gate = jax.nn.sigmoid(raw.vectors[layer, 0:1, :])
    lane = lanes_of(tokens, 128)
    grad = grad_ref[...]
    middle = keep.middle[...]
    gain_two = raw.vectors[layer, 2:3, :]
    normed_two = (side_norm(middle, side)[0] * gain_two).astype(BF16)
    top = grad.astype(BF16)
    reduce_grad = tn(top, c.active[layer])
    grad_inner = (c.slope[layer] * nn(top, w.reduce[...])).astype(BF16)
    expand_grad = tn(normed_two, grad_inner)
    for k in range(3):
        pack[place_of(6 + k)] = expand_grad[0:96, 128 * k : 128 * k + 128]
        pack[place_of(9 + k)] = reduce_grad[0:96, 128 * k : 128 * k + 128]
    through, gain_two_grad = norm_back(middle, gain_two, nt(grad_inner, w.expand[...]), side)
    grad_middle = grad + through
    branch = grad_middle.astype(BF16)
    heads = keep.heads[...]
    mixing_grad = nn(heads.astype(BF16), branch)
    grad_heads = nt(branch, w.mixing[...]).astype(BF16).astype(F32).T
    product = grad_heads[0:96] * heads
    group = lax.broadcasted_iota(jnp.int32, (16, 96), 1) // SIDE_HEAD_DIM
    group = (group == lax.broadcasted_iota(jnp.int32, (16, 96), 0)).astype(BF16)
    high = product.astype(BF16)
    inner = nn(group, high) + nn(group, (product - high.astype(F32)).astype(BF16))
    rows = jnp.concatenate([grad_heads[0:96], -inner, -inner], axis=0).T
    high = rows.astype(BF16)
    c.do_s[...] = jnp.where(lane < 112, high, (rows - high.astype(F32)).astype(BF16))
    pad_heads(c.dot_s, grad_heads, 0.0)
    wide = lanes_of(tokens, 256)
    query_head = jnp.where(wide < 96, wide // SIDE_HEAD_DIM, jnp.where(wide < 128, -1, (wide - 128) % 16))
    out_head = jnp.where(lane < 96, lane // SIDE_HEAD_DIM, (lane - 96) % 16)

    count = parts * tokens // 2

    def one_head(h, keys):
        rows = c.q_s[layer]
        rows = jnp.where((query_head == h) | (query_head < 0), rows, jnp.zeros_like(rows))
        probs = jnp.exp2(nt(rows, c.k_s[layer, keys, :]))
        rows = c.do_s[...]
        rows = jnp.where(out_head == h, rows, jnp.zeros_like(rows))
        scores = (probs * nt(rows, c.v_s[layer, keys, :])).astype(BF16)
        by_keys = nn(c.qt_s[layer, h], scores)[0:8] * LN2
        by_values = nn(c.dot_s[h], probs.astype(BF16))[0:8]
        return by_keys, by_values, nt(c.kt_s[layer, h, :, keys], scores)[0:8] * SIDE_HEAD_DIM**-0.5

    def terms_copy(pair, k):
        return remote(
            c.terms.at[pair, t ^ k],
            c.terms_in.at[layer, pair, t],
            c.terms_send.at[layer, pair, k - 1],
            c.terms_recv.at[layer, pair, t],
            (b, t ^ k),
        )

    def terms_wait(pair, k):
        return remote(
            c.terms.at[pair, t ^ k],
            c.terms_in.at[layer, pair, t ^ k],
            c.terms_send.at[layer, pair, k - 1],
            c.terms_recv.at[layer, pair, t ^ k],
            (b, t ^ k),
        )

    def pair_of(index, carry):
        between(index)
        queries = jnp.zeros((16, tokens), F32)
        for near in range(2):
            chip = t // 2 if near else (t // 2) ^ 1
            keys = pl.ds(pl.multiple_of(chip * count, count), count)
            first, second = one_head(2 * index, keys), one_head(2 * index + 1, keys)
            by_keys, by_values, by_queries = (
                jnp.concatenate([left, right], axis=0) for left, right in zip(first, second)
            )
            queries += by_queries
            for place in range(parts // 2):
                at = slice(place * tokens, (place + 1) * tokens)
                c.terms[index, chip * (parts // 2) + place, 0:16] = by_keys[:, at].astype(BF16)
                c.terms[index, chip * (parts // 2) + place, 16:32] = by_values[:, at].astype(BF16)
            for k in (1,) if near else (2, 3):
                terms_copy(index, k).start()
        c.dqkv[pl.ds(pl.multiple_of(index * 16, 16), 16), :] = queries.astype(BF16)
        return carry

    pairs = SIDE_HEADS // 2
    lax.fori_loop(0, pairs, pair_of, 0)
    mixed = keep.mixed[...]
    gain_one = raw.vectors[layer, 1:2, :]
    normed = side_norm(mixed, side)[0] * gain_one
    c.dqkv[288:384, :] = jnp.zeros((96, tokens), BF16)

    def gather(index, carry):
        total = c.terms[index, t].astype(F32)
        for k in range(1, parts):
            terms_wait(index, k).wait_recv()
            total += c.terms_in[layer, index, t ^ k].astype(F32)
        total = total.astype(BF16)
        c.dqkv[pl.ds(pl.multiple_of(96 + index * 16, 16), 16), :] = total[0:16]
        c.dqkv[pl.ds(pl.multiple_of(192 + index * 16, 16), 16), :] = total[16:32]
        return carry

    lax.fori_loop(0, pairs, gather, 0)
    dqkv = c.dqkv[...]
    project_grad = nt(normed.T.astype(BF16), dqkv)
    pack[place_of(12)] = project_grad[0:96, 0:128]
    pack[place_of(13)] = project_grad[0:96, 128:256]
    pack[place_of(14)] = project_grad[0:96, 256:384] + pltpu.roll(mixing_grad, 32, 1)
    early()
    grad_normed = nn(w.project[...], dqkv).T
    through, gain_one_grad = norm_back(mixed, gain_one, grad_normed, side)
    grad_mixed = grad_middle + through
    down_grad = nn((gate * grad_mixed).T.astype(BF16), f_ref[...])
    for k in range(6):
        pack[place_of(k)] = down_grad[0:96, 128 * k : 128 * k + 128]
    gate_grad = jnp.sum(grad_mixed * (keep.lifted[...] - prev[...]), axis=0, keepdims=True)
    gate_grad = gate_grad * gate * (1.0 - gate)
    row = lax.broadcasted_iota(jnp.int32, (96, 128), 0)
    pack[place_of(15)] = jnp.where(
        row == 0, gate_grad, jnp.where(row == 1, gain_one_grad, jnp.where(row == 2, gain_two_grad, 0.0))
    )
    grad_ref[...] = (1.0 - gate) * grad_mixed

    def sent(index, carry):
        for k in range(1, parts):
            terms_copy(index, k).wait_send()
        return carry

    lax.fori_loop(0, pairs, sent, 0)


class Sum:
    def __init__(self, r, b, t, parts, batch, pack, s):
        self.r, self.b, self.t, self.parts, self.batch, self.pack, self.s = r, b, t, parts, batch, pack, s
        self.place = lax.rem(b, RING)
        self.outer = batch // RING

    def across_tensor(self, half, k):
        r, s, t = self.r, self.s, self.t
        group = COLUMNS // self.parts
        return remote(
            s.out.at[r, pl.ds((t ^ k) * group + half * (group // 2), group // 2)],
            s.one.at[r, t, pl.ds(half * (group // 2), group // 2)],
            s.one_send.at[r, half, k - 1],
            s.one_recv.at[r, half, t],
            (self.b, t ^ k),
        )

    def from_tensor(self, half, k):
        r, s, t = self.r, self.s, self.t
        group = COLUMNS // self.parts
        view = s.one.at[r, t ^ k, pl.ds(half * (group // 2), group // 2)]
        return remote(view, view, s.one_send.at[r, half, k - 1], s.one_recv.at[r, half, t ^ k], (self.b, t ^ k))

    def across_batch(self, k):
        r, s = self.r, self.s
        return remote(
            s.mid_out.at[r, self.place ^ k], s.two.at[r, self.place], s.two_send.at[r, k - 1],
            s.two_recv.at[r, self.place], (self.b ^ k, self.t),
        )

    def from_batch(self, k):
        r, s = self.r, self.s
        return remote(
            s.two.at[r, self.place ^ k], s.two.at[r, self.place ^ k], s.two_send.at[r, k - 1],
            s.two_recv.at[r, self.place ^ k], (self.b ^ k, self.t),
        )

    def across_outer(self, k):
        r, s = self.r, self.s
        mine = self.b // RING
        target = lax.rem(mine + k, self.outer) * RING + self.place
        return remote(
            s.far.at[r, mine], s.far.at[r, mine], s.far_send.at[r, k - 1], s.far_recv.at[r, mine], (target, self.t)
        )

    def from_outer(self, k):
        r, s = self.r, self.s
        other = lax.rem(self.b // RING + k, self.outer)
        return remote(
            s.far.at[r, other], s.far.at[r, other], s.far_send.at[r, k - 1], s.far_recv.at[r, other],
            (self.b ^ 1, self.t),
        )

    def back_batch(self, k, place):
        r, s = self.r, self.s
        return remote(
            s.full.at[r, self.t, place], s.full.at[r, self.t, place], s.three_send.at[r, k - 1],
            s.three_recv.at[r, place], (self.b ^ k, self.t),
        )

    def back_tensor(self, k, slot, place):
        r, s = self.r, self.s
        view = s.full.at[r, slot, place]
        return remote(view, view, s.four_send.at[r, k - 1, place], s.four_recv.at[r, slot, place], (self.b, self.t ^ k))

    def pass_piece(self, place):
        for k in (2, 3, 1):
            self.back_tensor(k, self.t, place).start()

    def step_one(self, half):
        group = COLUMNS // self.parts
        for slot in range(self.parts):
            at = slot * group + half * (group // 2)
            self.s.out[self.r, at : at + group // 2] = self.pack[at : at + group // 2].astype(BF16)
        for k in (2, 3, 1):
            self.across_tensor(half, k).start()

    def step_two(self):
        r, s = self.r, self.s
        group = COLUMNS // self.parts
        total = self.pack[pl.ds(self.t * group, group)]
        for k in range(1, self.parts):
            for half in range(2):
                self.from_tensor(half, k).wait_recv()
            total += s.one[r, self.t ^ k].astype(F32)
        total = total.reshape(RING, total.shape[0] * total.shape[1] // RING, 128)
        s.mid[r] = total
        s.mid_out[r] = total.astype(BF16)
        for k in range(1, RING):
            self.across_batch(k).start()

    def step_three(self):
        r, s = self.r, self.s
        total = s.mid[r, self.place]
        for k in range(1, RING):
            self.from_batch(k).wait_recv()
            total += s.two[r, self.place ^ k].astype(F32)
        if self.outer > 1:
            s.far[r, self.b // RING] = total.astype(BF16)
            for k in range(1, self.outer):
                self.across_outer(k).start()
            for k in range(1, self.outer):
                self.from_outer(k).wait_recv()
            total = s.far[r, 0].astype(F32)
            for other in range(1, self.outer):
                total += s.far[r, other].astype(F32)
            for k in range(1, self.outer):
                self.across_outer(k).wait_send()
        s.full[r, self.t, self.place] = total.astype(BF16)
        for k in range(1, RING):
            self.back_batch(k, self.place).start()
        self.pass_piece(self.place)

    def step_four(self):
        for k in range(1, RING):
            self.back_batch(k, self.place ^ k).wait_recv()
            self.pass_piece(self.place ^ k)

    def step_five(self):
        for k in range(1, self.parts):
            for place in range(RING):
                self.back_tensor(k, self.t ^ k, place).wait_recv()
        for k in range(1, self.parts):
            for half in range(2):
                self.across_tensor(half, k).wait_send()
            for place in range(RING):
                self.back_tensor(k, self.t, place).wait_send()
        for k in range(1, RING):
            self.across_batch(k).wait_send()
            self.back_batch(k, self.place).wait_send()


def finish_kernel(parts, frozen, state, grad, full, *refs):
    outs = Refs(**dict(zip(("frozen", "state", "grad", *OUTS), refs)))
    outs.frozen[...] = frozen[...]
    outs.state[...] = state[...].T[0:96]
    outs.grad[...] = grad[...].T[0:96]
    per = COLUMNS // parts
    for layer in range(LAYERS):

        def column(index):
            at = place_of(index)
            both = full[layer, at // per, 2 * (at % per) : 2 * (at % per) + 2]
            return both.astype(F32).reshape(96, 128)

        for k in range(6):
            outs.down[layer, :, 128 * k : 128 * k + 128] = column(k)
        for k in range(3):
            outs.expand[layer, :, 128 * k : 128 * k + 128] = column(6 + k)
            outs.reduce[layer, :, 128 * k : 128 * k + 128] = column(9 + k)
        outs.project[layer, :, 0:128] = column(12)
        outs.project[layer, :, 128:256] = column(13)
        last = column(14)
        outs.project[layer, :, 256:288] = last[:, 0:32]
        outs.mixing[layer] = pltpu.roll(last, 96, 1)[:, 0:96]
        small = column(15)
        outs.gate[layer : layer + 1, :] = small[0:1, 0:96]
        outs.gains[layer] = small[1:3, 0:96]


RAW = ("gate", "gains", "down", "project", "mixing", "expand", "reduce")
WEIGHTS = RAW[2:]
KEEP = ("lifted", "mixed", "query", "sums", "heads", "middle")


def keep_shapes(tokens):
    return (
        ((tokens, 128), F32),
        ((tokens, 128), F32),
        ((tokens, 128), BF16),
        ((16, tokens), F32),
        ((96, tokens), F32),
        ((tokens, 128), F32),
    )


def weight_scratch(model, units):
    return [
        pltpu.VMEM((128, model), BF16),
        pltpu.VMEM((128, 384), BF16),
        pltpu.VMEM((128, 128), BF16),
        pltpu.VMEM((128, units), BF16),
        pltpu.VMEM((128, units), BF16),
    ]


def tensor_barrier(b, t, parts):
    barrier = pltpu.get_barrier_semaphore()
    for k in range(1, parts):
        pl.semaphore_signal(barrier, inc=1, device_id=(b, t ^ k), device_id_type=MESH)
    return barrier


def vmem_specs(count):
    return [pl.BlockSpec(memory_space=pltpu.VMEM)] * count


OUTS = ("down", "gate", "gains", "project", "mixing", "expand", "reduce")
SUMS = (
    *("out", "one", "mid", "mid_out", "two", "far"),
    *("one_send", "one_recv", "two_send", "two_recv", "far_send", "far_recv"),
    *("three_send", "three_recv", "four_send", "four_recv"),
)
LOCAL = (
    *("k_s", "vt_s", "scores", "kv_send", "kv_recv", "do_s", "dot_s", "q_s", "qt_s", "v_s", "kt_s"),
    *("active", "slope"),
    *("terms", "terms_in", "dqkv", "terms_send", "terms_recv"),
)


def side_rest_kernel(parts, batch, *refs):
    refs = list(refs)

    def pop(count):
        taken, refs[:count] = refs[:count], []
        return taken

    second_f, side_in, cotangent, ids_ref = pop(4)
    raw = Refs(**dict(zip(RAW, pop(7))))
    state_one, *handed = pop(9)
    side_out, grad, full = pop(3)
    local = pop(8)
    first_f, kvt_zero = local[0:2]
    keep_zero = Refs(**dict(zip(KEEP, local[2:])))
    hand_sem = pop(1)[0]
    hand = [pltpu.make_async_copy(*pair, hand_sem.at[k]) for k, pair in enumerate(zip(handed, local))]
    for copy in hand:
        copy.start()
    kvt_one, prev, pack, raw.vectors = pop(4)
    keep_one = Refs(**dict(zip(KEEP, pop(6))))
    w_one = Refs(**dict(zip(WEIGHTS, pop(5))))
    w_zero = Refs(**dict(zip(WEIGHTS, pop(5))))
    c = Refs(**dict(zip(LOCAL, pop(len(LOCAL)))))
    s = Refs(**dict(zip(SUMS, pop(len(SUMS)))))
    s.full = full
    b = lax.axis_index("batch")
    t = lax.axis_index("tensor")
    barrier = tensor_barrier(b, t, parts)
    for k in range(1, RING):
        pl.semaphore_signal(barrier, inc=1, device_id=(b ^ k, t), device_id_type=MESH)
    outer = batch // RING
    for k in range(1, outer):
        other = lax.rem(b // RING + k, outer) * RING + lax.rem(b, RING)
        pl.semaphore_signal(barrier, inc=1, device_id=(other, t), device_id_type=MESH)
    load_vectors(raw.vectors, raw)
    load_side_weights(1, w_one, raw)
    load_side_weights(0, w_zero, raw)
    grad[...] = widened(cotangent)
    prev[...] = widened(side_in)
    pl.semaphore_wait(barrier, parts - 1 + RING - 1 + outer - 1)

    def prepare_lower():
        for copy in hand:
            copy.wait()
        side_prepare(0, parts, w_zero, raw, c, keep_zero, kvt_zero, ids_ref, True)

    first = Refs(
        kvt=kvt_one, k_s=c.k_s.at[1], vt_s=c.vt_s, scores=c.scores, kv_send=c.kv_send, kv_recv=c.kv_recv
    )
    side_forward(
        1, b, t, parts, second_f, state_one, w_one, raw, first, keep_one, ids_ref, side_out,
        lambda: None, prepare_lower, lambda index: None,
    )
    side_prepare(1, parts, w_one, raw, c, keep_one, kvt_one, ids_ref, False)
    upper = Sum(1, b, t, parts, batch, pack.at[1], s)
    lower = Sum(0, b, t, parts, batch, pack.at[0], s)
    side_backward(
        1, b, t, parts, second_f, state_one, w_one, raw, c, keep_one, grad, pack.at[1],
        lambda index: None, lambda: upper.step_one(0),
    )
    upper.step_one(1)

    def between(index):
        pl.when(index == 2)(upper.step_two)
        pl.when(index == 4)(upper.step_three)
        pl.when(index == 5)(upper.step_four)

    side_backward(
        0, b, t, parts, first_f, prev, w_zero, raw, c, keep_zero, grad, pack.at[0],
        between, lambda: lower.step_one(0),
    )
    lower.step_one(1)
    upper.step_five()
    lower.step_two()
    lower.step_three()
    lower.step_four()
    lower.step_five()


def side_rest_call(first_f, second_f, side_in, cotangent, ids_all, raw, state_one, kvt_zero, keep_zero, parts, batch):
    tokens, model = first_f.shape
    length = parts * tokens
    units = raw[5].shape[2]
    dma = pltpu.SemaphoreType.DMA
    vmem = pltpu.VMEM
    pairs = SIDE_HEADS // 2
    group = COLUMNS // parts
    piece = group * 96 // RING
    outs = (
        ((tokens, 128), F32),
        ((tokens, 128), F32),
        ((LAYERS, parts, RING, piece, 128), BF16),
    )
    outer = max(batch // RING, 1)
    return pl.pallas_call(
        functools.partial(side_rest_kernel, parts, batch),
        out_shape=tuple(jax.ShapeDtypeStruct(*o) for o in outs),
        in_specs=vmem_specs(12) + [pl.BlockSpec(memory_space=pl.ANY)] * 8,
        out_specs=tuple(vmem_specs(len(outs))),
        scratch_shapes=[
            vmem((tokens, model), BF16),
            vmem((parts, 192, tokens), BF16),
            *[vmem(*shape) for shape in keep_shapes(tokens)],
            dma((8,)),
            vmem((parts, 192, tokens), BF16),
            vmem((tokens, 128), F32),
            vmem((LAYERS, COLUMNS, 96, 128), F32),
            vmem((LAYERS, 8, 128), F32),
            *[vmem(*shape) for shape in keep_shapes(tokens)],
            *weight_scratch(model, units),
            *weight_scratch(model, units),
            vmem((LAYERS, length, 256), BF16),
            vmem((SIDE_HEADS, 16, length), BF16),
            vmem((2, length, tokens), F32),
            dma((3,)),
            dma((parts,)),
            vmem((tokens, 128), BF16),
            vmem((SIDE_HEADS, 16, tokens), BF16),
            vmem((LAYERS, tokens, 256), BF16),
            vmem((LAYERS, SIDE_HEADS, 16, tokens), BF16),
            vmem((LAYERS, length, 128), BF16),
            vmem((LAYERS, SIDE_HEADS, 16, length), BF16),
            vmem((LAYERS, tokens, units), BF16),
            vmem((LAYERS, tokens, units), F32),
            vmem((pairs, parts, 32, tokens), BF16),
            vmem((LAYERS, pairs, parts, 32, tokens), BF16),
            vmem((384, tokens), BF16),
            dma((LAYERS, pairs, parts - 1)),
            dma((LAYERS, pairs, parts)),
            vmem((LAYERS, COLUMNS, 96, 128), BF16),
            vmem((LAYERS, parts, group, 96, 128), BF16),
            vmem((LAYERS, RING, piece, 128), F32),
            vmem((LAYERS, RING, piece, 128), BF16),
            vmem((LAYERS, RING, piece, 128), BF16),
            vmem((LAYERS, outer, piece, 128), BF16),
            dma((LAYERS, 2, parts - 1)),
            dma((LAYERS, 2, parts)),
            dma((LAYERS, RING - 1)),
            dma((LAYERS, RING)),
            dma((LAYERS, max(outer - 1, 1))),
            dma((LAYERS, outer)),
            dma((LAYERS, RING - 1)),
            dma((LAYERS, RING)),
            dma((LAYERS, parts - 1, RING)),
            dma((LAYERS, parts, RING)),
        ],
        compiler_params=pltpu.CompilerParams(
            collective_id=5, has_side_effects=True, vmem_limit_bytes=62 << 20
        ),
    )(second_f, side_in, cotangent, ids_all, *raw, state_one, first_f, kvt_zero, *keep_zero)


def finish_call(frozen, state, grad, full, side, parts):
    tokens, model = frozen.shape
    units = 4 * side
    outs = (
        ((tokens, model), BF16),
        ((side, tokens), F32),
        ((side, tokens), F32),
        ((LAYERS, side, model), F32),
        ((LAYERS, side), F32),
        ((LAYERS, 2, side), F32),
        ((LAYERS, side, 3 * side), F32),
        ((LAYERS, side, side), F32),
        ((LAYERS, side, units), F32),
        ((LAYERS, side, units), F32),
    )
    frozen, state, grad, down, *others, reduce_grad = pl.pallas_call(
        functools.partial(finish_kernel, parts),
        out_shape=tuple(jax.ShapeDtypeStruct(*o) for o in outs),
        in_specs=vmem_specs(4),
        out_specs=tuple(vmem_specs(len(outs))),
        compiler_params=pltpu.CompilerParams(vmem_limit_bytes=62 << 20),
    )(frozen, state, grad, full)
    turn = (0, 2, 1)
    return (frozen, state.T, grad.T, down.transpose(turn), *others, reduce_grad.transpose(turn))


def per_device(
    hidden_rows,
    side_input,
    segment_ids,
    side_cotangent,
    backbone_gains,
    backbone_project,
    backbone_mixing,
    backbone_expand,
    backbone_reduce,
    side_down,
    side_gate,
    side_gains,
    side_project,
    side_mixing,
    side_expand,
    side_reduce,
):
    parts = lax.axis_size("tensor")
    batch = lax.axis_size("batch")
    side = side_input.shape[1]
    turn = (0, 2, 1)
    qkv = backbone_project.transpose(0, 2, 3, 1)
    raw = (
        side_gate,
        side_gains,
        side_down.transpose(turn),
        side_project,
        side_mixing,
        side_expand,
        side_reduce.transpose(turn),
    )
    side_turned, cotangent_turned = side_input.T, side_cotangent.T
    ids_row = segment_ids.reshape(1, -1)

    second_f, first_f, ids_all, state_one, kvt_zero, *keep_zero = front_call(
        hidden_rows,
        ids_row,
        backbone_gains,
        qkv,
        backbone_mixing,
        backbone_expand,
        backbone_reduce,
        side_turned,
        raw,
        parts,
    )
    state, grad, full = side_rest_call(
        first_f, second_f, side_turned, cotangent_turned, ids_all, raw, state_one, kvt_zero, keep_zero, parts, batch
    )
    return finish_call(second_f, state, grad, full, side, parts)


def solution(mesh):
    return jax.shard_map(
        per_device,
        mesh=mesh,
        in_specs=(
            P(("batch", "tensor"), None),
            P(("batch", "tensor"), None),
            P(("batch", "tensor")),
            P(("batch", "tensor"), None),
            P(),
            P(None, None, None, "tensor"),
            P(None, "tensor", None),
            P(None, None, "tensor"),
            P(None, "tensor", None),
            P(),
            P(),
            P(),
            P(),
            P(),
            P(),
            P(),
        ),
        out_specs=(
            P(("batch", "tensor"), None),
            P(("batch", "tensor"), None),
            P(("batch", "tensor"), None),
            P(),
            P(),
            P(),
            P(),
            P(),
            P(),
            P(),
        ),
        check_vma=False,
    )
```

```python
import functools
import jax
import jax.numpy as jnp
from jax import lax
from jax.experimental import pallas as pl
from jax.experimental.pallas import tpu as pltpu
from jax.sharding import PartitionSpec as P

HEAD_DIM = 64
SIDE_HEADS = 12
SIDE_HEAD_DIM = 8
LAYERS = 2
EPS = 1e-06
BIG = 2.0**100
LOG2E = 1.4426950408889634
ID_BITS = 11
QUAD = 4
MESH = pl.DeviceIdType.MESH
F32 = jnp.float32
BF16 = jnp.bfloat16


def contract(left, right, dims):
    return lax.dot_general(left, right, ((dims[:1], dims[1:]), ((), ())), preferred_element_type=F32)


def nn(left, right):
    return contract(left, right, (1, 0))


def nt(left, right):
    return contract(left, right, (1, 1))


def tn(left, right):
    return contract(left, right, (0, 0))


def lanes_of(rows, lanes):
    return lax.broadcasted_iota(jnp.int32, (rows, lanes), 1)


def segment_lanes(id_row, offset):
    width = id_row.shape[1]
    place = lax.broadcasted_iota(jnp.int32, (128, width), 0) - offset
    flipped = place >= ID_BITS
    shift = jnp.clip(jnp.where(flipped, place - ID_BITS, place), 0, ID_BITS)
    bit = lax.shift_right_logical(jnp.broadcast_to(id_row, (128, width)), shift) & 1
    bit = jnp.where(flipped, 1 - bit, bit)
    used = (place >= 0) & (place < 2 * ID_BITS)
    keys = jnp.where(used, bit, 0).astype(F32)
    queries = jnp.where(used, (bit - 1).astype(F32) * BIG, 0.0)
    return keys.T, queries.T


def root_norm(values, gain):
    return values * lax.rsqrt(jnp.mean(values * values, axis=-1, keepdims=True) + EPS) * gain


class Refs:
    def __init__(self, **refs):
        self.__dict__.update(refs)


def remote(src, dst, send, recv, target):
    return pltpu.make_async_remote_copy(
        src_ref=src, dst_ref=dst, send_sem=send, recv_sem=recv, device_id=target, device_id_type=MESH
    )


class Weights:
    def __init__(self, layer, b, t, c):
        self.layer, self.b, self.t, self.c = layer, b, t, c
        self.part = lax.rem(b, QUAD)
        self.fulls = (c.mix_w, c.exp_w, c.red_w)
        self.sources = (c.mix_hbm, c.exp_hbm, c.red_hbm)
        self.slices = tuple(w.shape[2] // QUAD for w in self.fulls)
        mix, up, down = self.slices
        self.pieces = (
            (0, 0, mix),
            (1, 0, up // 2),
            (1, up // 2, up // 2),
            (2, 0, down // 2),
            (2, down // 2, down // 2),
        )

    def rows(self, p, part):
        w, low, size = self.pieces[p]
        return pl.ds(pl.multiple_of(part * self.slices[w] + low, 16), size)

    def view(self, p, slot, part):
        return self.fulls[self.pieces[p][0]].at[self.layer, slot, self.rows(p, part)]

    def load(self, w):
        return pltpu.make_async_copy(
            self.sources[w].at[self.layer],
            self.fulls[w].at[self.layer, self.t],
            self.c.load_sem.at[self.layer, w],
        )

    def own(self, w, slot):
        c = self.c
        return remote(
            self.sources[w].at[self.layer],
            self.fulls[w].at[self.layer, slot],
            c.own_send.at[self.layer, w],
            c.own_recv.at[self.layer, w],
            (self.b, self.t ^ 1),
        )

    def cross(self, p):
        c = self.c
        return remote(
            self.sources[self.pieces[p][0]].at[self.layer, self.rows(p, self.part)],
            self.view(p, self.t, self.part),
            c.cross_send.at[self.layer, p],
            c.w_recv.at[self.layer, p, self.part],
            (self.b, self.t ^ 2),
        )

    def spread(self, p, k):
        c = self.c
        view = self.view(p, self.t ^ 2, self.part)
        return remote(
            view, view, c.spread_send.at[self.layer, p, k - 1], c.w_recv.at[self.layer, p, self.part], (self.b ^ k, self.t)
        )

    def here(self, p, k):
        c = self.c
        view = self.view(p, self.t ^ 2, self.part ^ k)
        return remote(
            view, view, c.cross_send.at[self.layer, p], c.w_recv.at[self.layer, p, self.part ^ k], (self.b, self.t ^ 2)
        )

    def forward(self, p, k, slot):
        c = self.c
        view = self.view(p, slot, self.part ^ k)
        return remote(
            view,
            view,
            c.pass_send.at[self.layer, p, k],
            c.pass_recv.at[self.layer, p, self.part ^ k],
            (self.b, self.t ^ 1),
        )

    def start_cross(self):
        for p in range(5):
            self.cross(p).start()

    def start_spread(self, p):
        self.here(p, 0).wait_recv()
        for k in range(1, QUAD):
            self.spread(p, k).start()

    def start_forward(self, p):
        for k in range(1, QUAD):
            self.here(p, k).wait_recv()
        for k in range(QUAD):
            self.forward(p, k, self.t ^ 2).start()

    def wait_far(self, p):
        for k in range(QUAD):
            self.forward(p, k, self.t ^ 3).wait_recv()

    def wait_sent(self):
        for w in range(3):
            self.own(w, self.t).wait_send()
        for p in range(5):
            self.cross(p).wait_send()
            for k in range(1, QUAD):
                self.spread(p, k).wait_send()
            for k in range(QUAD):
                self.forward(p, k, self.t ^ 2).wait_send()


class Backbone:
    def __init__(self, layer, b, t, parts, c):
        self.layer, self.b, self.t, self.parts, self.c = layer, b, t, parts, c
        self.sib, self.across, self.far = t ^ 1, t ^ 2, t ^ 3
        self.tokens = c.rows_all.shape[1]
        self.half = self.tokens // 2
        self.width = c.mix_w.shape[2]
        self.heads = self.width // HEAD_DIM
        self.weights = Weights(layer, b, t, c)

    def row_copy(self, slot, chunk, send, target):
        c = self.c
        view = c.rows_all.at[slot, pl.ds(chunk * self.half, self.half)]
        return remote(
            view,
            view,
            c.row_send.at[self.layer, send, chunk],
            c.row_recv.at[self.layer, slot, chunk],
            (self.b, target),
        )

    def norm_rows(self, stream):
        c = self.c
        gain = c.gains[self.layer, 0:1, :].astype(F32)
        c.rows_all[self.t] = root_norm(stream, gain).astype(BF16)

    def send_rows(self):
        for chunk in range(2):
            self.row_copy(self.t, chunk, 1, self.across).start()
        for chunk in range(2):
            self.row_copy(self.t, chunk, 0, self.sib).start()

    def project(self, slot, chunk):
        c, width, half = self.c, self.width, self.half
        inside = pl.ds(pl.multiple_of(chunk * half, half), half)
        rows = c.rows_all[slot, inside, :]
        at = pl.ds(pl.multiple_of(slot * self.tokens + chunk * half, half), half)
        lane = lanes_of(half, 128)
        query = nt(rows, c.qkv_w[self.layer, 0]) * (HEAD_DIM**-0.5 * LOG2E)
        keys = nt(rows, c.qkv_w[self.layer, 1])
        bits = segment_lanes(c.ids_all[slot, 0:1, inside], HEAD_DIM)
        for target, columns, high in ((c.k_s, keys, bits[0]), (c.q_s, query, bits[1])):
            low = pltpu.roll(high, HEAD_DIM, 1)
            for h in range(self.heads):
                own = columns[:, h // 2 * 128 : h // 2 * 128 + 128]
                inner = jnp.where(lane < HEAD_DIM, own, high) if h % 2 == 0 else jnp.where(lane < HEAD_DIM, low, own)
                target[h, at] = inner.astype(BF16)
        values = nt(c.qkv_w[self.layer, 2, 0:width], rows)
        for h in range(self.heads):
            c.vt_s[h, 0:HEAD_DIM, at] = values[h * HEAD_DIM : (h + 1) * HEAD_DIM].astype(BF16)
            c.vt_s[h, HEAD_DIM:, at] = jnp.ones((16, half), BF16)

    def project_all(self, first, last, hook):
        def step(index, carry):
            for chunk in range(2):

                @pl.when(index == 2 + chunk)
                def _():
                    self.row_copy(self.sib, chunk, 0, self.sib).wait_recv()

                @pl.when(index == 4 + 2 * chunk)
                def _():
                    self.row_copy(self.across, chunk, 0, self.sib).wait_recv()
                    self.row_copy(self.across, chunk, 2, self.sib).start()

                @pl.when(index == 5 + 2 * chunk)
                def _():
                    self.row_copy(self.far, chunk, 0, self.sib).wait_recv()

            hook(index)
            early = index < 4
            k = jnp.where(early, index // 2, 2 + index % 2)
            chunk = jnp.where(early, index % 2, index // 2 - 2)
            self.project(self.t ^ k, chunk)
            return carry

        lax.fori_loop(first, last, step, 0)

    def wait_rows(self):
        for chunk in range(2):
            self.row_copy(self.t, chunk, 0, self.sib).wait_send()
            self.row_copy(self.t, chunk, 1, self.across).wait_send()
            self.row_copy(self.across, chunk, 2, self.sib).wait_send()

    def block_of(self, item):
        return self.t ^ (self.parts - 1 - item // self.heads)

    def make_scores(self, item, place):
        c = self.c
        h = lax.rem(item, self.heads)
        at = pl.ds(pl.multiple_of(self.block_of(item) * self.tokens, self.tokens), self.tokens)
        c.scores[place] = nt(c.k_s[h], c.q_s[h, at])

    def send_heads(self, block):
        c = self.c
        return remote(
            c.heads_buf.at[block],
            c.heads_buf.at[self.parts + self.t],
            c.head_send.at[self.layer, block],
            c.head_recv.at[self.layer, self.t],
            (self.b, block),
        )

    def attend(self, item, place):
        c = self.c
        block = self.block_of(item)
        h = lax.rem(item, self.heads)
        values = c.scores[place]
        weights = jnp.exp2(values - jnp.max(values, axis=0, keepdims=True)).astype(BF16)
        out = nn(c.vt_s[h], weights)
        slot = jnp.where(block == self.t, self.parts + self.t, block)
        c.heads_buf[slot, pl.ds(pl.multiple_of(h * HEAD_DIM, HEAD_DIM), HEAD_DIM), :] = (
            out[0:HEAD_DIM] * (1.0 / out[HEAD_DIM : HEAD_DIM + 1])
        ).astype(BF16)

        @pl.when((h == self.heads - 1) & (item < (self.parts - 1) * self.heads))
        def _():
            self.send_heads(block).start()

    def attention(self, hook):
        count = self.parts * self.heads
        self.make_scores(0, 0)

        def pair(index, carry):
            item = 2 * index
            hook(index)
            self.make_scores(item + 1, 1)
            self.attend(item, 0)
            self.make_scores(jnp.minimum(item + 2, count - 1), 0)
            self.attend(item + 1, 1)
            return carry

        lax.fori_loop(0, count // 2, pair, 0)

    def wait_heads(self):
        c = self.c
        for k in range(1, self.parts):
            self.send_heads(self.t ^ k).wait_send()
            remote(
                c.heads_buf.at[0],
                c.heads_buf.at[self.parts + (self.t ^ k)],
                c.head_send.at[self.layer, 0],
                c.head_recv.at[self.layer, self.t ^ k],
                (self.b, self.sib),
            ).wait_recv()

    def feed_forward(self, stream, hook):
        c, parts, layer = self.c, self.parts, self.layer
        attended = c.heads_buf[parts : 2 * parts].reshape(parts * self.width, self.tokens)
        stream = stream + tn(attended, c.mix_w[layer].reshape(parts * self.width, -1))
        c.acc[...] = stream
        c.normed[...] = root_norm(stream, c.gains[layer, 1:2, :].astype(F32)).astype(BF16)

        def feed(index, carry):
            hook(index)
            hidden = jax.nn.gelu(nn(c.normed[...], c.exp_w[layer, self.t ^ index])).astype(BF16)
            c.acc[...] += nn(hidden, c.red_w[layer, self.t ^ index])
            return carry

        def far_up(index, carry):
            hook(index)
            c.spare[index - 2] = jax.nn.gelu(nn(c.normed[...], c.exp_w[layer, self.t ^ index])).astype(BF16)
            return carry

        def far_down(index, carry):
            hook(index + 2)
            c.acc[...] += nn(c.spare[index - 2], c.red_w[layer, self.t ^ index])
            return carry

        lax.fori_loop(0, 2, feed, 0)
        lax.fori_loop(2, parts, far_up, 0)
        lax.fori_loop(2, parts, far_down, 0)


FRONT_SCRATCH = (
    *("vectors", "rows_all", "ids_scratch", "qkv_w", "mix_w", "exp_w", "red_w", "q_s", "k_s", "vt_s", "scores"),
    *("heads_buf", "acc", "normed", "load_sem", "qkv_sem", "row_send", "row_recv", "id_send", "id_recv"),
    *("head_send", "head_recv", "cross_send", "spread_send", "pass_send", "own_send", "w_recv", "pass_recv"),
    *("own_recv", "side_k", "side_vt", "kv_send", "kv_recv", "spare"),
)


def front_kernel(parts, *refs):
    refs = list(refs)

    def pop(count):
        taken, refs[:count] = refs[:count], []
        return taken

    x_ref, ids_ref, gains, qkv_hbm, mix_hbm, exp_hbm, red_hbm, side_in = pop(8)
    raw = Refs(**dict(zip(RAW, pop(7))))
    second_f, *handed = pop(11)
    local = pop(10)
    first_f, ids_all, state_one, kvt = local[0:4]
    keep = Refs(**dict(zip(KEEP, local[4:])))
    hand_sem = pop(1)[0]
    hand = [pltpu.make_async_copy(*pair, hand_sem.at[k]) for k, pair in enumerate(zip(local, handed))]
    prev = pop(1)[0]
    w = Refs(**dict(zip(WEIGHTS, pop(5))))
    c = Refs(**dict(zip(FRONT_SCRATCH, pop(len(FRONT_SCRATCH)))))
    c.gains, c.mix_hbm, c.exp_hbm, c.red_hbm, c.ids_all = gains, mix_hbm, exp_hbm, red_hbm, ids_all
    b = lax.axis_index("batch")
    t = lax.axis_index("tensor")
    tokens = x_ref.shape[0]
    width = c.mix_w.shape[2]
    lower, upper = Backbone(0, b, t, parts, c), Backbone(1, b, t, parts, c)
    load_qkv = [
        pltpu.make_async_copy(
            qkv_hbm.at[layer, k], c.qkv_w.at[layer, k, pl.ds(0, width)], c.qkv_sem.at[layer, k]
        )
        for layer in range(LAYERS)
        for k in range(3)
    ]
    for copy in load_qkv:
        copy.start()
    for layer in (lower, upper):
        for k in range(3):
            layer.weights.load(k).start()
    barrier = tensor_barrier(b, t, parts)
    for k in range(1, QUAD):
        pl.semaphore_signal(barrier, inc=1, device_id=(b ^ k, t), device_id_type=MESH)
    lower.norm_rows(x_ref[...].astype(F32))
    ids_all[t] = jnp.broadcast_to(ids_ref[...], (8, tokens))
    pl.semaphore_wait(barrier, parts - 1 + QUAD - 1)

    def id_copy(slot, k):
        return remote(ids_all.at[slot], ids_all.at[slot], c.id_send.at[k - 1], c.id_recv.at[slot], (b, t ^ k))

    for k in range(1, parts):
        id_copy(t, k).start()
    lower.weights.cross(1).start()
    lower.send_rows()
    for k in range(3):
        lower.weights.own(k, t).start()
    c.qkv_w[:, :, width:, :] = jnp.zeros((LAYERS, 3, 256 - width, x_ref.shape[1]), BF16)
    for copy in load_qkv:
        copy.wait()
    load_side_weights(0, w, raw)
    load_vectors(c.vectors, raw)
    raw.vectors = c.vectors
    prev[...] = widened(side_in)
    for k in range(1, parts):
        id_copy(t, k).wait_send()
        id_copy(t ^ k, k).wait_recv()

    def when(index, at, act, *args):
        @pl.when(index == at)
        def _():
            act(*args)

    def lower_project(index):
        when(index, 4, lower.weights.start_spread, 1)
        for p in (0, 2, 3, 4):
            when(index, 6, lambda p: lower.weights.cross(p).start(), p)

    def lower_attention(index):
        for at, p in ((1, 0), (2, 2), (3, 3), (5, 4)):
            when(index, at, lower.weights.start_spread, p)
        for at, p in ((4, 1), (5, 0)):
            when(index, at, lower.weights.start_forward, p)

    def feed_hook(layer):
        def hook(index):
            weights = layer.weights

            @pl.when(index == 0)
            def _():
                for k in (1, 2):
                    weights.load(k).wait()
                if layer is lower:
                    weights.start_forward(2)

            @pl.when(index == 1)
            def _():
                for k in (1, 2):
                    weights.own(k, layer.sib).wait_recv()

            @pl.when(index == 3)
            def _():
                for p in (1, 2):
                    weights.wait_far(p)

            @pl.when(index == 4)
            def _():
                if layer is lower:
                    for p in (3, 4):
                        weights.start_forward(p)

            @pl.when(index == 5)
            def _():
                for p in (3, 4):
                    weights.wait_far(p)

        return hook

    lower.project_all(0, 2 * parts, lower_project)
    lower.wait_rows()
    lower.attention(lower_attention)
    upper.weights.start_cross()
    for k in range(3):
        upper.weights.own(k, t).start()
    lower.weights.load(0).wait()
    lower.weights.own(0, lower.sib).wait_recv()
    lower.weights.wait_far(0)
    lower.wait_heads()
    lower.feed_forward(x_ref[...].astype(F32), feed_hook(lower))
    first_f[...] = c.acc[...].astype(BF16)

    side = Refs(
        kvt=kvt, k_s=c.side_k, vt_s=c.side_vt, scores=c.scores, kv_send=c.kv_send, kv_recv=c.kv_recv
    )

    def send_upper():
        upper.norm_rows(c.acc[...])
        upper.send_rows()

    def side_hook(index):
        for p in range(5):
            when(index, p, upper.weights.start_spread, p)

    side_forward(
        0, b, t, parts, first_f, prev, w, raw, side, keep, ids_all, state_one,
        send_upper, lambda: upper.project_all(0, parts, lambda index: None), side_hook,
    )

    for copy in hand:
        copy.start()

    def upper_attention(index):
        for p in range(5):
            when(index, p + 1, upper.weights.start_forward, p)

    upper.project_all(parts, 2 * parts, lambda index: None)
    upper.wait_rows()
    upper.attention(upper_attention)
    upper.weights.load(0).wait()
    upper.weights.own(0, upper.sib).wait_recv()
    upper.weights.wait_far(0)
    upper.wait_heads()
    upper.feed_forward(c.acc[...], feed_hook(upper))
    second_f[...] = c.acc[...].astype(BF16)
    for copy in hand:
        copy.wait()
    lower.weights.wait_sent()
    upper.weights.wait_sent()


def front_call(x, ids, gains, qkv, mix, exp, red, side_in, raw, parts):
    tokens, model = x.shape
    width = mix.shape[1]
    units = exp.shape[2]
    heads = width // HEAD_DIM
    length = parts * tokens
    side_units = raw[5].shape[2]
    anywhere = pl.BlockSpec(memory_space=pl.ANY)
    dma = pltpu.SemaphoreType.DMA
    vmem = pltpu.VMEM
    outs = (
        ((tokens, model), BF16),
        ((tokens, model), BF16),
        ((parts, 8, tokens), jnp.int32),
        ((tokens, 128), F32),
        ((parts, 192, tokens), BF16),
        *keep_shapes(tokens),
    )
    return pl.pallas_call(
        functools.partial(front_kernel, parts),
        out_shape=tuple(jax.ShapeDtypeStruct(*o) for o in outs),
        in_specs=vmem_specs(3) + [anywhere] * 4 + vmem_specs(8),
        out_specs=(*vmem_specs(1), *[anywhere] * 10),
        scratch_shapes=[
            *[vmem(*out) for out in outs[1:]],
            dma((10,)),
            vmem((tokens, 128), F32),
            *weight_scratch(model, side_units),
            vmem((LAYERS, 8, 128), F32),
            vmem((parts, tokens, model), BF16),
            vmem((8, 128), F32),
            vmem((LAYERS, 3, 256, model), BF16),
            vmem((LAYERS, parts, width, model), BF16),
            vmem((LAYERS, parts, model, units), BF16),
            vmem((LAYERS, parts, units, model), BF16),
            vmem((heads, length, 128), BF16),
            vmem((heads, length, 128), BF16),
            vmem((heads, HEAD_DIM + 16, length), BF16),
            vmem((2, length, tokens), F32),
            vmem((2 * parts, width, tokens), BF16),
            vmem((tokens, model), F32),
            vmem((tokens, model), BF16),
            dma((LAYERS, 3)),
            dma((LAYERS, 3)),
            dma((LAYERS, 3, 2)),
            dma((LAYERS, parts, 2)),
            dma((parts - 1,)),
            dma((parts,)),
            dma((LAYERS, parts)),
            dma((LAYERS, parts)),
            dma((LAYERS, 5)),
            dma((LAYERS, 5, QUAD - 1)),
            dma((LAYERS, 5, QUAD)),
            dma((LAYERS, 3)),
            dma((LAYERS, 5, QUAD)),
            dma((LAYERS, 5, QUAD)),
            dma((LAYERS, 3)),
            vmem((length, 128), BF16),
            vmem((SIDE_HEADS, 16, length), BF16),
            dma((3,)),
            dma((parts,)),
            vmem((2, tokens, model), BF16),
        ],
        compiler_params=pltpu.CompilerParams(
            collective_id=1, has_side_effects=True, vmem_limit_bytes=62 << 20
        ),
    )(x, ids, gains, qkv, mix, exp, red, side_in, *raw)


LN2 = 0.6931471805599453
COLUMNS = 16
EARLY = (6, 7, 8, 9, 10, 11, 12, 13)
LATE = (0, 1, 2, 3, 4, 5, 14, 15)


def place_of(column):
    order, low = (EARLY, 0) if column in EARLY else (LATE, 2)
    index = order.index(column)
    return index // 2 * 4 + low + index % 2


RING = 8


def side_norm(values, width):
    rstd = lax.rsqrt(jnp.sum(values * values, axis=-1, keepdims=True) * (1.0 / width) + EPS)
    return values * rstd, rstd


def gelu_parts(inner):
    root = 0.7978845608028654
    square = inner * inner
    curve = jnp.tanh(root * inner * (1.0 + 0.044715 * square))
    half = 0.5 * (1.0 + curve)
    slope = half + 0.5 * inner * (1.0 - curve * curve) * root * (1.0 + 3 * 0.044715 * square)
    return inner * half, slope


def load_side_weights(layer, w, raw):
    side = raw.mixing.shape[1]
    w.down[side:, :] = jnp.zeros_like(w.down[side:, :])
    w.down[0:side, :] = raw.down[layer]
    w.project[...] = jnp.zeros_like(w.project)
    w.project[0:side, 0 : 3 * side] = raw.project[layer]
    w.mixing[...] = jnp.zeros_like(w.mixing)
    w.mixing[0:side, 0:side] = raw.mixing[layer]
    w.expand[side:, :] = jnp.zeros_like(w.expand[side:, :])
    w.expand[0:side, :] = raw.expand[layer]
    w.reduce[side:, :] = jnp.zeros_like(w.reduce[side:, :])
    w.reduce[0:side, :] = raw.reduce[layer]


def load_vectors(vectors, raw):
    side = raw.mixing.shape[1]
    vectors[...] = jnp.zeros_like(vectors)
    for layer in range(LAYERS):
        vectors[layer, 0:1, 0:side] = raw.gate[layer : layer + 1, :]
        vectors[layer, 1:3, 0:side] = raw.gains[layer].astype(F32)


def widened(turned):
    values = turned[...].astype(F32)
    return jnp.concatenate([values, jnp.zeros((32, values.shape[1]), F32)], axis=0).T


def kv_copy(c, slot, send, target):
    return remote(c.kvt.at[slot], c.kvt.at[slot], c.kv_send.at[send], c.kv_recv.at[slot], target)


def keys_from(c, slot, ids_ref):
    tokens = c.kvt.shape[2]
    at = pl.ds(pl.multiple_of(slot * tokens, tokens), tokens)
    key_bits, _ = segment_lanes(ids_ref[slot][0:1, :], 96)
    keys = jnp.concatenate([c.kvt[slot, 0:96].astype(F32), jnp.zeros((32, tokens), F32)], axis=0)
    c.k_s[at, 0:128] = (keys.T + key_bits).astype(BF16)


def side_forward(layer, b, t, parts, f_ref, prev, w, raw, c, keep, ids_ref, result, after_send, meanwhile, between):
    side = raw.mixing.shape[1]
    tokens = f_ref.shape[0]
    gate = jax.nn.sigmoid(raw.vectors[layer, 0:1, :])
    lifted = nt(f_ref[...], w.down[...])
    mixed = gate * lifted + (1.0 - gate) * prev[...]
    keep.lifted[...] = lifted
    keep.mixed[...] = mixed
    normed = (side_norm(mixed, side)[0] * raw.vectors[layer, 1:2, :]).astype(BF16)
    turned = w.project[...].astype(F32).T.astype(BF16)
    c.kvt[t] = nt(turned[side : 3 * side], normed).astype(BF16)
    sib, across, far = t ^ 1, t ^ 2, t ^ 3
    kv_copy(c, t, 1, (b, across)).start()
    kv_copy(c, t, 0, (b, sib)).start()
    after_send()
    lane = lanes_of(tokens, 128)
    weight_q = jnp.where(lanes_of(128, 128) < side, w.project[:, 0:128], jnp.zeros((128, 128), BF16))
    query_bits = segment_lanes(ids_ref[t][0:1, :], 96)[1]
    keep.query[...] = (
        nn(normed, weight_q) * (SIDE_HEAD_DIM**-0.5 * LOG2E) + query_bits
    ).astype(BF16)
    keep.sums[...] = jnp.zeros_like(keep.sums)

    def take(index, carry):
        @pl.when(index == 1)
        def _():
            kv_copy(c, sib, 0, (b, sib)).wait_recv()

        @pl.when(index == 2)
        def _():
            meanwhile()
            kv_copy(c, across, 0, (b, sib)).wait_recv()
            kv_copy(c, across, 2, (b, sib)).start()

        @pl.when(index == 3)
        def _():
            kv_copy(c, far, 0, (b, sib)).wait_recv()

        slot = t ^ index
        at = pl.ds(pl.multiple_of(slot * tokens, tokens), tokens)
        keys_from(c, slot, ids_ref)
        values = c.kvt[slot, 96:192].astype(F32)
        for h in range(SIDE_HEADS):
            c.vt_s[h, :, at] = jnp.concatenate(
                [values[8 * h : 8 * h + 8], jnp.ones((8, tokens), F32)], axis=0
            ).astype(BF16)
        return carry

    lax.fori_loop(0, parts, take, 0)

    def make_scores(h, place):
        rows = keep.query[...]
        chosen = (lane // SIDE_HEAD_DIM == h) | (lane >= side)
        c.scores[place] = nt(c.k_s[:, 0:128], jnp.where(chosen, rows, jnp.zeros_like(rows)))

    def attend(h, place):
        values = c.scores[place]
        top = jnp.max(values, axis=0, keepdims=True)
        out = nn(c.vt_s[h], jnp.exp2(values - top).astype(BF16))
        total = out[8:9]
        keep.heads[pl.ds(pl.multiple_of(h * 8, 8), 8), :] = out[0:8] * (1.0 / total)
        here = lax.broadcasted_iota(jnp.int32, keep.sums.shape, 0) == h
        keep.sums[...] = jnp.where(here, top + jnp.log2(total), keep.sums[...])

    make_scores(0, 0)

    def pair(index, carry):
        h = 2 * index
        between(index)
        make_scores(h + 1, 1)
        attend(h, 0)
        make_scores(jnp.minimum(h + 2, SIDE_HEADS - 1), 0)
        attend(h + 1, 1)
        return carry

    lax.fori_loop(0, SIDE_HEADS // 2, pair, 0)
    kv_copy(c, t, 1, (b, across)).wait_send()
    kv_copy(c, t, 0, (b, sib)).wait_send()
    kv_copy(c, across, 2, (b, sib)).wait_send()
    middle = mixed + tn(keep.heads[...].astype(BF16), w.mixing[0:side, :])
    keep.middle[...] = middle
    normed_two = (side_norm(middle, side)[0] * raw.vectors[layer, 2:3, :]).astype(BF16)
    active = jax.nn.gelu(nn(normed_two, w.expand[...])).astype(BF16)
    result[...] = middle + nt(active, w.reduce[...])


def norm_back(values, gain, grad, side):
    hat, rstd = side_norm(values, side)
    gain_grad = jnp.sum(grad * hat, axis=0, keepdims=True)
    pulled = grad * gain
    mean = jnp.sum(pulled * hat, axis=-1, keepdims=True) * (1.0 / side)
    return rstd * (pulled - hat * mean), gain_grad


def pad_heads(target, rows, fill):
    for h in range(SIDE_HEADS):
        target[h] = jnp.concatenate(
            [rows[8 * h : 8 * h + 8], jnp.full((8, rows.shape[1]), fill, F32)], axis=0
        ).astype(BF16)


def side_prepare(layer, parts, w, raw, c, keep, kvt, ids_ref, again):
    side = raw.mixing.shape[1]
    tokens = c.q_s.shape[1]
    lane = lanes_of(tokens, 128)
    normed_two = side_norm(keep.middle[...], side)[0] * raw.vectors[layer, 2:3, :]
    active, slope = gelu_parts(nn(normed_two.astype(BF16), w.expand[...]))
    c.active[layer] = active.astype(BF16)
    c.slope[layer] = slope
    sums = keep.sums[...]
    rows = jnp.concatenate([sums, sums, sums, jnp.zeros((80, tokens), F32)], axis=0).T
    high = rows.astype(BF16).astype(F32)
    mid = (rows - high).astype(BF16).astype(F32)
    low = rows - high - mid
    rows = jnp.where(lane < 16, high, jnp.where(lane < 32, mid, low))
    query = keep.query[...]
    c.q_s[layer, :, 0:128] = query
    c.q_s[layer, :, 128:256] = jnp.where(lane < 48, -rows, 0.0).astype(BF16)
    pad_heads(c.qt_s.at[layer], query.astype(F32).T, 0.0)

    def take(slot, carry):
        at = pl.ds(pl.multiple_of(slot * tokens, tokens), tokens)
        if again:
            keys_from(Refs(kvt=kvt, k_s=c.k_s.at[layer]), slot, ids_ref)
        c.k_s[layer, at, 128:256] = jnp.where(lane < 48, 1.0, 0.0).astype(BF16)
        values = jnp.concatenate([kvt[slot, 96:192].astype(F32), jnp.ones((32, tokens), F32)], axis=0)
        c.v_s[layer, at, :] = values.T.astype(BF16)
        keys = kvt[slot, 0:96].astype(F32)
        for h in range(SIDE_HEADS):
            c.kt_s[layer, h, :, at] = jnp.concatenate(
                [keys[8 * h : 8 * h + 8], jnp.zeros((8, tokens), F32)], axis=0
            ).astype(BF16)
        return carry

    lax.fori_loop(0, parts, take, 0)


def side_backward(layer, b, t, parts, f_ref, prev, w, raw, c, keep, grad_ref, pack, between, early):
    side = raw.mixing.shape[1]
    tokens = f_ref.shape[0]
    gate = jax.nn.sigmoid(raw.vectors[layer, 0:1, :])
    lane = lanes_of(tokens, 128)
    grad = grad_ref[...]
    middle = keep.middle[...]
    gain_two = raw.vectors[layer, 2:3, :]
    normed_two = (side_norm(middle, side)[0] * gain_two).astype(BF16)
    top = grad.astype(BF16)
    reduce_grad = tn(top, c.active[layer])
    grad_inner = (c.slope[layer] * nn(top, w.reduce[...])).astype(BF16)
    expand_grad = tn(normed_two, grad_inner)
    for k in range(3):
        pack[place_of(6 + k)] = expand_grad[0:96, 128 * k : 128 * k + 128]
        pack[place_of(9 + k)] = reduce_grad[0:96, 128 * k : 128 * k + 128]
    through, gain_two_grad = norm_back(middle, gain_two, nt(grad_inner, w.expand[...]), side)
    grad_middle = grad + through
    branch = grad_middle.astype(BF16)
    heads = keep.heads[...]
    mixing_grad = nn(heads.astype(BF16), branch)
    grad_heads = nt(branch, w.mixing[...]).astype(BF16).astype(F32).T
    product = grad_heads[0:96] * heads
    group = lax.broadcasted_iota(jnp.int32, (16, 96), 1) // SIDE_HEAD_DIM
    group = (group == lax.broadcasted_iota(jnp.int32, (16, 96), 0)).astype(BF16)
    high = product.astype(BF16)
    inner = nn(group, high) + nn(group, (product - high.astype(F32)).astype(BF16))
    rows = jnp.concatenate([grad_heads[0:96], -inner, -inner], axis=0).T
    high = rows.astype(BF16)
    c.do_s[...] = jnp.where(lane < 112, high, (rows - high.astype(F32)).astype(BF16))
    pad_heads(c.dot_s, grad_heads, 0.0)
    wide = lanes_of(tokens, 256)
    query_head = jnp.where(wide < 96, wide // SIDE_HEAD_DIM, jnp.where(wide < 128, -1, (wide - 128) % 16))
    out_head = jnp.where(lane < 96, lane // SIDE_HEAD_DIM, (lane - 96) % 16)

    count = parts * tokens // 2

    def one_head(h, keys):
        rows = c.q_s[layer]
        rows = jnp.where((query_head == h) | (query_head < 0), rows, jnp.zeros_like(rows))
        probs = jnp.exp2(nt(rows, c.k_s[layer, keys, :]))
        rows = c.do_s[...]
        rows = jnp.where(out_head == h, rows, jnp.zeros_like(rows))
        scores = (probs * nt(rows, c.v_s[layer, keys, :])).astype(BF16)
        by_keys = nn(c.qt_s[layer, h], scores)[0:8] * LN2
        by_values = nn(c.dot_s[h], probs.astype(BF16))[0:8]
        return by_keys, by_values, nt(c.kt_s[layer, h, :, keys], scores)[0:8] * SIDE_HEAD_DIM**-0.5

    def terms_copy(pair, k):
        return remote(
            c.terms.at[pair, t ^ k],
            c.terms_in.at[layer, pair, t],
            c.terms_send.at[layer, pair, k - 1],
            c.terms_recv.at[layer, pair, t],
            (b, t ^ k),
        )

    def terms_wait(pair, k):
        return remote(
            c.terms.at[pair, t ^ k],
            c.terms_in.at[layer, pair, t ^ k],
            c.terms_send.at[layer, pair, k - 1],
            c.terms_recv.at[layer, pair, t ^ k],
            (b, t ^ k),
        )

    def pair_of(index, carry):
        between(index)
        queries = jnp.zeros((16, tokens), F32)
        for near in range(2):
            chip = t // 2 if near else (t // 2) ^ 1
            keys = pl.ds(pl.multiple_of(chip * count, count), count)
            first, second = one_head(2 * index, keys), one_head(2 * index + 1, keys)
            by_keys, by_values, by_queries = (
                jnp.concatenate([left, right], axis=0) for left, right in zip(first, second)
            )
            queries += by_queries
            for place in range(parts // 2):
                at = slice(place * tokens, (place + 1) * tokens)
                c.terms[index, chip * (parts // 2) + place, 0:16] = by_keys[:, at].astype(BF16)
                c.terms[index, chip * (parts // 2) + place, 16:32] = by_values[:, at].astype(BF16)
            for k in (1,) if near else (2, 3):
                terms_copy(index, k).start()
        c.dqkv[pl.ds(pl.multiple_of(index * 16, 16), 16), :] = queries.astype(BF16)
        return carry

    pairs = SIDE_HEADS // 2
    lax.fori_loop(0, pairs, pair_of, 0)
    mixed = keep.mixed[...]
    gain_one = raw.vectors[layer, 1:2, :]
    normed = side_norm(mixed, side)[0] * gain_one
    c.dqkv[288:384, :] = jnp.zeros((96, tokens), BF16)

    def gather(index, carry):
        total = c.terms[index, t].astype(F32)
        for k in range(1, parts):
            terms_wait(index, k).wait_recv()
            total += c.terms_in[layer, index, t ^ k].astype(F32)
        total = total.astype(BF16)
        c.dqkv[pl.ds(pl.multiple_of(96 + index * 16, 16), 16), :] = total[0:16]
        c.dqkv[pl.ds(pl.multiple_of(192 + index * 16, 16), 16), :] = total[16:32]
        return carry

    lax.fori_loop(0, pairs, gather, 0)
    dqkv = c.dqkv[...]
    project_grad = nt(normed.T.astype(BF16), dqkv)
    pack[place_of(12)] = project_grad[0:96, 0:128]
    pack[place_of(13)] = project_grad[0:96, 128:256]
    pack[place_of(14)] = project_grad[0:96, 256:384] + pltpu.roll(mixing_grad, 32, 1)
    early()
    grad_normed = nn(w.project[...], dqkv).T
    through, gain_one_grad = norm_back(mixed, gain_one, grad_normed, side)
    grad_mixed = grad_middle + through
    down_grad = nn((gate * grad_mixed).T.astype(BF16), f_ref[...])
    for k in range(6):
        pack[place_of(k)] = down_grad[0:96, 128 * k : 128 * k + 128]
    gate_grad = jnp.sum(grad_mixed * (keep.lifted[...] - prev[...]), axis=0, keepdims=True)
    gate_grad = gate_grad * gate * (1.0 - gate)
    row = lax.broadcasted_iota(jnp.int32, (96, 128), 0)
    pack[place_of(15)] = jnp.where(
        row == 0, gate_grad, jnp.where(row == 1, gain_one_grad, jnp.where(row == 2, gain_two_grad, 0.0))
    )
    grad_ref[...] = (1.0 - gate) * grad_mixed

    def sent(index, carry):
        for k in range(1, parts):
            terms_copy(index, k).wait_send()
        return carry

    lax.fori_loop(0, pairs, sent, 0)


class Sum:
    def __init__(self, r, b, t, parts, batch, pack, s):
        self.r, self.b, self.t, self.parts, self.batch, self.pack, self.s = r, b, t, parts, batch, pack, s
        self.place = lax.rem(b, RING)
        self.outer = batch // RING

    def across_tensor(self, half, k):
        r, s, t = self.r, self.s, self.t
        group = COLUMNS // self.parts
        return remote(
            s.out.at[r, pl.ds((t ^ k) * group + half * (group // 2), group // 2)],
            s.one.at[r, t, pl.ds(half * (group // 2), group // 2)],
            s.one_send.at[r, half, k - 1],
            s.one_recv.at[r, half, t],
            (self.b, t ^ k),
        )

    def from_tensor(self, half, k):
        r, s, t = self.r, self.s, self.t
        group = COLUMNS // self.parts
        view = s.one.at[r, t ^ k, pl.ds(half * (group // 2), group // 2)]
        return remote(view, view, s.one_send.at[r, half, k - 1], s.one_recv.at[r, half, t ^ k], (self.b, t ^ k))

    def across_batch(self, k):
        r, s = self.r, self.s
        return remote(
            s.mid_out.at[r, self.place ^ k], s.two.at[r, self.place], s.two_send.at[r, k - 1],
            s.two_recv.at[r, self.place], (self.b ^ k, self.t),
        )

    def from_batch(self, k):
        r, s = self.r, self.s
        return remote(
            s.two.at[r, self.place ^ k], s.two.at[r, self.place ^ k], s.two_send.at[r, k - 1],
            s.two_recv.at[r, self.place ^ k], (self.b ^ k, self.t),
        )

    def across_outer(self, k):
        r, s = self.r, self.s
        mine = self.b // RING
        target = lax.rem(mine + k, self.outer) * RING + self.place
        return remote(
            s.far.at[r, mine], s.far.at[r, mine], s.far_send.at[r, k - 1], s.far_recv.at[r, mine], (target, self.t)
        )

    def from_outer(self, k):
        r, s = self.r, self.s
        other = lax.rem(self.b // RING + k, self.outer)
        return remote(
            s.far.at[r, other], s.far.at[r, other], s.far_send.at[r, k - 1], s.far_recv.at[r, other],
            (self.b ^ 1, self.t),
        )

    def back_batch(self, k, place):
        r, s = self.r, self.s
        return remote(
            s.full.at[r, self.t, place], s.full.at[r, self.t, place], s.three_send.at[r, k - 1],
            s.three_recv.at[r, place], (self.b ^ k, self.t),
        )

    def back_tensor(self, k, slot, place):
        r, s = self.r, self.s
        view = s.full.at[r, slot, place]
        return remote(view, view, s.four_send.at[r, k - 1, place], s.four_recv.at[r, slot, place], (self.b, self.t ^ k))

    def pass_piece(self, place):
        for k in (2, 3, 1):
            self.back_tensor(k, self.t, place).start()

    def step_one(self, half):
        group = COLUMNS // self.parts
        for slot in range(self.parts):
            at = slot * group + half * (group // 2)
            self.s.out[self.r, at : at + group // 2] = self.pack[at : at + group // 2].astype(BF16)
        for k in (2, 3, 1):
            self.across_tensor(half, k).start()

    def step_two(self):
        r, s = self.r, self.s
        group = COLUMNS // self.parts
        total = self.pack[pl.ds(self.t * group, group)]
        for k in range(1, self.parts):
            for half in range(2):
                self.from_tensor(half, k).wait_recv()
            total += s.one[r, self.t ^ k].astype(F32)
        total = total.reshape(RING, total.shape[0] * total.shape[1] // RING, 128)
        s.mid[r] = total
        s.mid_out[r] = total.astype(BF16)
        for k in range(1, RING):
            self.across_batch(k).start()

    def step_three(self):
        r, s = self.r, self.s
        total = s.mid[r, self.place]
        for k in range(1, RING):
            self.from_batch(k).wait_recv()
            total += s.two[r, self.place ^ k].astype(F32)
        if self.outer > 1:
            s.far[r, self.b // RING] = total.astype(BF16)
            for k in range(1, self.outer):
                self.across_outer(k).start()
            for k in range(1, self.outer):
                self.from_outer(k).wait_recv()
            total = s.far[r, 0].astype(F32)
            for other in range(1, self.outer):
                total += s.far[r, other].astype(F32)
            for k in range(1, self.outer):
                self.across_outer(k).wait_send()
        s.full[r, self.t, self.place] = total.astype(BF16)
        for k in range(1, RING):
            self.back_batch(k, self.place).start()
        self.pass_piece(self.place)

    def step_four(self):
        for k in range(1, RING):
            self.back_batch(k, self.place ^ k).wait_recv()
            self.pass_piece(self.place ^ k)

    def step_five(self):
        for k in range(1, self.parts):
            for place in range(RING):
                self.back_tensor(k, self.t ^ k, place).wait_recv()
        for k in range(1, self.parts):
            for half in range(2):
                self.across_tensor(half, k).wait_send()
            for place in range(RING):
                self.back_tensor(k, self.t, place).wait_send()
        for k in range(1, RING):
            self.across_batch(k).wait_send()
            self.back_batch(k, self.place).wait_send()


def finish_kernel(parts, frozen, state, grad, full, *refs):
    outs = Refs(**dict(zip(("frozen", "state", "grad", *OUTS), refs)))
    outs.frozen[...] = frozen[...]
    outs.state[...] = state[...].T[0:96]
    outs.grad[...] = grad[...].T[0:96]
    per = COLUMNS // parts
    for layer in range(LAYERS):

        def column(index):
            at = place_of(index)
            both = full[layer, at // per, 2 * (at % per) : 2 * (at % per) + 2]
            return both.astype(F32).reshape(96, 128)

        for k in range(6):
            outs.down[layer, :, 128 * k : 128 * k + 128] = column(k)
        for k in range(3):
            outs.expand[layer, :, 128 * k : 128 * k + 128] = column(6 + k)
            outs.reduce[layer, :, 128 * k : 128 * k + 128] = column(9 + k)
        outs.project[layer, :, 0:128] = column(12)
        outs.project[layer, :, 128:256] = column(13)
        last = column(14)
        outs.project[layer, :, 256:288] = last[:, 0:32]
        outs.mixing[layer] = pltpu.roll(last, 96, 1)[:, 0:96]
        small = column(15)
        outs.gate[layer : layer + 1, :] = small[0:1, 0:96]
        outs.gains[layer] = small[1:3, 0:96]


RAW = ("gate", "gains", "down", "project", "mixing", "expand", "reduce")
WEIGHTS = RAW[2:]
KEEP = ("lifted", "mixed", "query", "sums", "heads", "middle")


def keep_shapes(tokens):
    return (
        ((tokens, 128), F32),
        ((tokens, 128), F32),
        ((tokens, 128), BF16),
        ((16, tokens), F32),
        ((96, tokens), F32),
        ((tokens, 128), F32),
    )


def weight_scratch(model, units):
    return [
        pltpu.VMEM((128, model), BF16),
        pltpu.VMEM((128, 384), BF16),
        pltpu.VMEM((128, 128), BF16),
        pltpu.VMEM((128, units), BF16),
        pltpu.VMEM((128, units), BF16),
    ]


def tensor_barrier(b, t, parts):
    barrier = pltpu.get_barrier_semaphore()
    for k in range(1, parts):
        pl.semaphore_signal(barrier, inc=1, device_id=(b, t ^ k), device_id_type=MESH)
    return barrier


def vmem_specs(count):
    return [pl.BlockSpec(memory_space=pltpu.VMEM)] * count


OUTS = ("down", "gate", "gains", "project", "mixing", "expand", "reduce")
SUMS = (
    *("out", "one", "mid", "mid_out", "two", "far"),
    *("one_send", "one_recv", "two_send", "two_recv", "far_send", "far_recv"),
    *("three_send", "three_recv", "four_send", "four_recv"),
)
LOCAL = (
    *("k_s", "vt_s", "scores", "kv_send", "kv_recv", "do_s", "dot_s", "q_s", "qt_s", "v_s", "kt_s"),
    *("active", "slope"),
    *("terms", "terms_in", "dqkv", "terms_send", "terms_recv"),
)


def side_rest_kernel(parts, batch, *refs):
    refs = list(refs)

    def pop(count):
        taken, refs[:count] = refs[:count], []
        return taken

    second_f, side_in, cotangent, ids_ref = pop(4)
    raw = Refs(**dict(zip(RAW, pop(7))))
    state_one, *handed = pop(9)
    side_out, grad, full = pop(3)
    local = pop(8)
    first_f, kvt_zero = local[0:2]
    keep_zero = Refs(**dict(zip(KEEP, local[2:])))
    hand_sem = pop(1)[0]
    hand = [pltpu.make_async_copy(*pair, hand_sem.at[k]) for k, pair in enumerate(zip(handed, local))]
    for copy in hand:
        copy.start()
    kvt_one, prev, pack, raw.vectors = pop(4)
    keep_one = Refs(**dict(zip(KEEP, pop(6))))
    w_one = Refs(**dict(zip(WEIGHTS, pop(5))))
    w_zero = Refs(**dict(zip(WEIGHTS, pop(5))))
    c = Refs(**dict(zip(LOCAL, pop(len(LOCAL)))))
    s = Refs(**dict(zip(SUMS, pop(len(SUMS)))))
    s.full = full
    b = lax.axis_index("batch")
    t = lax.axis_index("tensor")
    barrier = tensor_barrier(b, t, parts)
    for k in range(1, RING):
        pl.semaphore_signal(barrier, inc=1, device_id=(b ^ k, t), device_id_type=MESH)
    outer = batch // RING
    for k in range(1, outer):
        other = lax.rem(b // RING + k, outer) * RING + lax.rem(b, RING)
        pl.semaphore_signal(barrier, inc=1, device_id=(other, t), device_id_type=MESH)
    load_vectors(raw.vectors, raw)
    load_side_weights(1, w_one, raw)
    load_side_weights(0, w_zero, raw)
    grad[...] = widened(cotangent)
    prev[...] = widened(side_in)
    pl.semaphore_wait(barrier, parts - 1 + RING - 1 + outer - 1)

    def prepare_lower():
        for copy in hand:
            copy.wait()
        side_prepare(0, parts, w_zero, raw, c, keep_zero, kvt_zero, ids_ref, True)

    first = Refs(
        kvt=kvt_one, k_s=c.k_s.at[1], vt_s=c.vt_s, scores=c.scores, kv_send=c.kv_send, kv_recv=c.kv_recv
    )
    side_forward(
        1, b, t, parts, second_f, state_one, w_one, raw, first, keep_one, ids_ref, side_out,
        lambda: None, prepare_lower, lambda index: None,
    )
    side_prepare(1, parts, w_one, raw, c, keep_one, kvt_one, ids_ref, False)
    upper = Sum(1, b, t, parts, batch, pack.at[1], s)
    lower = Sum(0, b, t, parts, batch, pack.at[0], s)
    side_backward(
        1, b, t, parts, second_f, state_one, w_one, raw, c, keep_one, grad, pack.at[1],
        lambda index: None, lambda: upper.step_one(0),
    )
    upper.step_one(1)

    def between(index):
        pl.when(index == 2)(upper.step_two)
        pl.when(index == 4)(upper.step_three)
        pl.when(index == 5)(upper.step_four)

    side_backward(
        0, b, t, parts, first_f, prev, w_zero, raw, c, keep_zero, grad, pack.at[0],
        between, lambda: lower.step_one(0),
    )
    lower.step_one(1)
    upper.step_five()
    lower.step_two()
    lower.step_three()
    lower.step_four()
    lower.step_five()


def side_rest_call(first_f, second_f, side_in, cotangent, ids_all, raw, state_one, kvt_zero, keep_zero, parts, batch):
    tokens, model = first_f.shape
    length = parts * tokens
    units = raw[5].shape[2]
    dma = pltpu.SemaphoreType.DMA
    vmem = pltpu.VMEM
    pairs = SIDE_HEADS // 2
    group = COLUMNS // parts
    piece = group * 96 // RING
    outs = (
        ((tokens, 128), F32),
        ((tokens, 128), F32),
        ((LAYERS, parts, RING, piece, 128), BF16),
    )
    outer = max(batch // RING, 1)
    return pl.pallas_call(
        functools.partial(side_rest_kernel, parts, batch),
        out_shape=tuple(jax.ShapeDtypeStruct(*o) for o in outs),
        in_specs=vmem_specs(12) + [pl.BlockSpec(memory_space=pl.ANY)] * 8,
        out_specs=tuple(vmem_specs(len(outs))),
        scratch_shapes=[
            vmem((tokens, model), BF16),
            vmem((parts, 192, tokens), BF16),
            *[vmem(*shape) for shape in keep_shapes(tokens)],
            dma((8,)),
            vmem((parts, 192, tokens), BF16),
            vmem((tokens, 128), F32),
            vmem((LAYERS, COLUMNS, 96, 128), F32),
            vmem((LAYERS, 8, 128), F32),
            *[vmem(*shape) for shape in keep_shapes(tokens)],
            *weight_scratch(model, units),
            *weight_scratch(model, units),
            vmem((LAYERS, length, 256), BF16),
            vmem((SIDE_HEADS, 16, length), BF16),
            vmem((2, length, tokens), F32),
            dma((3,)),
            dma((parts,)),
            vmem((tokens, 128), BF16),
            vmem((SIDE_HEADS, 16, tokens), BF16),
            vmem((LAYERS, tokens, 256), BF16),
            vmem((LAYERS, SIDE_HEADS, 16, tokens), BF16),
            vmem((LAYERS, length, 128), BF16),
            vmem((LAYERS, SIDE_HEADS, 16, length), BF16),
            vmem((LAYERS, tokens, units), BF16),
            vmem((LAYERS, tokens, units), F32),
            vmem((pairs, parts, 32, tokens), BF16),
            vmem((LAYERS, pairs, parts, 32, tokens), BF16),
            vmem((384, tokens), BF16),
            dma((LAYERS, pairs, parts - 1)),
            dma((LAYERS, pairs, parts)),
            vmem((LAYERS, COLUMNS, 96, 128), BF16),
            vmem((LAYERS, parts, group, 96, 128), BF16),
            vmem((LAYERS, RING, piece, 128), F32),
            vmem((LAYERS, RING, piece, 128), BF16),
            vmem((LAYERS, RING, piece, 128), BF16),
            vmem((LAYERS, outer, piece, 128), BF16),
            dma((LAYERS, 2, parts - 1)),
            dma((LAYERS, 2, parts)),
            dma((LAYERS, RING - 1)),
            dma((LAYERS, RING)),
            dma((LAYERS, max(outer - 1, 1))),
            dma((LAYERS, outer)),
            dma((LAYERS, RING - 1)),
            dma((LAYERS, RING)),
            dma((LAYERS, parts - 1, RING)),
            dma((LAYERS, parts, RING)),
        ],
        compiler_params=pltpu.CompilerParams(
            collective_id=5, has_side_effects=True, vmem_limit_bytes=62 << 20
        ),
    )(second_f, side_in, cotangent, ids_all, *raw, state_one, first_f, kvt_zero, *keep_zero)


def finish_call(frozen, state, grad, full, side, parts):
    tokens, model = frozen.shape
    units = 4 * side
    outs = (
        ((tokens, model), BF16),
        ((side, tokens), F32),
        ((side, tokens), F32),
        ((LAYERS, side, model), F32),
        ((LAYERS, side), F32),
        ((LAYERS, 2, side), F32),
        ((LAYERS, side, 3 * side), F32),
        ((LAYERS, side, side), F32),
        ((LAYERS, side, units), F32),
        ((LAYERS, side, units), F32),
    )
    frozen, state, grad, down, *others, reduce_grad = pl.pallas_call(
        functools.partial(finish_kernel, parts),
        out_shape=tuple(jax.ShapeDtypeStruct(*o) for o in outs),
        in_specs=vmem_specs(4),
        out_specs=tuple(vmem_specs(len(outs))),
        compiler_params=pltpu.CompilerParams(vmem_limit_bytes=62 << 20),
    )(frozen, state, grad, full)
    turn = (0, 2, 1)
    return (frozen, state.T, grad.T, down.transpose(turn), *others, reduce_grad.transpose(turn))


def per_device(
    hidden_rows,
    side_input,
    segment_ids,
    side_cotangent,
    backbone_gains,
    backbone_project,
    backbone_mixing,
    backbone_expand,
    backbone_reduce,
    side_down,
    side_gate,
    side_gains,
    side_project,
    side_mixing,
    side_expand,
    side_reduce,
):
    parts = lax.axis_size("tensor")
    batch = lax.axis_size("batch")
    side = side_input.shape[1]
    turn = (0, 2, 1)
    qkv = backbone_project.transpose(0, 2, 3, 1)
    raw = (
        side_gate,
        side_gains,
        side_down.transpose(turn),
        side_project,
        side_mixing,
        side_expand,
        side_reduce.transpose(turn),
    )
    side_turned, cotangent_turned = side_input.T, side_cotangent.T
    ids_row = segment_ids.reshape(1, -1)

    second_f, first_f, ids_all, state_one, kvt_zero, *keep_zero = front_call(
        hidden_rows,
        ids_row,
        backbone_gains,
        qkv,
        backbone_mixing,
        backbone_expand,
        backbone_reduce,
        side_turned,
        raw,
        parts,
    )
    state, grad, full = side_rest_call(
        first_f, second_f, side_turned, cotangent_turned, ids_all, raw, state_one, kvt_zero, keep_zero, parts, batch
    )
    return finish_call(second_f, state, grad, full, side, parts)


def solution(mesh):
    return jax.shard_map(
        per_device,
        mesh=mesh,
        in_specs=(
            P(("batch", "tensor"), None),
            P(("batch", "tensor"), None),
            P(("batch", "tensor")),
            P(("batch", "tensor"), None),
            P(),
            P(None, None, None, "tensor"),
            P(None, "tensor", None),
            P(None, None, "tensor"),
            P(None, "tensor", None),
            P(),
            P(),
            P(),
            P(),
            P(),
            P(),
            P(),
        ),
        out_specs=(
            P(("batch", "tensor"), None),
            P(("batch", "tensor"), None),
            P(("batch", "tensor"), None),
            P(),
            P(),
            P(),
            P(),
            P(),
            P(),
            P(),
        ),
        check_vma=False,
    )
```
